32 devices in a mesh: dp: 16 (over z, y, x), seq: 2 (over core).
Axes of the slice: x: 2, y: 2, z: 4, core: 2. Of those that a mesh axis runs over, the one named last changes fastest.
Arguments:
- tokens: bfloat16 [2, 32, 512, 512], P(None, 'dp', 'seq'), may hold values from -6 to 6
- cotangent: bfloat16 [2, 32, 512, 512], P(None, 'dp', 'seq'), may hold values from -6 to 6
- segments: int32 [2, 32, 512], P(None, 'dp', 'seq'), may hold values from 0 to 3, as said below
- pad_mask: int32 [2, 32, 512], P(None, 'dp', 'seq'), may hold values from 0 to 1, as said below
- row_counts: int32 [2, 16], P(None, 'dp'), may hold values from 1 to 2, as said below
- attend_gain: float32 [512], replicated, may hold values from 0.5 to 1.5
- w_query: bfloat16 [512, 512], replicated, may hold values from -0.125 to 0.125
- w_key: bfloat16 [512, 512], replicated, may hold values from -0.125 to 0.125
- w_value: bfloat16 [512, 512], replicated, may hold values from -0.25 to 0.25
- w_out: bfloat16 [512, 512], replicated, may hold values from -0.75 to 0.75
- forward_gain: float32 [512], replicated, may hold values from 0.5 to 1.5
- w_in: bfloat16 [512, 2048], replicated, may hold values from -0.25 to 0.25
- w_down: bfloat16 [2048, 512], replicated, may hold values from -0.125 to 0.125
- position_bias_table: float32 [32, 8], replicated, may hold values from -4 to 4
Outputs:
- output: bfloat16 [2, 32, 512, 512], P(None, 'dp', 'seq')
- gradient_input: bfloat16 [2, 32, 512, 512], P(None, 'dp', 'seq')
- grad_attend: float32 [512], replicated
- grad_query: float32 [512, 512], replicated
- grad_key: float32 [512, 512], replicated
- grad_value: float32 [512, 512], replicated
- grad_out: float32 [512, 512], replicated
- grad_forward: float32 [512], replicated
- grad_in: float32 [512, 2048], replicated
- grad_down: float32 [2048, 512], replicated
- grad_table: float32 [32, 8], replicated
The draws below stay inside these ranges and needn't reach their ends.
Inputs may be any that keep to these rules, and one draw needn't show every extreme that they name: Rows of data group g with slot number row_counts[m, g] or more in micro-batch m are unused; in every draw some group has 2 live rows and some has one. `segments`: each row is cut into items of 128, 256 or 512 tokens that start on quarters of the row, numbered from 0 at the row's start; in each micro-batch every data group has a live row that is one item of 512 tokens. `pad_mask`: within an item the real tokens come first and are more than seven eighths of it.
All inputs are finite; a program needn't handle non-finite values.
Results may differ from the reference program's by a relative error of at most 0.014.
Values may be sent and summed in bfloat16 or wider, within the bound.
No kernel may reach another device: no remote copies, remote signals or barrier semaphores. Data moves between devices by JAX's collectives and lax.ppermute only.
A program may use at most 192 MiB of HBM per device.

```python
import jax
import jax.numpy as jnp
import numpy as np
from jax import lax

MODEL_WIDTH = 512
HEADS = 8
FF = 2048
BUCKETS = 32
PACKED_LENGTH = 512
MICRO_BATCHES = 2
CAP = 2
INNER = 512
ROW_SLOTS = 32
N_DP = 16


PATTERNS = np.array([[0, 0, 0, 0], [0, 0, 1, 1], [0, 0, 1, 2], [0, 1, 1, 2], [0, 1, 2, 2], [0, 1, 2, 3]], np.int32)


STARTS = np.array([[0, 0, 0, 0], [0, 0, 2, 2], [0, 0, 2, 3], [0, 1, 1, 3], [0, 1, 2, 2], [0, 1, 2, 3]], np.int32)


SPANS = np.array([[4, 4, 4, 4], [2, 2, 2, 2], [2, 2, 1, 1], [1, 2, 2, 1], [1, 1, 2, 2], [1, 1, 1, 1]], np.int32)


def common_layout(key):
    keys = jax.random.split(key, 5)
    rows_all = N_DP * CAP
    counts = jax.random.randint(keys[0], (MICRO_BATCHES, N_DP), 1, CAP + 1).astype(jnp.int32)
    flat_counts = counts.reshape(-1)
    chosen = jax.random.randint(keys[1], (), 0, MICRO_BATCHES * N_DP)
    flat_counts = flat_counts.at[chosen].set(CAP)
    flat_counts = flat_counts.at[(chosen + 1) % (MICRO_BATCHES * N_DP)].set(1)
    counts = flat_counts.reshape(MICRO_BATCHES, N_DP)
    spanning = jax.random.randint(keys[2], (MICRO_BATCHES, N_DP), 0, 1 << 20) % counts
    row_ids = jnp.arange(rows_all, dtype=jnp.int32)
    owner = row_ids // CAP
    slot_ids = row_ids % CAP
    is_span = slot_ids[None, :] == spanning[:, owner]
    pattern = jax.random.randint(keys[3], (MICRO_BATCHES, rows_all), 0, 6)
    pattern = jnp.where(is_span, 0, pattern)
    fourth_part = PACKED_LENGTH // 4
    owning_block = jnp.arange(PACKED_LENGTH, dtype=jnp.int32) // fourth_part
    segs = jnp.asarray(PATTERNS)[pattern][:, :, owning_block]
    opening_blocks = jnp.asarray(STARTS)[pattern][:, :, owning_block]
    lengths = jnp.asarray(SPANS)[pattern][:, :, owning_block] * fourth_part
    cuts = jax.random.randint(keys[4], (MICRO_BATCHES, rows_all, 4), 0, 1 << 20)
    cut_here = jnp.take_along_axis(cuts, opening_blocks, axis=2) % jnp.maximum(lengths // 8, 1)
    shift_amounts = jnp.arange(PACKED_LENGTH, dtype=jnp.int32)[None, None, :] - opening_blocks * fourth_part
    pads = (shift_amounts < lengths - cut_here).astype(jnp.int32)
    return (counts.astype(jnp.int32), segs.astype(jnp.int32), pads)


def draw_row_counts(key, part):
    counts, segs, pads = common_layout(key)
    return counts


def draw_segments(key, part):
    counts, segs, pads = common_layout(key)
    return segs


def draw_pad_mask(key, part):
    counts, segs, pads = common_layout(key)
    return pads


def block_levels(stream_key, shape, shards, low, high):
    gain, own = 1.0, jax.random.fold_in(stream_key, 6)
    for position, parts in shards:
        steps = jnp.exp(jax.random.uniform(jax.random.fold_in(own, position), (parts,), jnp.float32, low / len(shards), high / len(shards)))
        gain = gain * jnp.repeat(steps, shape[position] // parts).reshape([-1 if axis == position else 1 for axis in range(len(shape))])
    return gain


def scatter_about(rng, extent, deviation, limit, shards=(), kind=jnp.bfloat16):
    values = deviation * jax.random.normal(rng, extent, jnp.float32)
    if shards:
        values = values * block_levels(rng, extent, shards, -0.22, 0.18)
    return jnp.clip(values, -limit, limit).astype(kind)


def setup_inputs(seed: int = 0) -> dict:
    key_of = jax.random.split(jax.random.key(seed), 15)
    tokens = scatter_about(key_of[0], (MICRO_BATCHES, ROW_SLOTS, PACKED_LENGTH, MODEL_WIDTH), 1.0, 6.0, ((1, 16), (2, 2)))
    cotangent = scatter_about(key_of[1], (MICRO_BATCHES, ROW_SLOTS, PACKED_LENGTH, MODEL_WIDTH), 1.0, 6.0, ((1, 16), (2, 2)))
    segments = draw_segments(jax.random.fold_in(key_of[14], 71), 0)
    pad_mask = draw_pad_mask(jax.random.fold_in(key_of[14], 71), 0)
    row_counts = draw_row_counts(jax.random.fold_in(key_of[14], 71), 0)
    attend_gain = jnp.clip(1.0 + 0.1 * jax.random.normal(key_of[5], (MODEL_WIDTH,), jnp.float32), 0.5, 1.5)
    w_query = scatter_about(key_of[6], (MODEL_WIDTH, INNER), (4 * MODEL_WIDTH) ** -0.5, 0.125)
    w_key = scatter_about(key_of[7], (MODEL_WIDTH, INNER), (4 * MODEL_WIDTH) ** -0.5, 0.125)
    w_value = scatter_about(key_of[8], (MODEL_WIDTH, INNER), MODEL_WIDTH ** -0.5, 0.25)
    w_out = scatter_about(key_of[9], (INNER, MODEL_WIDTH), (INNER // 8) ** -0.5, 0.75)
    forward_gain = jnp.clip(1.0 + 0.1 * jax.random.normal(key_of[10], (MODEL_WIDTH,), jnp.float32), 0.5, 1.5)
    w_in = scatter_about(key_of[11], (MODEL_WIDTH, FF), MODEL_WIDTH ** -0.5, 0.25)
    w_down = scatter_about(key_of[12], (FF, MODEL_WIDTH), FF ** -0.5, 0.125)
    position_bias_table = scatter_about(key_of[13], (BUCKETS, HEADS), 1.0, 4.0, (), jnp.float32)
    return {"tokens": tokens, "cotangent": cotangent, "segments": segments, "pad_mask": pad_mask, "row_counts": row_counts, "attend_gain": attend_gain, "w_query": w_query, "w_key": w_key, "w_value": w_value, "w_out": w_out, "forward_gain": forward_gain, "w_in": w_in, "w_down": w_down, "position_bias_table": position_bias_table}


EPSILON = 1e-06
MASKED = -1000000000.0
LIMITS = (12, 16, 23, 32, 46, 64, 91)
MAX_ACCURACY = lax.Precision.HIGHEST

@jax.custom_vjp
def low(v):
    return lax.optimization_barrier(v.astype(jnp.bfloat16)).astype(jnp.float32)

@jax.custom_vjp
def low_back(v):
    return v

def low_keep(v):
    return (low(v), None)

def low_pass(kept, grad):
    return (grad,)

def back_keep(v):
    return (v, None)

def back_low(kept, grad):
    return (low(grad),)
low.defvjp(low_keep, low_pass)
low_back.defvjp(back_keep, back_low)

def bucket_of(relative, half_count):
    distance = jnp.abs(relative)
    far_bucket = 8 + sum(((distance >= bound_value).astype(jnp.int32) for bound_value in LIMITS))
    near_or_far = jnp.where(distance < 8, distance, far_bucket)
    return (near_or_far + jnp.where(relative > 0, half_count, 0)).astype(jnp.int32)

def rms_norm(values, gain_vec):
    return values * lax.rsqrt(lax.optimization_barrier(jnp.mean(values * values, -1, keepdims=True)) + EPSILON) * gain_vec

def layer(params, inputs, seg_ids, kept_mask, buckets):
    attend_gain, w_query, w_key, w_value, w_out, forward_gain, w_in, w_down, position_bias_table = params
    row_count, length, model_dim = inputs.shape
    head_count = position_bias_table.shape[1]
    head_size = w_query.shape[1] // head_count
    normed = low(rms_norm(inputs, attend_gain))

    def project(weight):
        mixed = jnp.einsum('rlm,mi->rli', normed, weight, precision=MAX_ACCURACY)
        return low_back(low(mixed)).reshape(row_count, length, head_count, head_size)
    query_matrix = project(w_query)
    keys_all = project(w_key)
    values_all = project(w_value)
    pairwise_bias = jnp.transpose(position_bias_table[buckets], (2, 0, 1))
    scores = jnp.einsum('rqhd,rkhd->rhqk', query_matrix, keys_all, precision=MAX_ACCURACY) + pairwise_bias[None]
    scores = low_back(scores)
    allowed = (seg_ids[:, :, None] == seg_ids[:, None, :]) & (kept_mask[:, None, :] > 0)
    scores = jnp.where(allowed[:, None], scores, MASKED)
    probability = jax.nn.softmax(scores, axis=-1)
    attended = jnp.einsum('rhqk,rkhd->rqhd', low(probability), values_all, precision=MAX_ACCURACY)
    attended = low_back(low(attended)).reshape(row_count, length, head_count * head_size)
    branch = low_back(jnp.einsum('rli,im->rlm', attended, w_out, precision=MAX_ACCURACY))
    middle = inputs + kept_mask[..., None] * branch
    second = low(rms_norm(middle, forward_gain))
    upward = low_back(jnp.einsum('rlm,mf->rlf', second, w_in, precision=MAX_ACCURACY))
    active = low(jax.nn.gelu(upward, approximate=False))
    feed = low_back(jnp.einsum('rlf,fm->rlm', active, w_down, precision=MAX_ACCURACY))
    return middle + kept_mask[..., None] * feed

def reference(tokens, cotangent, segments, pad_mask, row_counts, attend_gain, w_query, w_key, w_value, w_out, forward_gain, w_in, w_down, position_bias_table):
    params = tuple((item.astype(jnp.float32) for item in (attend_gain, w_query, w_key, w_value, w_out, forward_gain, w_in, w_down, position_bias_table)))
    rows_overall = N_DP * CAP
    slot_index = jnp.arange(rows_overall, dtype=jnp.int32) % CAP
    counts_wide = jnp.repeat(row_counts, CAP, axis=1)
    live_rows = slot_index[None, :] < counts_wide
    every_kept = jnp.where(live_rows[:, :, None] & (pad_mask > 0), 1.0, 0.0).astype(jnp.float32)
    token_places = jnp.arange(PACKED_LENGTH, dtype=jnp.int32)
    buckets = bucket_of(token_places[None, :] - token_places[:, None], BUCKETS // 2)
    grouped_rows = 8
    count_of_blocks = MICRO_BATCHES * rows_overall // grouped_rows
    every_input = tokens.astype(jnp.float32).reshape(count_of_blocks, grouped_rows, PACKED_LENGTH, MODEL_WIDTH)
    every_upstream = cotangent.astype(jnp.float32).reshape(count_of_blocks, grouped_rows, PACKED_LENGTH, MODEL_WIDTH)
    every_segment = segments.reshape(count_of_blocks, grouped_rows, PACKED_LENGTH)
    retained_blocks = every_kept.reshape(count_of_blocks, grouped_rows, PACKED_LENGTH)
    checked = jax.checkpoint(layer)

    def step(totals, block):
        inputs, upstream, seg_ids, kept_mask = block

        def apply_encoder_step(weights_now, inputs_now):
            return checked(weights_now, inputs_now, seg_ids, kept_mask, buckets)
        result, back = jax.vjp(apply_encoder_step, params, inputs)
        param_grads, input_part = back(upstream)
        totals = jax.tree.map(lambda summed_fragment, new_part: summed_fragment + new_part, totals, param_grads)
        return (totals, (result.astype(jnp.bfloat16), input_part.astype(jnp.bfloat16)))
    zero_grads = jax.tree.map(jnp.zeros_like, params)
    grads, (output_values, gradients_of_input) = lax.scan(step, zero_grads, (every_input, every_upstream, every_segment, retained_blocks))
    output = output_values.reshape(MICRO_BATCHES, rows_overall, PACKED_LENGTH, MODEL_WIDTH)
    gradient_input = gradients_of_input.reshape(MICRO_BATCHES, rows_overall, PACKED_LENGTH, MODEL_WIDTH)
    return (output, gradient_input, grads[0], grads[1], grads[2], grads[3], grads[4], grads[5], grads[6], grads[7], grads[8])
```

```python
import functools
import math

import jax
import jax.numpy as jnp
from jax import lax
from jax.experimental import pallas as pl
from jax.experimental.pallas import tpu as pltpu
from jax.sharding import PartitionSpec as P

EPSILON = 1e-06
MASKED = -1000000000.0
LIMITS = (12, 16, 23, 32, 46, 64, 91)
BF = jnp.bfloat16
F32 = jnp.float32
VMEM_BYTES = 14 * 1024 * 1024
TILE = 128
LEVELS = 4
SPLIT = 2
SMALL = 32
PARTS = 4


def whole():
    return pl.BlockSpec(memory_space=pltpu.VMEM)


def hbm():
    return pl.BlockSpec(memory_space=pl.ANY)


def far():
    return pl.BlockSpec(memory_space=pltpu.HBM)


def smem():
    return pl.BlockSpec(memory_space=pltpu.SMEM)


class Order:
    def __init__(self):
        self.last = None

    def call(self, kernel, name, micros, inputs, in_specs, out_shape, grid=1, out_specs=None, scratch=()):
        count = len(inputs)
        extra = () if self.last is None else (self.last,)

        def body(*refs):
            kernel(*refs[:count], *refs[count + len(extra) :])

        outs = pl.pallas_call(
            body,
            grid=(grid,),
            in_specs=list(in_specs) + [hbm()] * len(extra),
            out_specs=out_specs or [whole() for _ in out_shape],
            out_shape=out_shape,
            scratch_shapes=list(scratch),
            compiler_params=pltpu.CompilerParams(vmem_limit_bytes=VMEM_BYTES),
            cost_estimate=pl.CostEstimate(
                flops=int(micros * 1e9), bytes_accessed=int(micros * 1e6), transcendentals=0
            ),
            name=name,
        )(*inputs, *extra)
        self.last = min(outs, key=lambda out: out.size * out.dtype.itemsize)
        return outs


def dot(a, b, contract=((1,), (0,))):
    return lax.dot_general(a, b, (contract, ((), ())), preferred_element_type=F32)


def dot_nt(a, b):
    return dot(a, b, ((1,), (1,)))


def dot_tn(a, b):
    return dot(a, b, ((0,), (0,)))


def bucket_of(relative, half_count):
    distance = jnp.abs(relative)
    far = jnp.full(relative.shape, 8, jnp.int32)
    for bound in LIMITS:
        far = far + (distance >= bound).astype(jnp.int32)
    near_or_far = jnp.where(distance < 8, distance, far)
    return near_or_far + jnp.where(relative > 0, half_count, 0)


def diagonal_buckets(length, half_count):
    lane = lax.broadcasted_iota(jnp.int32, (8, 2 * length), 1)
    relative = lane - (length - TILE)
    relative = jnp.where(lane < 2 * length - TILE, relative, relative - 2 * length)
    return bucket_of(relative, half_count)


def wide(column, width):
    return jnp.concatenate([column] * (width // TILE), axis=1)


def put_block(keep, send, who, block, blocks, value):
    count = value.shape[0] >> LEVELS
    places = 1 << LEVELS
    for core in range(2):

        @pl.when(who[0] == core)
        def _():
            for k in range(places):
                place = jnp.bitwise_xor(k % (places // 2), who[1 + 2 * k // places])
                start = pl.multiple_of((place * blocks + block) * count, count)
                ref = keep if 2 * k // places == core else send
                ref[pl.ds(start, count), :] = value[k * count : (k + 1) * count].astype(ref.dtype)


def half_of(ref, i, half):
    return ref[pl.ds(pl.multiple_of(i * half, half), half), :]


def fill_row(row_ref, own_ref, got_ref, m, c, half):
    row_ref[m, pl.ds(pl.multiple_of(c * half, half), half), :] = own_ref[m]
    row_ref[m, pl.ds(pl.multiple_of((1 - c) * half, half), half), :] = got_ref[m]
    return row_ref[m]


def join(own, got, c):
    return jnp.where(c == 0, jnp.concatenate([own, got], 1), jnp.concatenate([got, own], 1))


def fetches(sources, targets, sems):
    return [pltpu.make_async_copy(a, b, sems.at[i]) for i, (a, b) in enumerate(zip(sources, targets))]


def feed_weights(w_in, w_down, chunk, width):
    start = pl.multiple_of(chunk * width, width)
    return w_in.at[:, pl.ds(start, width)], w_down.at[pl.ds(start, width), :]


def pick_kernel(who, tok, cot, seg, pad, tok_own, tok_send, cot_own, cot_send, marks_own, marks_send, sems):
    c = who[0]
    rows = tok.shape[0]
    copies = []
    for m in range(rows):
        for source, own, send in ((tok, tok_own, tok_send), (cot, cot_own, cot_send)):
            for slot, target in ((c, own), (1 - c, send)):
                copies.append(pltpu.make_async_copy(source.at[m, slot], target.at[m], sems.at[len(copies)]))
    for copy in copies:
        copy.start()
    for kind, marks in enumerate((seg, pad)):
        for m in range(rows):
            first, second = marks[m, pl.ds(0, 1)], marks[m, pl.ds(1, 1)]
            marks_own[kind, pl.ds(m, 1)] = jnp.where(c == 0, first, second)
            marks_send[kind, pl.ds(m, 1)] = jnp.where(c == 0, second, first)
    for copy in copies:
        copy.wait()


def forward_kernel(
    who, counts, own, got, marks, marks_got, table, gain, fgain, wq_far, wk_far, wv_far, wo_far,
    x_out, normed_out, q_out, k_out, v_out, e_out, inv_out, att_out, kept_out, middle_out, second_out,
    segq, segk, diag, wq, wk, wv, wo, sems,
):
    c = who[0]
    pair = pl.program_id(0)
    rows, half = own.shape[0], own.shape[1]
    length = 2 * half
    pairs = wq.shape[1] // TILE
    bucket_count = table.shape[0]
    copies = fetches((wq_far, wk_far, wv_far, wo_far), (wq, wk, wv, wo), sems)

    @pl.when(pair == 0)
    def _():
        for copy in copies:
            copy.start()
        buckets = diagonal_buckets(length, bucket_count // 2)
        strip = jnp.zeros(buckets.shape, F32)
        for b in range(bucket_count):
            strip = jnp.where(buckets == b, table[b], strip)
        for h in range(strip.shape[0]):
            diag[h] = strip[h : h + 1]
        for m in range(rows):
            x = fill_row(x_out, own, got, m, c, half).astype(F32)
            r = lax.rsqrt(jnp.mean(x * x, -1, keepdims=True) + EPSILON)
            normed = (x * r * gain[...]).astype(BF)
            normed_out[m] = normed
            if m == 0:
                for copy in copies:
                    copy.wait()
            for w, out in ((wq, q_out), (wk, k_out), (wv, v_out)):
                projected = dot(normed, w[...]).astype(BF)
                for p in range(pairs):
                    out[m, p] = projected[:, p * TILE : (p + 1) * TILE]
            seg = join(marks[0, pl.ds(m, 1)], marks_got[0, pl.ds(m, 1)], c)
            pad = join(marks[1, pl.ds(m, 1)], marks_got[1, pl.ds(m, 1)], c)
            kept = (pad > 0) & (counts[m] > c)
            item = lax.broadcasted_iota(jnp.int32, (TILE, length), 0)
            same = item == seg
            segq[m] = jnp.where(same, 1.0, 0.0).T.astype(BF)
            segk[m] = jnp.where(same & kept, 0.0, MASKED).T.astype(BF)
            kept_out[m] = jnp.broadcast_to(jnp.where(kept, 1.0, 0.0), (TILE, length)).T

    lane = lax.broadcasted_iota(jnp.int32, (length, TILE), 1)
    for head in range(2):
        mine = (lane < TILE // 2) if head == 0 else (lane >= TILE // 2)
        line = jnp.broadcast_to(diag[2 * pair + head], (TILE, 2 * length))
        strip = pltpu.roll(line, 0, 1, stride=1, stride_axis=0)
        bias = jnp.concatenate(
            [strip[:, length - (i + 1) * TILE : 2 * length - (i + 1) * TILE] for i in range(length // TILE)], 0
        )
        for m in range(rows):
            query = jnp.concatenate([q_out[m, pair], segq[m]], 1)
            key = jnp.concatenate([jnp.where(mine, k_out[m, pair], 0), segk[m]], 1)
            value = jnp.concatenate([jnp.where(mine, v_out[m, pair], 0), jnp.where(mine, 1.0, 0.0).astype(BF)], 1)
            scores = dot_nt(query, key) + bias
            e = jnp.exp(scores - jnp.max(scores, -1, keepdims=True)).astype(BF)
            e_out[m, pair, head] = e
            weighed = dot(e, value)
            if head == 0:
                att_acc = weighed
                inv_out[m, pair] = att_acc[:, TILE:]
                half_att = att_acc[:, :TILE]
                middle_out[m, :, :TILE] = half_att
            else:
                inv = 1.0 / (inv_out[m, pair] + weighed[:, TILE:])
                inv_out[m, pair] = inv
                att_out[m, pair] = ((middle_out[m, :, :TILE] + weighed[:, :TILE]) * inv).astype(BF)

    @pl.when(pair == pairs - 1)
    def _():
        for m in range(rows):
            attended = jnp.concatenate([att_out[m, p] for p in range(pairs)], 1)
            branch = dot(attended, wo[...])
            middle = x_out[m].astype(F32) + wide(kept_out[m], branch.shape[1]) * branch
            middle_out[m] = middle
            r = lax.rsqrt(jnp.mean(middle * middle, -1, keepdims=True) + EPSILON)
            second_out[m] = (middle * r * fgain[...]).astype(BF)


def gelu_parts(u):
    z = jnp.abs(u) * (0.5**0.5)
    t = 1.0 / (1.0 + 0.3275911 * z)
    bell = jnp.exp(u * u * -0.5)
    poly = ((((1.061405429 * t - 1.453152027) * t + 1.421413741) * t - 0.284496736) * t + 0.254829592) * t
    tail = 0.5 * poly * bell
    upper = jnp.where(u >= 0, 1.0 - tail, tail)
    return upper, u * bell * ((2.0 * math.pi) ** -0.5)


def feed_chunk(m, second, fg, w_in, w_down, act, ug, acc, sg):
    u = dot(second[m], w_in[...])
    upper, slope = gelu_parts(u)
    active = (u * upper).astype(BF)
    act[m] = active
    acc[m] += dot(active, w_down[...])
    up = (dot_nt(fg[m], w_down[...]) * (upper + slope)).astype(BF)
    ug[m] = up
    sg[m] += dot_nt(up, w_in[...])


def tall(ref):
    return jnp.concatenate([ref[m] for m in range(ref.shape[0])], 0)


def feed_first_kernel(
    who, own, got, kept, second, w_in_far, w_down_far,
    g_out, fg_out, acc_out, sg_out, keep, send, act, ug,
    w_ins, w_downs, sems,
    *, steps,
):
    step = pl.program_id(0)
    rows, half, width = own.shape
    copies = [
        fetches(feed_weights(w_in_far, w_down_far, i, width), (w_ins.at[i], w_downs.at[i]), sems.at[i])
        for i in range(steps)
    ]

    @pl.when(step == 0)
    def _():
        for copy in sum(copies, []):
            copy.start()
        for m in range(rows):
            g = fill_row(g_out, own, got, m, who[0], half)
            fg_out[m] = (g.astype(F32) * wide(kept[m], g.shape[1])).astype(BF)
        acc_out[...] = jnp.zeros_like(acc_out)
        sg_out[...] = jnp.zeros_like(sg_out)

    for i in range(steps):

        @pl.when(step == i)
        def _():
            for copy in copies[i]:
                copy.wait()

    for m in range(rows):
        feed_chunk(m, second, fg_out, w_ins.at[step], w_downs.at[step], act, ug, acc_out, sg_out)
    put_block(keep, send, who, step, 2 * steps, dot_tn(tall(act), tall(fg_out)))
    put_block(keep, send, who, steps + step, 2 * steps, dot_tn(tall(second), tall(ug)))


def feed_second_kernel(
    chunk, fg, acc_in, sg_in, second, w_in_far, w_down_far,
    acc_out, sg_out, down_out, in_out, act, ug,
    w_in, w_down, sems,
):
    copies = fetches(feed_weights(w_in_far, w_down_far, chunk, fg.shape[2]), (w_in, w_down), sems)
    for copy in copies:
        copy.start()
    acc_out[...] = acc_in[...]
    sg_out[...] = sg_in[...]
    for copy in copies:
        copy.wait()
    for m in range(fg.shape[0]):
        feed_chunk(m, second, fg, w_in, w_down, act, ug, acc_out, sg_out)
    down_out[...] = dot_tn(tall(act), tall(fg)).astype(BF)
    in_out[...] = dot_tn(tall(second), tall(ug)).astype(BF)


def feed_third_kernel(
    chunk, who, g, fg, acc_in, sg_in, kept, middle, second, att, fgain, wo_far, w_in_far, w_down_far, down_in, in_in,
    keep_out, send_out, mg_out, back_out, gf_out, keep, send, act, ug,
    acc, sg, half_rows, w_in, w_down, wo, sems,
):
    c = who[0]
    rows, length, width = g.shape
    half = length // 2
    pairs = width // TILE
    copies = fetches((*feed_weights(w_in_far, w_down_far, chunk, width), wo_far), (w_in, w_down, wo), sems)
    for copy in copies:
        copy.start()
    acc[...] = acc_in[...]
    sg[...] = sg_in[...]
    for copy in copies:
        copy.wait()
    for m in range(rows):
        feed_chunk(m, second, fg, w_in, w_down, act, ug, acc, sg)
    put_block(keep, send, who, 0, 5, down_in)
    put_block(keep, send, who, 1, 5, dot_tn(tall(act), tall(fg)))
    put_block(keep, send, who, 2, 5, in_in)
    put_block(keep, send, who, 3, 5, dot_tn(tall(second), tall(ug)))
    gf = jnp.zeros(gf_out.shape, F32)
    for m in range(rows):
        mid = middle[m]
        held = wide(kept[m], width)
        half_rows[...] = mid + held * acc[m]
        keep_out[m, c] = half_of(half_rows, c, half).astype(BF)
        send_out[m] = half_of(half_rows, 1 - c, half).astype(BF)
        r = lax.rsqrt(jnp.mean(mid * mid, -1, keepdims=True) + EPSILON)
        later = sg[m]
        across = later * mid
        gf = gf + jnp.sum(across * r, 0, keepdims=True)
        inner = jnp.mean(across * fgain[...], -1, keepdims=True)
        mg = g[m].astype(F32) + r * (later * fgain[...]) - mid * (r * r * r * inner)
        mg_out[m] = mg
        branch = (held * mg).astype(BF)
        back = dot_nt(branch, wo[...]).astype(BF)
        attended = jnp.concatenate([att[m, p] for p in range(pairs)], 1)
        for p in range(pairs):
            back_out[m, p] = back[:, p * TILE : (p + 1) * TILE]
        out_now = dot_tn(attended, branch)
        go = out_now if m == 0 else go + out_now
    gf_out[...] = gf
    put_block(keep, send, who, 4, 5, go)


def backward_kernel(
    e_in, q, k, v, inv, att, grad_att,
    dq_out, dk_out, dv_out, diag_out,
    strip,
    *, base,
):
    step = pl.program_id(0)
    pair = step + base
    rows, length = q.shape[0], q.shape[2]
    lane = lax.broadcasted_iota(jnp.int32, (length, TILE), 1)
    low = lane < TILE // 2
    strip[...] = jnp.zeros_like(strip)
    for m in range(rows):
        got = grad_att[m, pair].astype(F32)
        inverse = inv[m, pair]
        scaled = (got * inverse).astype(BF)
        weighed = got * inverse * att[m, pair].astype(F32)
        extra = jnp.zeros((length, TILE), F32)
        for head in range(2):
            mine = low if head == 0 else jnp.logical_not(low)
            centre = -jnp.sum(jnp.where(mine, weighed, 0.0), -1, keepdims=True)
            rough = centre.astype(BF).astype(F32)
            extra = jnp.where(lane == 2 * head, rough, extra)
            extra = jnp.where(lane == 2 * head + 1, centre - rough, extra)
        left = jnp.concatenate([scaled, extra.astype(BF)], 1)
        dq = dk = dv = None
        for head in range(2):
            mine = low if head == 0 else jnp.logical_not(low)
            ones = jnp.where((lane == 2 * head) | (lane == 2 * head + 1), 1.0, 0.0).astype(BF)
            right = jnp.concatenate([jnp.where(mine, v[m, pair], 0), ones], 1)
            e = e_in[m, pair, head]
            ds = e.astype(F32) * dot_nt(left, right)
            for i in range(length // TILE):
                start = length - (i + 1) * TILE
                strip[head, :, start : start + length] += ds[i * TILE : (i + 1) * TILE]
            ds = ds.astype(BF)
            dq_now = dot(ds, jnp.where(mine, k[m, pair], 0))
            dk_now = dot_tn(ds, jnp.where(mine, q[m, pair], 0))
            dv_now = dot_tn(e, jnp.where(mine, scaled, 0))
            dq = dq_now if dq is None else dq + dq_now
            dk = dk_now if dk is None else dk + dk_now
            dv = dv_now if dv is None else dv + dv_now
        dq_out[m, step] = dq.astype(BF)
        dk_out[m, step] = dk.astype(BF)
        dv_out[m, step] = dv.astype(BF)
    lanes = strip.shape[2]
    for head in range(2):
        total = strip[head]
        count = TILE
        while count > 1:
            count //= 2
            total = total[:count] + pltpu.roll(total[count:], lanes - count, 1)
        diag_out[2 * step + head] = total


def joined(grads, m):
    return jnp.concatenate([grad[m, p] for grad in grads for p in range(grad.shape[1])], 1)


def weight_kernel(parts, bucket_count, *refs):
    who, normed = refs[:2]
    dq, dk, dv, diags = (refs[2 + i * parts : 2 + (i + 1) * parts] for i in range(4))
    gf, wq_far, wk_far, wv_far, gain, keep, send, small_out, wq, wk, wv, sems = refs[2 + 4 * parts :]
    rows, length, width = normed.shape
    copies = fetches((wq_far, wk_far, wv_far), (wq, wk, wv), sems)
    for copy in copies:
        copy.start()
    n = tall(normed)
    summed = jnp.zeros((width, 1), F32)
    for place, (grads, weight) in enumerate(((dq, wq), (dk, wk), (dv, wv))):
        value = dot_tn(n, jnp.concatenate([joined(grads, m) for m in range(rows)], 0))
        copies[place].wait()
        summed = summed + jnp.sum(value * weight[...].astype(F32), -1, keepdims=True)
        put_block(keep, send, who, place, 3, value)
    ga = jnp.broadcast_to(summed, (width, TILE)).T[:1] / gain[...]
    lines = jnp.concatenate([diag[h] for diag in diags for h in range(diag.shape[0])], 0)
    buckets = diagonal_buckets(length, bucket_count // 2)
    lane = lax.broadcasted_iota(jnp.int32, (8, width), 1)
    table = jnp.zeros((8, width), F32)
    for b in range(bucket_count):
        total = jnp.sum(jnp.where(buckets == b, lines, 0.0), -1, keepdims=True)
        table = jnp.where(lane == b, total, table)
    small = jnp.concatenate([ga, gf[...], jnp.zeros((6, width), F32), table], 0)
    rough = small.astype(BF)
    small = jnp.concatenate([rough, (small - rough.astype(F32)).astype(BF)], 0)
    small_out[...] = small
    send[send.shape[0] - small.shape[0] :, :] = small


def input_kernel(parts, *refs):
    who, x, mg = refs[:3]
    dq, dk, dv = (refs[3 + i * parts : 3 + (i + 1) * parts] for i in range(3))
    wq_far, wk_far, wv_far, gain, keep_out, send_out, half_rows, wq, wk, wv, sems = refs[3 + 3 * parts :]
    copies = fetches((wq_far, wk_far, wv_far), (wq, wk, wv), sems)
    for copy in copies:
        copy.start()
    c = who[0]
    rows, length, width = x.shape
    half = length // 2
    for m in range(rows):
        back = None
        for i, (grads, weight) in enumerate(((dq, wq), (dk, wk), (dv, wv))):
            if m == 0:
                copies[i].wait()
            now = dot_nt(joined(grads, m), weight[...])
            back = now if back is None else back + now
        xm = x[m].astype(F32)
        r = lax.rsqrt(jnp.mean(xm * xm, -1, keepdims=True) + EPSILON)
        grown = back * gain[...]
        inner = jnp.mean(grown * xm, -1, keepdims=True)
        half_rows[...] = mg[m] + r * grown - xm * (r * r * r * inner)
        keep_out[m, c] = half_of(half_rows, c, half).astype(BF)
        send_out[m] = half_of(half_rows, 1 - c, half).astype(BF)


def take_chunk(k, masks, piece, own, got, chunk):
    places = 1 << LEVELS
    core = 2 * k // places
    place = jnp.bitwise_xor(k % (places // 2), masks[piece, 1 + core])
    start = pl.multiple_of(place * chunk, chunk)
    mine = masks[piece, 0] == core
    return jnp.where(mine, own[pl.ds(start, chunk), :], got[pl.ds(start, chunk), :]).astype(F32)


def feed_result_kernel(masks, a_own, a_got, b_own, b_got, down_out, in_out, o_out, *, splits):
    width = a_own.shape[1]
    count = width >> LEVELS
    before = 0
    for piece, (own, got) in enumerate(((a_own, a_got), (b_own, b_got))):
        for k in range(1 << LEVELS):
            value = take_chunk(k, masks, piece, own, got, own.shape[0] >> (LEVELS - 1))
            rows = slice(k * count, (k + 1) * count)
            for i in range(value.shape[0] // count):
                part = value[i * count : (i + 1) * count]
                block = before + i
                if i < splits[piece]:
                    down_out[block * width + k * count : block * width + (k + 1) * count, :] = part
                elif i < 2 * splits[piece]:
                    block -= splits[piece]
                    in_out[rows, block * width : (block + 1) * width] = part
                else:
                    o_out[rows, :] = part
        before += splits[piece]


def rest_result_kernel(masks, own, got, q_out, k_out, v_out, small_out):
    outs = (q_out, k_out, v_out)
    count = q_out.shape[0] >> LEVELS
    for k in range(1 << LEVELS):
        value = take_chunk(k, masks, 2, own, got, 3 * count)
        for i, out in enumerate(outs):
            out[k * count : (k + 1) * count, :] = value[i * count : (i + 1) * count]
    tail = own.shape[0] - SMALL
    small = jnp.where(masks[2, 0] == 0, own[tail:, :].astype(F32), got[tail:, :].astype(F32))
    small_out[...] = small[: SMALL // 2] + small[SMALL // 2 :]


def land_kernel(has_small, then, *refs):
    kind, after = then
    keep, got = refs[:2]
    refs = refs[2:]
    rows = keep.shape[0]
    if has_small:
        small, refs = refs[0], refs[1:]
    send = refs[0]
    if kind == "gather":
        send[:rows, :] = keep[...]
        send[rows : 2 * rows, :] = got[...]
        if has_small:
            send[2 * rows :, :] = small[...]
        return
    total = (keep[...].astype(F32) + got[:rows, :].astype(F32)).astype(BF)
    if after == "halve":
        refs[1][...] = total[: rows // 2]
        total = total[rows // 2 :]
    send[: total.shape[0], :] = total
    if has_small:
        half = SMALL // 2
        grown = (small[:half, :].astype(F32) + got[rows : rows + half, :].astype(F32)) + (
            small[half:, :].astype(F32) + got[rows + half :, :].astype(F32)
        )
        rough = grown.astype(BF)
        grown = jnp.concatenate([rough, (grown - rough.astype(F32)).astype(BF)], 0)
        refs[-1][...] = grown
        if after != "gather":
            send[total.shape[0] :, :] = grown
            if after != "halve":
                refs[1][...] = total


def swap_pairs(dp, bits):
    if bits is None:
        return [(i, i ^ 1) for i in range(2 * dp)]
    return [(i, i ^ (2 << bits[i % 2])) for i in range(2 * dp)]


class Piece:
    def __init__(self, calls, keep, send, small, order, rest, dp):
        self.calls, self.keep, self.send, self.small, self.dp = calls, keep, send, small, dp
        steps = [("halve", None)] + [("halve", bits) for bits in order]
        steps += [("exchange", (bit, bit)) for bit in rest]
        self.steps = steps + [("gather", bits) for bits in order[::-1]] + [("finish", None)]
        self.got = None
        self.fly()

    def fly(self):
        self.got = lax.ppermute(self.send, ("dp", "seq"), swap_pairs(self.dp, self.steps[0][1]))

    def land(self):
        kind, _ = self.steps.pop(0)
        after = self.steps[0][0]
        rows, width = self.keep.shape
        small = self.small is not None and (kind != "gather" or after == "finish")
        more = SMALL if small and after != "gather" else 0
        sds = lambda count: jax.ShapeDtypeStruct((count, width), BF)
        if kind == "gather":
            outs = [sds(2 * rows + more)]
        elif after == "halve":
            outs = [sds(rows // 2 + more), sds(rows // 2)]
        else:
            outs = [sds(rows + more)] + [sds(rows)] * (more > 0)
        if small and kind != "gather":
            outs.append(sds(SMALL))
        inputs = [self.keep, self.got] + [self.small] * small
        outs = self.calls.call(
            functools.partial(land_kernel, small, (kind, after)), "land", 0.5, inputs, [whole()] * len(inputs), outs
        )
        self.send = outs[0]
        if small and kind != "gather":
            self.small = outs[-1]
        split = kind != "gather" and (after == "halve" or more > 0)
        self.keep = outs[1] if split else outs[0]
        self.fly()
        return self

    def done(self):
        while len(self.steps) > 1:
            self.land()
        return self.send, self.got


def on_device(
    tokens, cotangent, segments, pad_mask, row_counts, attend_gain, w_query, w_key, w_value, w_out,
    forward_gain, w_in, w_down, position_bias_table,
):
    rows, slots, half, width = tokens.shape
    dp, seq = lax.axis_size("dp"), lax.axis_size("seq")
    bits = dp.bit_length() - 1
    assert seq == 2 and slots == 2 and dp == 1 << bits and bits >= 3
    length = seq * half
    inner = w_query.shape[1]
    ff = w_in.shape[1]
    bucket_count, heads = position_bias_table.shape
    pairs = inner // TILE
    assert heads == 2 * pairs == 8 and inner == width
    blocks = ff // width
    assert blocks == SPLIT + 2
    splits = (SPLIT, 2)
    me = lax.axis_index("dp")
    c = lax.axis_index("seq")
    orders = ([(0, 1), (1, 0), (2, 2)], [(2, 2), (0, 1), (1, 0)], [(0, 1), (1, 0), (2, 2)])
    rest = list(range(3, bits))

    def mask_of(order, core):
        mask = 0
        for pair in order:
            mask = 2 * mask + ((me >> pair[core]) & 1)
        return mask

    who = [jnp.stack([c, mask_of(order, 0), mask_of(order, 1)]).astype(jnp.int32) for order in orders]
    masks = jnp.stack(who)
    swap = lambda a: lax.ppermute(a, ("dp", "seq"), swap_pairs(dp, None))
    tokens, cotangent, w_query, w_key, w_value, w_out, w_in, w_down = (
        pltpu.with_memory_space_constraint(array, pltpu.HBM)
        for array in (tokens, cotangent, w_query, w_key, w_value, w_out, w_in, w_down)
    )
    table = jnp.broadcast_to(position_bias_table[:, :, None], (bucket_count, heads, 1))
    gain, fgain = attend_gain.reshape(1, width), forward_gain.reshape(1, width)
    sds = jax.ShapeDtypeStruct
    vm = pltpu.VMEM
    dma = pltpu.SemaphoreType.DMA
    paired = sds((rows, pairs, length, TILE), BF)
    wide_bf, wide_f32 = sds((rows, length, width), BF), sds((rows, length, width), F32)
    narrow, items = sds((rows, length, TILE), F32), sds((rows, length, TILE), BF)
    square, square_bf = sds((inner, width), F32), sds((inner, width), BF)
    row_half, marked = sds((rows, half, width), BF), sds((2, rows, half), jnp.int32)
    calls = Order()
    call = calls.call

    tok_own, tok_send, cot_own, cot_send, marks_own, marks_send = call(
        pick_kernel, "pick", 2, (who[0], tokens, cotangent, segments, pad_mask),
        [smem(), far(), far(), whole(), whole()],
        (row_half, row_half, row_half, row_half, marked, marked),
        scratch=[dma((4 * rows,))],
    )
    tok_got, marks_got, cot_got = swap(tok_send), swap(marks_send), swap(cot_send)
    x, normed, q, k, v, e, inv, att, kept, middle, second, _, _ = call(
        forward_kernel, "attend_forward", 14,
        (
            who[0], row_counts.reshape(rows), tok_own, tok_got, marks_own, marks_got, table, gain, fgain,
            w_query, w_key, w_value, w_out,
        ),
        [smem(), smem()] + [whole()] * 7 + [far()] * 4,
        (
            wide_bf, wide_bf, paired, paired, paired, sds((rows, pairs, 2, length, length), BF),
            sds((rows, pairs, length, TILE), F32), paired, narrow, wide_f32, wide_bf, items, items,
        ),
        grid=pairs,
        scratch=[vm((heads, 1, 2 * length), F32)] + [vm((width, inner), BF)] * 4 + [dma((4,))],
    )

    block = vm((width, width), BF)
    piece_halves = lambda count, more=0: (sds((count * width // 2, width), BF), sds((count * width // 2 + more, width), BF))
    g, fg, acc, sg, keep, send, _, _ = call(
        functools.partial(feed_first_kernel, steps=splits[0]), "feed_first", 5 * splits[0],
        (who[0], cot_own, cot_got, kept, second, w_in, w_down),
        [smem()] + [whole()] * 4 + [far()] * 2,
        (wide_bf, wide_bf, wide_f32, wide_f32, *piece_halves(2 * splits[0]), wide_bf, wide_bf),
        grid=splits[0],
        scratch=[vm((splits[0], width, width), BF)] * 2 + [dma((splits[0], 2))],
    )
    a = Piece(calls, keep, send, None, orders[0], rest, dp)
    acc, sg, down_block, in_block, _, _ = call(
        functools.partial(feed_second_kernel, splits[0]), "feed_second", 6, (fg, acc, sg, second, w_in, w_down),
        [whole()] * 4 + [far()] * 2,
        (wide_f32, wide_f32, square_bf, square_bf, wide_bf, wide_bf),
        scratch=[block, block, dma((2,))],
    )
    a.land()
    out_keep, out_send, mg, grad_att, gf, keep, send, _, _ = call(
        functools.partial(feed_third_kernel, splits[0] + 1), "feed_third", 8,
        (who[1], g, fg, acc, sg, kept, middle, second, att, fgain, w_out, w_in, w_down, down_block, in_block),
        [smem()] + [whole()] * 9 + [far()] * 3 + [whole()] * 2,
        (
            sds((rows, slots, half, width), BF), row_half, wide_f32, paired, sds((1, width), F32),
            *piece_halves(5), wide_bf, wide_bf,
        ),
        scratch=[vm((rows, length, width), F32)] * 2 + [vm((length, width), F32), block, block, block, dma((3,))],
    )
    b = Piece(calls, keep, send, None, orders[1], rest, dp)
    a.land()

    some = sds((rows, pairs // PARTS, length, TILE), BF)
    dq, dk, dv, diag = [], [], [], []
    for part in range(PARTS):
        base = part * (pairs // PARTS)
        outs = call(
            functools.partial(backward_kernel, base=base), "attend_backward", 12 / PARTS,
            (e, q, k, v, inv, att, grad_att), [whole()] * 7,
            (some, some, some, sds((heads // PARTS, 1, 2 * length), F32)),
            grid=pairs // PARTS,
            scratch=[vm((2, TILE, 2 * length), F32)],
        )
        for kept_list, out in zip((dq, dk, dv, diag), outs):
            kept_list.append(out)
        if part % 2 == 0:
            b.land()
        else:
            a.land()
    keep, send, small = call(
        functools.partial(weight_kernel, PARTS, bucket_count), "weight_grads", 3,
        (who[2], normed, *dq, *dk, *dv, *diag, gf, w_query, w_key, w_value, gain),
        [smem()] + [whole()] * (2 + 4 * PARTS) + [far()] * 3 + [whole()],
        (*piece_halves(3, SMALL), sds((SMALL, width), BF)),
        scratch=[block, block, block, dma((3,))],
    )
    c_piece = Piece(calls, keep, send, small, orders[2], rest, dp)
    a.land()
    c_piece.land()
    in_keep, in_send = call(
        functools.partial(input_kernel, PARTS), "input_grad", 4,
        (who[2], x, mg, *dq, *dk, *dv, w_query, w_key, w_value, gain),
        [smem()] + [whole()] * (2 + 3 * PARTS) + [far()] * 3 + [whole()],
        (sds((rows, slots, half, width), BF), row_half),
        scratch=[vm((length, width), F32), block, block, block, dma((3,))],
    )
    out_got, in_got = swap(out_send), swap(in_send)
    while len(c_piece.steps) > 1:
        c_piece.land()
        for piece in (a, b):
            if len(piece.steps) > 1:
                piece.land()
        if len(c_piece.steps) == 2:
            a_done, b_done = a.done(), b.done()
            grad_down, grad_in, grad_out = call(
                functools.partial(feed_result_kernel, splits=splits), "feed_result", 4,
                (masks, *a_done, *b_done), [smem()] + [whole()] * 4,
                (sds((ff, width), F32), sds((width, ff), F32), square),
            )
    grad_query, grad_key, grad_value, smalls = call(
        rest_result_kernel, "rest_result", 3,
        (masks, *c_piece.done()), [smem()] + [whole()] * 2,
        (square, square, square, sds((SMALL // 2, width), F32)),
    )

    place = lambda keep, got: lax.dynamic_update_index_in_dim(keep, got[:, None], 1 - c, 1)
    return (
        place(out_keep, out_got),
        place(in_keep, in_got),
        smalls[0],
        grad_query,
        grad_key,
        grad_value,
        grad_out,
        smalls[1],
        grad_in,
        grad_down,
        smalls[8 : 8 + heads, :bucket_count].T,
    )


def solution(mesh):
    placed = (P(None, "dp", "seq", None),) * 2 + (P(None, "dp", "seq"),) * 2 + (P(None, "dp"),) + (P(),) * 9
    return jax.shard_map(
        on_device,
        mesh=mesh,
        in_specs=placed,
        out_specs=(P(None, "dp", "seq", None),) * 2 + (P(),) * 9,
        check_vma=False,
    )
```

```python
import functools
import math

import jax
import jax.numpy as jnp
from jax import lax
from jax.experimental import pallas as pl
from jax.experimental.pallas import tpu as pltpu
from jax.sharding import PartitionSpec as P

EPSILON = 1e-06
MASKED = -1000000000.0
LIMITS = (12, 16, 23, 32, 46, 64, 91)
BF = jnp.bfloat16
F32 = jnp.float32
TILE = 128
LEVELS = 4
SPLIT = 2
SMALL = 32
PARTS = 2
ORDERS = ([(0, 2), (1, 0), (2, 1)], [(1, 0), (0, 1), (2, 2)])
VMEM = (16, 14, 12, 16, 12, 10, 10, 14)


def whole():
    return pl.BlockSpec(memory_space=pltpu.VMEM)


def hbm():
    return pl.BlockSpec(memory_space=pl.ANY)


def far():
    return pl.BlockSpec(memory_space=pltpu.HBM)


def smem():
    return pl.BlockSpec(memory_space=pltpu.SMEM)


class Order:
    def __init__(self):
        self.token = None

    def call(self, kernel, name, micros, inputs, in_specs, out_shape, grid=1, out_specs=None, scratch=(), vmem=8, aliases=None):
        count, results = len(inputs), len(out_shape)
        extra = () if self.token is None or name in ("pick_rest", "attend_forward", "feed_first", "feed_second", "feed_third") else (self.token,)

        def body(*refs):
            token = refs[count + len(extra) + results]
            token[...] = jnp.zeros_like(token)
            kernel(*refs[:count], *refs[count + len(extra) : count + len(extra) + results], *refs[count + len(extra) + results + 1 :])

        *outs, self.token = pl.pallas_call(
            body,
            grid=(grid,),
            in_specs=list(in_specs) + [whole()] * len(extra),
            out_specs=list(out_specs or [whole() for _ in out_shape]) + [whole()],
            out_shape=(*out_shape, jax.ShapeDtypeStruct((8, TILE), F32)),
            scratch_shapes=list(scratch),
            input_output_aliases=aliases or {},
            compiler_params=pltpu.CompilerParams(vmem_limit_bytes=vmem * 1024 * 1024),
            cost_estimate=pl.CostEstimate(
                flops=int(micros * 1e9), bytes_accessed=int(micros * 1e6), transcendentals=0
            ),
            name=name,
        )(*inputs, *extra)
        return outs


def dot(a, b, contract=((1,), (0,))):
    return lax.dot_general(a, b, (contract, ((), ())), preferred_element_type=F32)


def dot_nt(a, b):
    return dot(a, b, ((1,), (1,)))


def dot_tn(a, b):
    return dot(a, b, ((0,), (0,)))


def bucket_of(relative, half_count):
    distance = jnp.abs(relative)
    far = jnp.full(relative.shape, 8, jnp.int32)
    for bound in LIMITS:
        far = far + (distance >= bound).astype(jnp.int32)
    near_or_far = jnp.where(distance < 8, distance, far)
    return near_or_far + jnp.where(relative > 0, half_count, 0)


def diagonal_buckets(length, half_count):
    lane = lax.broadcasted_iota(jnp.int32, (8, 2 * length), 1)
    relative = lane - (length - TILE)
    relative = jnp.where(lane < 2 * length - TILE, relative, relative - 2 * length)
    return bucket_of(relative, half_count)


def wide(column, width):
    return jnp.concatenate([column] * (width // TILE), axis=1)


def put_block(keep, send, who, block, blocks, value):
    count = value.shape[0] >> LEVELS
    places = 1 << LEVELS
    for core in range(2):

        @pl.when(who[0] == core)
        def _():
            for k in range(places):
                place = jnp.bitwise_xor(k % (places // 2), who[1 + 2 * k // places])
                start = pl.multiple_of((place * blocks + block) * count, count)
                ref = keep if 2 * k // places == core else send
                ref[pl.ds(start, count), :] = value[k * count : (k + 1) * count].astype(ref.dtype)


def half_of(ref, i, half):
    return ref[pl.ds(pl.multiple_of(i * half, half), half), :]


def fill_row(row_ref, own_ref, got_ref, m, c, half):
    row_ref[m, pl.ds(pl.multiple_of(c * half, half), half), :] = own_ref[m]
    row_ref[m, pl.ds(pl.multiple_of((1 - c) * half, half), half), :] = got_ref[m]
    return row_ref[m]


def join(own, got, c):
    return jnp.where(c == 0, jnp.concatenate([own, got], 1), jnp.concatenate([got, own], 1))


def fetches(sources, targets, sems):
    return [pltpu.make_async_copy(a, b, sems.at[i]) for i, (a, b) in enumerate(zip(sources, targets))]


def feed_weights(w_in, w_down, chunk, width):
    start = pl.multiple_of(chunk * width, width)
    return w_in.at[:, pl.ds(start, width)], w_down.at[pl.ds(start, width), :]


def pick_kernel(who, tok, seg, pad, tok_send, marks_own, marks_send, sems):
    c = who[0]
    rows = tok.shape[0]
    copies = [pltpu.make_async_copy(tok.at[m, 1 - c], tok_send.at[m], sems.at[m]) for m in range(rows)]
    for copy in copies:
        copy.start()
    for kind, marks in enumerate((seg, pad)):
        for m in range(rows):
            first, second = marks[m, pl.ds(0, 1)], marks[m, pl.ds(1, 1)]
            marks_own[kind, pl.ds(m, 1)] = jnp.where(c == 0, first, second)
            marks_send[kind, pl.ds(m, 1)] = jnp.where(c == 0, second, first)
    for copy in copies:
        copy.wait()


def pick_rest_kernel(who, tok, cot, tok_own, cot_own, cot_send, sems):
    c = who[0]
    copies = []
    for m in range(tok.shape[0]):
        for source, slot, target in ((tok, c, tok_own), (cot, 1 - c, cot_send), (cot, c, cot_own)):
            copies.append(pltpu.make_async_copy(source.at[m, slot], target.at[m], sems.at[len(copies)]))
    for copy in copies:
        copy.start()
    for copy in copies:
        copy.wait()


def place_kernel(who, *refs):
    c = who[0]
    count = (len(refs) - 1) // 3
    sems = refs[-1]
    copies = []
    for i in range(count):
        own, got, out = refs[2 * i], refs[2 * i + 1], refs[2 * count + i]
        for m in range(own.shape[0]):
            for source, slot in ((own, c), (got, 1 - c)):
                copies.append(pltpu.make_async_copy(source.at[m], out.at[m, slot], sems.at[len(copies)]))
    for copy in copies:
        copy.start()
    for copy in copies:
        copy.wait()


def forward_kernel(
    who, counts, own, got, marks, marks_got, table, gain, fgain, wq_far, wk_far, wv_far, wo_far,
    x_out, normed_out, q_out, k_out, v_out, e_out, inv_out, att_out, kept_out, middle_out, second_out,
    segq, segk, diag, wq, wk, wv, wo, sems,
):
    c = who[0]
    pair = pl.program_id(0)
    rows, half = own.shape[0], own.shape[1]
    length = 2 * half
    pairs = wq.shape[1] // TILE
    bucket_count = table.shape[0]
    copies = fetches((wq_far, wk_far, wv_far, wo_far), (wq, wk, wv, wo), sems)

    @pl.when(pair == 0)
    def _():
        for copy in copies:
            copy.start()
        buckets = diagonal_buckets(length, bucket_count // 2)
        strip = jnp.zeros(buckets.shape, F32)
        for b in range(bucket_count):
            strip = jnp.where(buckets == b, table[b], strip)
        for h in range(strip.shape[0]):
            diag[h] = strip[h : h + 1]
        for m in range(rows):
            x = fill_row(x_out, own, got, m, c, half).astype(F32)
            r = lax.rsqrt(jnp.mean(x * x, -1, keepdims=True) + EPSILON)
            normed = (x * r * gain[...]).astype(BF)
            normed_out[m] = normed
            if m == 0:
                for copy in copies:
                    copy.wait()
            for w, out in ((wq, q_out), (wk, k_out), (wv, v_out)):
                projected = dot(normed, w[...]).astype(BF)
                for p in range(pairs):
                    out[m, p] = projected[:, p * TILE : (p + 1) * TILE]
            seg = join(marks[0, pl.ds(m, 1)], marks_got[0, pl.ds(m, 1)], c)
            pad = join(marks[1, pl.ds(m, 1)], marks_got[1, pl.ds(m, 1)], c)
            kept = (pad > 0) & (counts[m] > c)
            item = lax.broadcasted_iota(jnp.int32, (TILE, length), 0)
            same = item == seg
            segq[m] = jnp.where(same, 1.0, 0.0).T.astype(BF)
            segk[m] = jnp.where(same & kept, 0.0, MASKED).T.astype(BF)
            kept_out[m] = jnp.broadcast_to(jnp.where(kept, 1.0, 0.0), (TILE, length)).T

    lane = lax.broadcasted_iota(jnp.int32, (length, TILE), 1)
    for head in range(2):
        mine = (lane < TILE // 2) if head == 0 else (lane >= TILE // 2)
        line = jnp.broadcast_to(diag[2 * pair + head], (TILE, 2 * length))
        strip = pltpu.roll(line, 0, 1, stride=1, stride_axis=0)
        bias = jnp.concatenate(
            [strip[:, length - (i + 1) * TILE : 2 * length - (i + 1) * TILE] for i in range(length // TILE)], 0
        )
        for m in range(rows):
            query = jnp.concatenate([q_out[m, pair], segq[m]], 1)
            key = jnp.concatenate([jnp.where(mine, k_out[m, pair], 0), segk[m]], 1)
            value = jnp.concatenate([jnp.where(mine, v_out[m, pair], 0), jnp.where(mine, 1.0, 0.0).astype(BF)], 1)
            scores = dot_nt(query, key) + bias
            e = jnp.exp(scores - jnp.max(scores, -1, keepdims=True)).astype(BF)
            e_out[m, 0, head] = e
            weighed = dot(e, value)
            if head == 0:
                att_acc = weighed
                inv_out[m, pair] = att_acc[:, TILE:]
                half_att = att_acc[:, :TILE]
                middle_out[m, :, :TILE] = half_att
            else:
                inv = 1.0 / (inv_out[m, pair] + weighed[:, TILE:])
                inv_out[m, pair] = inv
                att_out[m, pair] = ((middle_out[m, :, :TILE] + weighed[:, :TILE]) * inv).astype(BF)

    @pl.when(pair == pairs - 1)
    def _():
        for m in range(rows):
            attended = jnp.concatenate([att_out[m, p] for p in range(pairs)], 1)
            branch = dot(attended, wo[...])
            middle = x_out[m].astype(F32) + wide(kept_out[m], branch.shape[1]) * branch
            middle_out[m] = middle
            r = lax.rsqrt(jnp.mean(middle * middle, -1, keepdims=True) + EPSILON)
            second_out[m] = (middle * r * fgain[...]).astype(BF)


def gelu_parts(u):
    z = jnp.abs(u) * (0.5**0.5)
    t = 1.0 / (1.0 + 0.3275911 * z)
    bell = jnp.exp(u * u * -0.5)
    poly = ((((1.061405429 * t - 1.453152027) * t + 1.421413741) * t - 0.284496736) * t + 0.254829592) * t
    tail = 0.5 * poly * bell
    upper = jnp.where(u >= 0, 1.0 - tail, tail)
    return upper, u * bell * ((2.0 * math.pi) ** -0.5)


def feed_chunk(second, fg, w_in, w_down, acc, sg):
    down = into = None
    for m in range(second.shape[0]):
        u = dot(second[m], w_in[...])
        upper, slope = gelu_parts(u)
        active = (u * upper).astype(BF)
        acc[m] += dot(active, w_down[...])
        up = (dot_nt(fg[m], w_down[...]) * (upper + slope)).astype(BF)
        sg[m] += dot_nt(up, w_in[...])
        down_now, into_now = dot_tn(active, fg[m]), dot_tn(second[m], up)
        down = down_now if m == 0 else down + down_now
        into = into_now if m == 0 else into + into_now
    return down, into


def tall(ref):
    return jnp.concatenate([ref[m] for m in range(ref.shape[0])], 0)


def feed_first_kernel(
    who, own, got, kept, second, w_in_far, w_down_far,
    g_out, fg_out, acc_out, sg_out, down_out, in_out,
    w_ins, w_downs, sems,
    *, steps,
):
    step = pl.program_id(0)
    rows, half, width = own.shape
    copies = [
        fetches(feed_weights(w_in_far, w_down_far, i, width), (w_ins.at[i], w_downs.at[i]), sems.at[i])
        for i in range(steps)
    ]

    @pl.when(step == 0)
    def _():
        for copy in sum(copies, []):
            copy.start()
        for m in range(rows):
            g = fill_row(g_out, own, got, m, who[0], half)
            fg_out[m] = (g.astype(F32) * wide(kept[m], g.shape[1])).astype(BF)
        acc_out[...] = jnp.zeros_like(acc_out)
        sg_out[...] = jnp.zeros_like(sg_out)

    for i in range(steps):

        @pl.when(step == i)
        def _():
            for copy in copies[i]:
                copy.wait()

    down, into = feed_chunk(second, fg_out, w_ins.at[step], w_downs.at[step], acc_out, sg_out)
    down_out[step] = down.astype(BF)
    in_out[step] = into.astype(BF)


def feed_second_kernel(
    chunk, fg, acc_in, sg_in, second, w_in_far, w_down_far,
    acc, sg, down_out, in_out,
    w_in, w_down, sems,
):
    copies = fetches(feed_weights(w_in_far, w_down_far, chunk, fg.shape[2]), (w_in, w_down), sems)
    for copy in copies:
        copy.start()
    for copy in copies:
        copy.wait()
    down, into = feed_chunk(second, fg, w_in, w_down, acc, sg)
    down_out[...] = down.astype(BF)
    in_out[...] = into.astype(BF)


def feed_third_kernel(
    chunk, who, g, fg, acc_in, sg_in, kept, middle, second, att, fgain, wo_far, w_in_far, w_down_far, down_first, in_first, down_in, in_in,
    acc, sg, keep_out, send_out, mg_out, back_out, gf_out, keep, send,
    half_rows, w_in, w_down, wo, sems,
):
    c = who[0]
    rows, length, width = g.shape
    half = length // 2
    pairs = width // TILE
    copies = fetches((*feed_weights(w_in_far, w_down_far, chunk, width), wo_far), (w_in, w_down, wo), sems)
    for copy in copies:
        copy.start()
    for copy in copies:
        copy.wait()
    down, into = feed_chunk(second, fg, w_in, w_down, acc, sg)
    steps = down_first.shape[0] + 2
    blocks = 2 * steps + 1
    for i in range(steps - 2):
        put_block(keep, send, who, i, blocks, down_first[i])
        put_block(keep, send, who, steps + i, blocks, in_first[i])
    put_block(keep, send, who, steps - 2, blocks, down_in[...])
    put_block(keep, send, who, steps - 1, blocks, down)
    put_block(keep, send, who, 2 * steps - 2, blocks, in_in[...])
    put_block(keep, send, who, 2 * steps - 1, blocks, into)
    gf = jnp.zeros(gf_out.shape, F32)
    for m in range(rows):
        mid = middle[m]
        held = wide(kept[m], width)
        half_rows[...] = mid + held * acc[m]
        keep_out[m] = half_of(half_rows, c, half).astype(BF)
        send_out[m] = half_of(half_rows, 1 - c, half).astype(BF)
        r = lax.rsqrt(jnp.mean(mid * mid, -1, keepdims=True) + EPSILON)
        later = sg[m]
        across = later * mid
        gf = gf + jnp.sum(across * r, 0, keepdims=True)
        inner = jnp.mean(across * fgain[...], -1, keepdims=True)
        mg = g[m].astype(F32) + r * (later * fgain[...]) - mid * (r * r * r * inner)
        mg_out[m] = mg
        branch = (held * mg).astype(BF)
        back = dot_nt(branch, wo[...]).astype(BF)
        attended = jnp.concatenate([att[m, p] for p in range(pairs)], 1)
        for p in range(pairs):
            back_out[m, p] = back[:, p * TILE : (p + 1) * TILE]
        out_now = dot_tn(attended, branch)
        go = out_now if m == 0 else go + out_now
    gf_out[...] = gf
    put_block(keep, send, who, 2 * steps, blocks, go)


def backward_kernel(
    e_in, q, k, v, inv, att, grad_att,
    dq_out, dk_out, dv_out, diag_out,
    strip,
    *, base,
):
    step = pl.program_id(0)
    pair = step + base
    rows, length = q.shape[0], q.shape[2]
    lane = lax.broadcasted_iota(jnp.int32, (length, TILE), 1)
    low = lane < TILE // 2
    strip[...] = jnp.zeros_like(strip)
    for m in range(rows):
        got = grad_att[m, pair].astype(F32)
        inverse = inv[m, pair]
        scaled = (got * inverse).astype(BF)
        weighed = got * inverse * att[m, pair].astype(F32)
        extra = jnp.zeros((length, TILE), F32)
        for head in range(2):
            mine = low if head == 0 else jnp.logical_not(low)
            centre = -jnp.sum(jnp.where(mine, weighed, 0.0), -1, keepdims=True)
            rough = centre.astype(BF).astype(F32)
            extra = jnp.where(lane == 2 * head, rough, extra)
            extra = jnp.where(lane == 2 * head + 1, centre - rough, extra)
        left = jnp.concatenate([scaled, extra.astype(BF)], 1)
        dq = dk = dv = None
        for head in range(2):
            mine = low if head == 0 else jnp.logical_not(low)
            ones = jnp.where((lane == 2 * head) | (lane == 2 * head + 1), 1.0, 0.0).astype(BF)
            right = jnp.concatenate([jnp.where(mine, v[m, pair], 0), ones], 1)
            e = e_in[m, 0, head]
            ds = e.astype(F32) * dot_nt(left, right)
            for i in range(length // TILE):
                start = length - (i + 1) * TILE
                strip[head, :, start : start + length] += ds[i * TILE : (i + 1) * TILE]
            ds = ds.astype(BF)
            dq_now = dot(ds, jnp.where(mine, k[m, pair], 0))
            dk_now = dot_tn(ds, jnp.where(mine, q[m, pair], 0))
            dv_now = dot_tn(e, jnp.where(mine, scaled, 0))
            dq = dq_now if dq is None else dq + dq_now
            dk = dk_now if dk is None else dk + dk_now
            dv = dv_now if dv is None else dv + dv_now
        dq_out[m, step] = dq.astype(BF)
        dk_out[m, step] = dk.astype(BF)
        dv_out[m, step] = dv.astype(BF)
    lanes = strip.shape[2]
    for head in range(2):
        total = strip[head]
        count = TILE
        while count > 1:
            count //= 2
            total = total[:count] + pltpu.roll(total[count:], lanes - count, 1)
        diag_out[2 * step + head] = total


def joined(grads, m):
    return jnp.concatenate([grad[m, p] for grad in grads for p in range(grad.shape[1])], 1)


def weight_kernel(parts, bucket_count, *refs):
    who, normed = refs[:2]
    dq, dk, dv, diags = (refs[2 + i * parts : 2 + (i + 1) * parts] for i in range(4))
    gf, wq_far, wk_far, wv_far, gain, keep, send, small_out, wq, wk, wv, sems = refs[2 + 4 * parts :]
    rows, length, width = normed.shape
    copies = fetches((wq_far, wk_far, wv_far), (wq, wk, wv), sems)
    for copy in copies:
        copy.start()
    n = tall(normed)
    summed = jnp.zeros((width, 1), F32)
    for place, (grads, weight) in enumerate(((dq, wq), (dk, wk), (dv, wv))):
        value = dot_tn(n, jnp.concatenate([joined(grads, m) for m in range(rows)], 0))
        copies[place].wait()
        summed = summed + jnp.sum(value * weight[...].astype(F32), -1, keepdims=True)
        put_block(keep, send, who, place, 3, value)
    ga = jnp.broadcast_to(summed, (width, TILE)).T[:1] / gain[...]
    lines = jnp.concatenate([diag[h] for diag in diags for h in range(diag.shape[0])], 0)
    buckets = diagonal_buckets(length, bucket_count // 2)
    lane = lax.broadcasted_iota(jnp.int32, (8, width), 1)
    table = jnp.zeros((8, width), F32)
    for b in range(bucket_count):
        total = jnp.sum(jnp.where(buckets == b, lines, 0.0), -1, keepdims=True)
        table = jnp.where(lane == b, total, table)
    small = jnp.concatenate([ga, gf[...], jnp.zeros((6, width), F32), table], 0)
    rough = small.astype(BF)
    small = jnp.concatenate([rough, (small - rough.astype(F32)).astype(BF)], 0)
    small_out[...] = small
    send[send.shape[0] - small.shape[0] :, :] = small


def input_kernel(parts, *refs):
    who, x, mg = refs[:3]
    dq, dk, dv = (refs[3 + i * parts : 3 + (i + 1) * parts] for i in range(3))
    wq_far, wk_far, wv_far, gain, keep_out, send_out, half_rows, wq, wk, wv, sems = refs[3 + 3 * parts :]
    copies = fetches((wq_far, wk_far, wv_far), (wq, wk, wv), sems)
    for copy in copies:
        copy.start()
    c = who[0]
    rows, length, width = x.shape
    half = length // 2
    for m in range(rows):
        back = None
        for i, (grads, weight) in enumerate(((dq, wq), (dk, wk), (dv, wv))):
            if m == 0:
                copies[i].wait()
            now = dot_nt(joined(grads, m), weight[...])
            back = now if back is None else back + now
        xm = x[m].astype(F32)
        r = lax.rsqrt(jnp.mean(xm * xm, -1, keepdims=True) + EPSILON)
        grown = back * gain[...]
        inner = jnp.mean(grown * xm, -1, keepdims=True)
        half_rows[...] = mg[m] + r * grown - xm * (r * r * r * inner)
        keep_out[m] = half_of(half_rows, c, half).astype(BF)
        send_out[m] = half_of(half_rows, 1 - c, half).astype(BF)


def take_chunk(k, masks, piece, own, got, chunk):
    places = 1 << LEVELS
    core = 2 * k // places
    place = jnp.bitwise_xor(k % (places // 2), masks[piece, 1 + core])
    start = pl.multiple_of(place * chunk, chunk)
    mine = masks[piece, 0] == core
    return jnp.where(mine, own[pl.ds(start, chunk), :], got[pl.ds(start, chunk), :]).astype(F32)


def feed_result_kernel(masks, own, got, down_out, in_out, o_out):
    width = own.shape[1]
    count = width >> LEVELS
    steps = down_out.shape[0] // width
    for k in range(1 << LEVELS):
        value = take_chunk(k, masks, 0, own, got, own.shape[0] >> (LEVELS - 1))
        rows = slice(k * count, (k + 1) * count)
        for i in range(2 * steps + 1):
            part = value[i * count : (i + 1) * count]
            if i < steps:
                down_out[i * width + k * count : i * width + (k + 1) * count, :] = part
            elif i < 2 * steps:
                in_out[rows, (i - steps) * width : (i - steps + 1) * width] = part
            else:
                o_out[rows, :] = part


def rest_result_kernel(masks, own, got, q_out, k_out, v_out, ga_out, gf_out, table_out):
    outs = (q_out, k_out, v_out)
    count = q_out.shape[0] >> LEVELS
    for k in range(1 << LEVELS):
        value = take_chunk(k, masks, 1, own, got, 3 * count)
        for i, out in enumerate(outs):
            out[k * count : (k + 1) * count, :] = value[i * count : (i + 1) * count]
    tail = own.shape[0] - SMALL
    small = jnp.where(masks[1, 0] == 0, own[tail:, :].astype(F32), got[tail:, :].astype(F32))
    small = small[: SMALL // 2] + small[SMALL // 2 :]
    ga_out[...] = small[:1]
    gf_out[...] = small[1:2]
    table = jnp.concatenate([small[8:, :TILE], jnp.zeros((TILE - 8, TILE), F32)], 0).T
    table_out[...] = table[: table_out.shape[0], : table_out.shape[1]]


def land_kernel(has_small, then, *refs):
    kind, after = then
    keep, got = refs[:2]
    refs = refs[2:]
    rows = keep.shape[0]
    if has_small:
        small, refs = refs[0], refs[1:]
    send = refs[0]
    if kind == "gather":
        send[:rows, :] = keep[...]
        send[rows : 2 * rows, :] = got[...]
        if has_small:
            send[2 * rows :, :] = small[...]
        return
    total = (keep[...].astype(F32) + got[:rows, :].astype(F32)).astype(BF)
    if after == "halve":
        refs[1][...] = total[: rows // 2]
        total = total[rows // 2 :]
    send[: total.shape[0], :] = total
    if has_small:
        half = SMALL // 2
        grown = (small[:half, :].astype(F32) + got[rows : rows + half, :].astype(F32)) + (
            small[half:, :].astype(F32) + got[rows + half :, :].astype(F32)
        )
        rough = grown.astype(BF)
        grown = jnp.concatenate([rough, (grown - rough.astype(F32)).astype(BF)], 0)
        refs[-1][...] = grown
        if after != "gather":
            send[total.shape[0] :, :] = grown
            if after != "halve":
                refs[1][...] = total


def swap_pairs(dp, bits):
    if bits is None:
        return [(i, i ^ 1) for i in range(2 * dp)]
    return [(i, i ^ (2 << bits[i % 2])) for i in range(2 * dp)]


class Piece:
    def __init__(self, calls, keep, send, small, order, rest, dp):
        self.calls, self.keep, self.send, self.small, self.dp = calls, keep, send, small, dp
        steps = [("halve", None)] + [("halve", bits) for bits in order]
        steps += [("exchange", (bit, bit)) for bit in rest]
        self.steps = steps + [("gather", bits) for bits in order[::-1]] + [("finish", None)]
        self.got = None
        self.fly()

    def fly(self):
        self.got = lax.ppermute(self.send, ("dp", "seq"), swap_pairs(self.dp, self.steps[0][1]))

    def land(self):
        kind, _ = self.steps.pop(0)
        after = self.steps[0][0]
        rows, width = self.keep.shape
        small = self.small is not None and (kind != "gather" or after == "finish")
        more = SMALL if small and after != "gather" else 0
        sds = lambda count: jax.ShapeDtypeStruct((count, width), BF)
        if kind == "gather":
            outs = [sds(2 * rows + more)]
        elif after == "halve":
            outs = [sds(rows // 2 + more), sds(rows // 2)]
        else:
            outs = [sds(rows + more)] + [sds(rows)] * (more > 0)
        if small and kind != "gather":
            outs.append(sds(SMALL))
        inputs = [self.keep, self.got] + [self.small] * small
        outs = self.calls.call(
            functools.partial(land_kernel, small, (kind, after)), "land", 0.5, inputs, [whole()] * len(inputs), outs
        )
        self.send = outs[0]
        if small and kind != "gather":
            self.small = outs[-1]
        split = kind != "gather" and (after == "halve" or more > 0)
        self.keep = outs[1] if split else outs[0]
        self.fly()
        return self

    def done(self):
        while len(self.steps) > 1:
            self.land()
        return self.send, self.got


def on_device(
    tokens, cotangent, segments, pad_mask, row_counts, attend_gain, w_query, w_key, w_value, w_out,
    forward_gain, w_in, w_down, position_bias_table,
):
    rows, slots, half, width = tokens.shape
    dp, seq = lax.axis_size("dp"), lax.axis_size("seq")
    bits = dp.bit_length() - 1
    assert seq == 2 and slots == 2 and dp == 1 << bits and bits >= 3
    length = seq * half
    inner = w_query.shape[1]
    ff = w_in.shape[1]
    bucket_count, heads = position_bias_table.shape
    pairs = inner // TILE
    assert heads == 2 * pairs == 8 and inner == width
    blocks = ff // width
    assert blocks == SPLIT + 2
    splits = (SPLIT, 2)
    me = lax.axis_index("dp")
    c = lax.axis_index("seq")
    orders = ORDERS
    rests = [[bit for bit in range(bits) if all(bit not in pair for pair in order)] for order in orders]

    def mask_of(order, core):
        mask = 0
        for pair in order:
            mask = 2 * mask + ((me >> pair[core]) & 1)
        return mask

    who = [jnp.stack([c, mask_of(order, 0), mask_of(order, 1)]).astype(jnp.int32) for order in orders]
    masks = jnp.stack(who)
    swap = lambda a: lax.ppermute(a, ("dp", "seq"), swap_pairs(dp, None))
    tokens, cotangent, w_query, w_key, w_value, w_out, w_in, w_down = (
        pltpu.with_memory_space_constraint(array, pltpu.HBM)
        for array in (tokens, cotangent, w_query, w_key, w_value, w_out, w_in, w_down)
    )
    table = jnp.broadcast_to(position_bias_table[:, :, None], (bucket_count, heads, 1))
    gain, fgain = attend_gain.reshape(1, width), forward_gain.reshape(1, width)
    sds = jax.ShapeDtypeStruct
    vm = pltpu.VMEM
    dma = pltpu.SemaphoreType.DMA
    paired = sds((rows, pairs, length, TILE), BF)
    wide_bf, wide_f32 = sds((rows, length, width), BF), sds((rows, length, width), F32)
    narrow, items = sds((rows, length, TILE), F32), sds((rows, length, TILE), BF)
    square, square_bf = sds((inner, width), F32), sds((inner, width), BF)
    row_half, marked = sds((rows, half, width), BF), sds((2, rows, half), jnp.int32)
    calls = Order()
    call = calls.call

    tok_send, marks_own, marks_send = call(
        pick_kernel, "pick", 1, (who[0], tokens, segments, pad_mask), [smem(), far(), whole(), whole()],
        (row_half, marked, marked), scratch=[dma((rows,))],
    )
    tok_got, marks_got = swap(tok_send), swap(marks_send)
    tok_own, cot_own, cot_send = call(
        pick_rest_kernel, "pick_rest", 1, (who[0], tokens, cotangent), [smem(), far(), far()],
        (row_half, row_half, row_half), scratch=[dma((3 * rows,))],
    )
    cot_got = swap(cot_send)
    e_shape = (rows, pairs, 2, length, length)
    x, normed, q, k, v, e, inv, att, kept, middle, second = call(
        forward_kernel, "attend_forward", 14,
        (
            who[0], row_counts.reshape(rows), tok_own, tok_got, marks_own, marks_got, table, gain, fgain,
            w_query, w_key, w_value, w_out,
        ),
        [smem(), smem()] + [whole()] * 7 + [far()] * 4,
        (
            wide_bf, wide_bf, paired, paired, paired, sds(e_shape, BF),
            sds((rows, pairs, length, TILE), F32), paired, narrow, wide_f32, wide_bf,
        ),
        grid=pairs,
        out_specs=[whole()] * 5 + [pl.BlockSpec((rows, 1, 2, length, length), lambda p: (0, p, 0, 0, 0))] + [whole()] * 5,
        scratch=[vm((rows, length, TILE), BF)] * 2 + [vm((heads, 1, 2 * length), F32)] + [vm((width, inner), BF)] * 4 + [dma((4,))],
        vmem=VMEM[0],
    )

    block = vm((width, width), BF)
    piece_halves = lambda count, more=0: (sds((count * width // 2, width), BF), sds((count * width // 2 + more, width), BF))
    g, fg, acc, sg, down_first, in_first = call(
        functools.partial(feed_first_kernel, steps=splits[0]), "feed_first", 5 * splits[0],
        (who[0], cot_own, cot_got, kept, second, w_in, w_down),
        [smem()] + [whole()] * 4 + [far()] * 2,
        (wide_bf, wide_bf, wide_f32, wide_f32, *[sds((splits[0], width, width), BF)] * 2),
        grid=splits[0],
        scratch=[vm((splits[0], width, width), BF)] * 2 + [dma((splits[0], 2))],
        vmem=VMEM[1],
    )
    acc, sg, down_block, in_block = call(
        functools.partial(feed_second_kernel, splits[0]), "feed_second", 6, (fg, acc, sg, second, w_in, w_down),
        [whole()] * 4 + [far()] * 2,
        (wide_f32, wide_f32, square_bf, square_bf),
        scratch=[block, block, dma((2,))],
        vmem=VMEM[2],
        aliases={1: 0, 2: 1},
    )
    _, _, out_own, out_send, mg, grad_att, gf, keep, send = call(
        functools.partial(feed_third_kernel, splits[0] + 1), "feed_third", 8,
        (who[0], g, fg, acc, sg, kept, middle, second, att, fgain, w_out, w_in, w_down, down_first, in_first, down_block, in_block),
        [smem()] + [whole()] * 9 + [far()] * 3 + [whole()] * 4,
        (
            wide_f32, wide_f32, row_half, row_half, wide_f32, paired, sds((1, width), F32), *piece_halves(2 * blocks + 1),
        ),
        scratch=[vm((length, width), F32), block, block, block, dma((3,))],
        vmem=VMEM[3],
        aliases={3: 0, 4: 1},
    )
    a = Piece(calls, keep, send, None, orders[0], rests[0], dp)

    some = sds((rows, pairs // PARTS, length, TILE), BF)
    dq, dk, dv, diag = [], [], [], []
    for part in range(PARTS):
        base = part * (pairs // PARTS)
        outs = call(
            functools.partial(backward_kernel, base=base), "attend_backward", 12 / PARTS,
            (e, q, k, v, inv, att, grad_att),
            [pl.BlockSpec((rows, 1, 2, length, length), lambda p, base=base: (0, p + base, 0, 0, 0))] + [whole()] * 6,
            (some, some, some, sds((heads // PARTS, 1, 2 * length), F32)),
            grid=pairs // PARTS,
            scratch=[vm((2, TILE, 2 * length), F32)],
            vmem=VMEM[4],
        )
        for kept_list, out in zip((dq, dk, dv, diag), outs):
            kept_list.append(out)
        if part == 0:
            a.land()
    keep, send, small = call(
        functools.partial(weight_kernel, PARTS, bucket_count), "weight_grads", 3,
        (who[1], normed, *dq, *dk, *dv, *diag, gf, w_query, w_key, w_value, gain),
        [smem()] + [whole()] * (2 + 4 * PARTS) + [far()] * 3 + [whole()],
        (*piece_halves(3, SMALL), sds((SMALL, width), BF)),
        scratch=[block, block, block, dma((3,))],
        vmem=VMEM[5],
    )
    c_piece = Piece(calls, keep, send, small, orders[1], rests[1], dp)
    a.land()
    in_own, in_send = call(
        functools.partial(input_kernel, PARTS), "input_grad", 4,
        (who[1], x, mg, *dq, *dk, *dv, w_query, w_key, w_value, gain),
        [smem()] + [whole()] * (2 + 3 * PARTS) + [far()] * 3 + [whole()],
        (row_half, row_half),
        scratch=[vm((length, width), F32), block, block, block, dma((3,))],
        vmem=VMEM[6],
    )
    out_got = swap(out_send)
    in_got = swap(in_send)
    while len(c_piece.steps) > 1:
        c_piece.land()
        if len(a.steps) > 1:
            a.land()
    early = call(
        feed_result_kernel, "feed_result", 4, (masks, *a.done()), [smem()] + [whole()] * 2,
        (sds((ff, width), F32), sds((width, ff), F32), square),
        vmem=VMEM[7],
    )
    grad_down, grad_in, grad_out = early
    all_rows = sds((rows, slots, half, width), BF)
    output, grad_input = call(
        place_kernel, "place", 1, (who[0], out_own, out_got, in_own, in_got), [smem()] + [whole()] * 4,
        (all_rows, all_rows), out_specs=[far(), far()], scratch=[dma((4 * rows,))],
    )
    grad_query, grad_key, grad_value, ga, gf, grad_table = call(
        rest_result_kernel, "rest_result", 3,
        (masks, *c_piece.done()), [smem()] + [whole()] * 2,
        (square, square, square, sds((1, width), F32), sds((1, width), F32), sds((bucket_count, heads), F32)),
        vmem=VMEM[7],
    )

    return (
        output,
        grad_input,
        ga.reshape(width),
        grad_query,
        grad_key,
        grad_value,
        grad_out,
        gf.reshape(width),
        grad_in,
        grad_down,
        grad_table,
    )


def solution(mesh):
    placed = (P(None, "dp", "seq", None),) * 2 + (P(None, "dp", "seq"),) * 2 + (P(None, "dp"),) + (P(),) * 9
    return jax.shard_map(
        on_device,
        mesh=mesh,
        in_specs=placed,
        out_specs=(P(None, "dp", "seq", None),) * 2 + (P(),) * 9,
        check_vma=False,
    )
```

```python
import functools
import math

import jax
import jax.numpy as jnp
from jax import lax
from jax.experimental import pallas as pl
from jax.experimental.pallas import tpu as pltpu
from jax.sharding import PartitionSpec as P

EPSILON = 1e-06
MASKED = -1000000000.0
LIMITS = (12, 16, 23, 32, 46, 64, 91)
BF = jnp.bfloat16
F32 = jnp.float32
TILE = 128
LEVELS = 4
SPLIT = 2
SMALL = 32
PARTS = 2
FREE = ("pick_rest", "attend_forward", "feed_first", "feed_third")
ORDERS = ([(0, 2), (1, 0), (2, 1)], [(1, 0), (2, 1), (0, 2)])
VMEM = (16, 15, 12, 14, 12, 10, 10, 14)


def whole():
    return pl.BlockSpec(memory_space=pltpu.VMEM)


def hbm():
    return pl.BlockSpec(memory_space=pl.ANY)


def far():
    return pl.BlockSpec(memory_space=pltpu.HBM)


def smem():
    return pl.BlockSpec(memory_space=pltpu.SMEM)


class Order:
    def __init__(self):
        self.token = None

    def call(self, kernel, name, micros, inputs, in_specs, out_shape, grid=1, out_specs=None, scratch=(), vmem=8, aliases=None, who=None):
        count, results = len(inputs), len(out_shape)
        extra = () if self.token is None or name in FREE else (self.token,)

        skip = count + len(extra)

        def body(*refs):
            token = refs[skip + results]
            token[...] = jnp.zeros_like(token)
            first = () if who is None else (who(),)
            kernel(*first, *refs[:count], *refs[skip : skip + results], *refs[skip + results + 1 :])

        *outs, self.token = pl.pallas_call(
            body,
            grid=(grid,),
            in_specs=list(in_specs) + [whole()] * len(extra),
            out_specs=list(out_specs or [whole() for _ in out_shape]) + [whole()],
            out_shape=(*out_shape, jax.ShapeDtypeStruct((8, TILE), F32)),
            scratch_shapes=list(scratch),
            input_output_aliases=aliases or {},
            compiler_params=pltpu.CompilerParams(vmem_limit_bytes=vmem * 1024 * 1024),
            cost_estimate=pl.CostEstimate(
                flops=int(micros * 1e9), bytes_accessed=int(micros * 1e6), transcendentals=0
            ),
            name=name,
        )(*inputs, *extra)
        return outs


def dot(a, b, contract=((1,), (0,))):
    return lax.dot_general(a, b, (contract, ((), ())), preferred_element_type=F32)


def dot_nt(a, b):
    return dot(a, b, ((1,), (1,)))


def dot_tn(a, b):
    return dot(a, b, ((0,), (0,)))


def bucket_of(relative, half_count):
    distance = jnp.abs(relative)
    far = jnp.full(relative.shape, 8, jnp.int32)
    for bound in LIMITS:
        far = far + (distance >= bound).astype(jnp.int32)
    near_or_far = jnp.where(distance < 8, distance, far)
    return near_or_far + jnp.where(relative > 0, half_count, 0)


def diagonal_buckets(length, half_count):
    lane = lax.broadcasted_iota(jnp.int32, (8, 2 * length), 1)
    relative = lane - (length - TILE)
    relative = jnp.where(lane < 2 * length - TILE, relative, relative - 2 * length)
    return bucket_of(relative, half_count)


def wide(column, width):
    return jnp.concatenate([column] * (width // TILE), axis=1)


def put_block(keep, send, who, block, blocks, value):
    count = value.shape[0] >> LEVELS
    places = 1 << LEVELS
    for core in range(2):

        @pl.when(who[0] == core)
        def _():
            for k in range(places):
                place = jnp.bitwise_xor(k % (places // 2), who[1 + 2 * k // places])
                start = pl.multiple_of((place * blocks + block) * count, count)
                ref = keep if 2 * k // places == core else send
                ref[pl.ds(start, count), :] = value[k * count : (k + 1) * count].astype(ref.dtype)


def half_of(ref, i, half):
    return ref[pl.ds(pl.multiple_of(i * half, half), half), :]


def fill_row(row_ref, own_ref, got_ref, m, c, half):
    row_ref[m, pl.ds(pl.multiple_of(c * half, half), half), :] = own_ref[m]
    row_ref[m, pl.ds(pl.multiple_of((1 - c) * half, half), half), :] = got_ref[m]
    return row_ref[m]


def join(own, got, c):
    return jnp.where(c == 0, jnp.concatenate([own, got], 1), jnp.concatenate([got, own], 1))


def fetches(sources, targets, sems):
    return [pltpu.make_async_copy(a, b, sems.at[i]) for i, (a, b) in enumerate(zip(sources, targets))]


def feed_weights(w_in, w_down, chunk, width):
    start = pl.multiple_of(chunk * width, width)
    return w_in.at[:, pl.ds(start, width)], w_down.at[pl.ds(start, width), :]


def pick_kernel(who, tok, seg, pad, tok_send, marks_own, marks_send, sems):
    c = who[0]
    rows = tok.shape[0]
    copies = [pltpu.make_async_copy(tok.at[m, 1 - c], tok_send.at[m], sems.at[m]) for m in range(rows)]
    for copy in copies:
        copy.start()
    for kind, marks in enumerate((seg, pad)):
        for m in range(rows):
            first, second = marks[m, pl.ds(0, 1)], marks[m, pl.ds(1, 1)]
            marks_own[kind, pl.ds(m, 1)] = jnp.where(c == 0, first, second)
            marks_send[kind, pl.ds(m, 1)] = jnp.where(c == 0, second, first)
    for copy in copies:
        copy.wait()


def pick_rest_kernel(who, tok, cot, tok_own, cot_own, cot_send, sems):
    c = who[0]
    copies = []
    for m in range(tok.shape[0]):
        for source, slot, target in ((tok, c, tok_own), (cot, 1 - c, cot_send), (cot, c, cot_own)):
            copies.append(pltpu.make_async_copy(source.at[m, slot], target.at[m], sems.at[len(copies)]))
    for copy in copies:
        copy.start()
    for copy in copies:
        copy.wait()


def place_kernel(who, *refs):
    c = who[0]
    count = (len(refs) - 1) // 3
    sems = refs[-1]
    copies = []
    for i in range(count):
        own, got, out = refs[2 * i], refs[2 * i + 1], refs[2 * count + i]
        for m in range(own.shape[0]):
            for source, slot in ((own, c), (got, 1 - c)):
                copies.append(pltpu.make_async_copy(source.at[m], out.at[m, slot], sems.at[len(copies)]))
    for copy in copies:
        copy.start()
    for copy in copies:
        copy.wait()


def forward_kernel(
    who, counts, own, got, marks, marks_got, table, gain, fgain, wq_far, wk_far, wv_far, wo_far,
    x_out, normed_out, q_out, k_out, v_out, e_out, inv_out, att_out, kept_out, middle_out, second_out,
    segq, segk, diag, wq, wk, wv, wo, sems,
):
    c = who[0]
    pair = pl.program_id(0)
    rows, half = own.shape[0], own.shape[1]
    length = 2 * half
    pairs = wq.shape[1] // TILE
    bucket_count = table.shape[0]
    copies = fetches((wq_far, wk_far, wv_far, wo_far), (wq, wk, wv, wo), sems)

    @pl.when(pair == 0)
    def _():
        for copy in copies:
            copy.start()
        buckets = diagonal_buckets(length, bucket_count // 2)
        strip = jnp.zeros(buckets.shape, F32)
        for b in range(bucket_count):
            strip = jnp.where(buckets == b, table[b], strip)
        for h in range(strip.shape[0]):
            diag[h] = strip[h : h + 1]
        for m in range(rows):
            x = fill_row(x_out, own, got, m, c, half).astype(F32)
            r = lax.rsqrt(jnp.mean(x * x, -1, keepdims=True) + EPSILON)
            normed = (x * r * gain[...]).astype(BF)
            normed_out[m] = normed
            if m == 0:
                for copy in copies:
                    copy.wait()
            for w, out in ((wq, q_out), (wk, k_out), (wv, v_out)):
                projected = dot(normed, w[...]).astype(BF)
                for p in range(pairs):
                    out[m, p] = projected[:, p * TILE : (p + 1) * TILE]
            seg = join(marks[0, pl.ds(m, 1)], marks_got[0, pl.ds(m, 1)], c)
            pad = join(marks[1, pl.ds(m, 1)], marks_got[1, pl.ds(m, 1)], c)
            kept = (pad > 0) & (counts[m] > c)
            item = lax.broadcasted_iota(jnp.int32, (TILE, length), 0)
            same = item == seg
            segq[m] = jnp.where(same, 1.0, 0.0).T.astype(BF)
            segk[m] = jnp.where(same & kept, 0.0, MASKED).T.astype(BF)
            kept_out[m] = jnp.broadcast_to(jnp.where(kept, 1.0, 0.0), (TILE, length)).T

    lane = lax.broadcasted_iota(jnp.int32, (length, TILE), 1)
    for head in range(2):
        mine = (lane < TILE // 2) if head == 0 else (lane >= TILE // 2)
        line = jnp.broadcast_to(diag[2 * pair + head], (TILE, 2 * length))
        strip = pltpu.roll(line, 0, 1, stride=1, stride_axis=0)
        bias = jnp.concatenate(
            [strip[:, length - (i + 1) * TILE : 2 * length - (i + 1) * TILE] for i in range(length // TILE)], 0
        )
        for m in range(rows):
            query = jnp.concatenate([q_out[m, pair], segq[m]], 1)
            key = jnp.concatenate([jnp.where(mine, k_out[m, pair], 0), segk[m]], 1)
            value = jnp.concatenate([jnp.where(mine, v_out[m, pair], 0), jnp.where(mine, 1.0, 0.0).astype(BF)], 1)
            scores = dot_nt(query, key) + bias
            e = jnp.exp(scores - jnp.max(scores, -1, keepdims=True)).astype(BF)
            e_out[m, 0, head] = e
            weighed = dot(e, value)
            if head == 0:
                att_acc = weighed
                inv_out[m, pair] = att_acc[:, TILE:]
                half_att = att_acc[:, :TILE]
                middle_out[m, :, :TILE] = half_att
            else:
                inv = 1.0 / (inv_out[m, pair] + weighed[:, TILE:])
                inv_out[m, pair] = inv
                att_out[m, pair] = ((middle_out[m, :, :TILE] + weighed[:, :TILE]) * inv).astype(BF)

    @pl.when(pair == pairs - 1)
    def _():
        for m in range(rows):
            attended = jnp.concatenate([att_out[m, p] for p in range(pairs)], 1)
            branch = dot(attended, wo[...])
            middle = x_out[m].astype(F32) + wide(kept_out[m], branch.shape[1]) * branch
            middle_out[m] = middle
            r = lax.rsqrt(jnp.mean(middle * middle, -1, keepdims=True) + EPSILON)
            second_out[m] = (middle * r * fgain[...]).astype(BF)


def gelu_parts(u):
    z = jnp.abs(u) * (0.5**0.5)
    t = 1.0 / (1.0 + 0.3275911 * z)
    bell = jnp.exp(u * u * -0.5)
    poly = ((((1.061405429 * t - 1.453152027) * t + 1.421413741) * t - 0.284496736) * t + 0.254829592) * t
    tail = 0.5 * poly * bell
    upper = jnp.where(u >= 0, 1.0 - tail, tail)
    return upper, u * bell * ((2.0 * math.pi) ** -0.5)


def feed_chunk(second, fg, w_in, w_down, acc, sg):
    down = into = None
    for m in range(second.shape[0]):
        u = dot(second[m], w_in[...])
        upper, slope = gelu_parts(u)
        active = (u * upper).astype(BF)
        acc[m] += dot(active, w_down[...])
        up = (dot_nt(fg[m], w_down[...]) * (upper + slope)).astype(BF)
        sg[m] += dot_nt(up, w_in[...])
        down_now, into_now = dot_tn(active, fg[m]), dot_tn(second[m], up)
        down = down_now if m == 0 else down + down_now
        into = into_now if m == 0 else into + into_now
    return down, into


def tall(ref):
    return jnp.concatenate([ref[m] for m in range(ref.shape[0])], 0)


def feed_first_kernel(
    who, own, got, kept, second, w_in_far, w_down_far,
    g_out, fg_out, acc_out, sg_out, keep, send,
    w_ins, w_downs, sems,
    *, steps,
):
    step = pl.program_id(0)
    rows, half, width = own.shape
    copies = [
        fetches(feed_weights(w_in_far, w_down_far, i, width), (w_ins.at[i], w_downs.at[i]), sems.at[i])
        for i in range(steps)
    ]

    @pl.when(step == 0)
    def _():
        for copy in sum(copies, []):
            copy.start()
        for m in range(rows):
            g = fill_row(g_out, own, got, m, who[0], half)
            fg_out[m] = (g.astype(F32) * wide(kept[m], g.shape[1])).astype(BF)
        acc_out[...] = jnp.zeros_like(acc_out)
        sg_out[...] = jnp.zeros_like(sg_out)

    for i in range(steps):

        @pl.when(step == i)
        def _():
            for copy in copies[i]:
                copy.wait()

    down, into = feed_chunk(second, fg_out, w_ins.at[step], w_downs.at[step], acc_out, sg_out)
    put_block(keep, send, who, step, 2 * steps, down)
    put_block(keep, send, who, steps + step, 2 * steps, into)


def feed_third_kernel(
    chunk, who, g, fg, acc_in, sg_in, kept, middle, second, att, fgain, wo_far, w_in_far, w_down_far,
    acc, sg, keep_out, send_out, mg_out, back_out, gf_out, down_out, in_out, o_out,
    half_rows, w_in, w_down, wo, sems,
):
    c = who[0]
    rows, length, width = g.shape
    half = length // 2
    pairs = width // TILE
    copies = fetches((*feed_weights(w_in_far, w_down_far, chunk, width), wo_far), (w_in, w_down, wo), sems)
    for copy in copies:
        copy.start()
    for copy in copies:
        copy.wait()
    down, into = feed_chunk(second, fg, w_in, w_down, acc, sg)
    down_out[...] = down.astype(BF)
    in_out[...] = into.astype(BF)
    gf = jnp.zeros(gf_out.shape, F32)
    for m in range(rows):
        mid = middle[m]
        held = wide(kept[m], width)
        half_rows[...] = mid + held * acc[m]
        keep_out[m] = half_of(half_rows, c, half).astype(BF)
        send_out[m] = half_of(half_rows, 1 - c, half).astype(BF)
        r = lax.rsqrt(jnp.mean(mid * mid, -1, keepdims=True) + EPSILON)
        later = sg[m]
        across = later * mid
        gf = gf + jnp.sum(across * r, 0, keepdims=True)
        inner = jnp.mean(across * fgain[...], -1, keepdims=True)
        mg = g[m].astype(F32) + r * (later * fgain[...]) - mid * (r * r * r * inner)
        mg_out[m] = mg
        branch = (held * mg).astype(BF)
        back = dot_nt(branch, wo[...]).astype(BF)
        attended = jnp.concatenate([att[m, p] for p in range(pairs)], 1)
        for p in range(pairs):
            back_out[m, p] = back[:, p * TILE : (p + 1) * TILE]
        out_now = dot_tn(attended, branch)
        go = out_now if m == 0 else go + out_now
    gf_out[...] = gf
    o_out[...] = go.astype(BF)


def backward_kernel(
    e_in, q, k, v, inv, att, grad_att,
    dq_out, dk_out, dv_out, diag_out,
    strip,
    *, base,
):
    step = pl.program_id(0)
    pair = step + base
    rows, length = q.shape[0], q.shape[2]
    lane = lax.broadcasted_iota(jnp.int32, (length, TILE), 1)
    low = lane < TILE // 2
    strip[...] = jnp.zeros_like(strip)
    for m in range(rows):
        got = grad_att[m, pair].astype(F32)
        inverse = inv[m, pair]
        scaled = (got * inverse).astype(BF)
        weighed = got * inverse * att[m, pair].astype(F32)
        extra = jnp.zeros((length, TILE), F32)
        for head in range(2):
            mine = low if head == 0 else jnp.logical_not(low)
            centre = -jnp.sum(jnp.where(mine, weighed, 0.0), -1, keepdims=True)
            rough = centre.astype(BF).astype(F32)
            extra = jnp.where(lane == 2 * head, rough, extra)
            extra = jnp.where(lane == 2 * head + 1, centre - rough, extra)
        left = jnp.concatenate([scaled, extra.astype(BF)], 1)
        dq = dk = dv = None
        for head in range(2):
            mine = low if head == 0 else jnp.logical_not(low)
            ones = jnp.where((lane == 2 * head) | (lane == 2 * head + 1), 1.0, 0.0).astype(BF)
            right = jnp.concatenate([jnp.where(mine, v[m, pair], 0), ones], 1)
            e = e_in[m, 0, head]
            ds = e.astype(F32) * dot_nt(left, right)
            for i in range(length // TILE):
                start = length - (i + 1) * TILE
                strip[head, :, start : start + length] += ds[i * TILE : (i + 1) * TILE]
            ds = ds.astype(BF)
            dq_now = dot(ds, jnp.where(mine, k[m, pair], 0))
            dk_now = dot_tn(ds, jnp.where(mine, q[m, pair], 0))
            dv_now = dot_tn(e, jnp.where(mine, scaled, 0))
            dq = dq_now if dq is None else dq + dq_now
            dk = dk_now if dk is None else dk + dk_now
            dv = dv_now if dv is None else dv + dv_now
        dq_out[m, step] = dq.astype(BF)
        dk_out[m, step] = dk.astype(BF)
        dv_out[m, step] = dv.astype(BF)
    lanes = strip.shape[2]
    for head in range(2):
        total = strip[head]
        count = TILE
        while count > 1:
            count //= 2
            total = total[:count] + pltpu.roll(total[count:], lanes - count, 1)
        diag_out[2 * step + head] = total


def joined(grads, m):
    return jnp.concatenate([grad[m, p] for grad in grads for p in range(grad.shape[1])], 1)


def weight_kernel(parts, bucket_count, *refs):
    who, normed = refs[:2]
    dq, dk, dv, diags = (refs[2 + i * parts : 2 + (i + 1) * parts] for i in range(4))
    gf, *blocks = refs[2 + 4 * parts : 6 + 4 * parts]
    wq_far, wk_far, wv_far, gain, keep, send, small_out, wq, wk, wv, sems = refs[6 + 4 * parts :]
    rows, length, width = normed.shape
    copies = fetches((wq_far, wk_far, wv_far), (wq, wk, wv), sems)
    for copy in copies:
        copy.start()
    n = tall(normed)
    summed = jnp.zeros((width, 1), F32)
    for place, (grads, weight) in enumerate(((dq, wq), (dk, wk), (dv, wv))):
        value = dot_tn(n, jnp.concatenate([joined(grads, m) for m in range(rows)], 0))
        copies[place].wait()
        summed = summed + jnp.sum(value * weight[...].astype(F32), -1, keepdims=True)
        put_block(keep, send, who, 3 + place, 6, value)
    for place, ready in enumerate(blocks):
        put_block(keep, send, who, place, 6, ready[...])
    ga = jnp.broadcast_to(summed, (width, TILE)).T[:1] / gain[...]
    lines = jnp.concatenate([diag[h] for diag in diags for h in range(diag.shape[0])], 0)
    buckets = diagonal_buckets(length, bucket_count // 2)
    lane = lax.broadcasted_iota(jnp.int32, (8, width), 1)
    table = jnp.zeros((8, width), F32)
    for b in range(bucket_count):
        total = jnp.sum(jnp.where(buckets == b, lines, 0.0), -1, keepdims=True)
        table = jnp.where(lane == b, total, table)
    small = jnp.concatenate([ga, gf[...], jnp.zeros((6, width), F32), table], 0)
    rough = small.astype(BF)
    small = jnp.concatenate([rough, (small - rough.astype(F32)).astype(BF)], 0)
    small_out[...] = small
    send[send.shape[0] - small.shape[0] :, :] = small


def input_kernel(parts, *refs):
    who, x, mg = refs[:3]
    dq, dk, dv = (refs[3 + i * parts : 3 + (i + 1) * parts] for i in range(3))
    wq_far, wk_far, wv_far, gain, keep_out, send_out, half_rows, wq, wk, wv, sems = refs[3 + 3 * parts :]
    copies = fetches((wq_far, wk_far, wv_far), (wq, wk, wv), sems)
    for copy in copies:
        copy.start()
    c = who[0]
    rows, length, width = x.shape
    half = length // 2
    for m in range(rows):
        back = None
        for i, (grads, weight) in enumerate(((dq, wq), (dk, wk), (dv, wv))):
            if m == 0:
                copies[i].wait()
            now = dot_nt(joined(grads, m), weight[...])
            back = now if back is None else back + now
        xm = x[m].astype(F32)
        r = lax.rsqrt(jnp.mean(xm * xm, -1, keepdims=True) + EPSILON)
        grown = back * gain[...]
        inner = jnp.mean(grown * xm, -1, keepdims=True)
        half_rows[...] = mg[m] + r * grown - xm * (r * r * r * inner)
        keep_out[m] = half_of(half_rows, c, half).astype(BF)
        send_out[m] = half_of(half_rows, 1 - c, half).astype(BF)


def fill_block(target, i, blocks, who, own, got):
    places = 1 << LEVELS
    count = target.shape[0] >> LEVELS
    for k in range(places):
        core = 2 * k // places
        place = jnp.bitwise_xor(k % (places // 2), who[1 + core])
        start = pl.multiple_of((place * blocks + i) * count, count)
        mine = who[0] == core
        value = jnp.where(mine, own[pl.ds(start, count), :], got[pl.ds(start, count), :])
        target[k * count : (k + 1) * count, :] = value.astype(F32)


def feed_result_kernel(who, own, got, down_out, in_out, made, sems):
    width = own.shape[1]
    steps = made.shape[0] // 2
    copies = []
    for i in range(2 * steps):
        fill_block(made.at[i], i, 2 * steps, who, own, got)
        part = slice((i % steps) * width, (i % steps + 1) * width)
        target = down_out.at[part, :] if i < steps else in_out.at[:, part]
        copies.append(pltpu.make_async_copy(made.at[i], target, sems.at[i]))
        copies[-1].start()
    for copy in copies:
        copy.wait()


def rest_result_kernel(
    who, own, got, down_in, in_in, down_out, in_out, o_out, q_out, k_out, v_out, ga_out, gf_out, table_out, made, sems
):
    width = own.shape[1]
    last = slice(down_out.shape[0] - width, down_out.shape[0])
    targets = (down_out.at[last, :], in_out.at[:, last], o_out, q_out, k_out, v_out)
    copies = []
    for i, target in enumerate(targets):
        fill_block(made.at[i], i, 6, who, own, got)
        copies.append(pltpu.make_async_copy(made.at[i], target, sems.at[i]))
        copies[-1].start()
    tail = own.shape[0] - SMALL
    small = jnp.where(who[0] == 0, own[tail:, :].astype(F32), got[tail:, :].astype(F32))
    small = small[: SMALL // 2] + small[SMALL // 2 :]
    ga_out[...] = small[:1]
    gf_out[...] = small[1:2]
    table = jnp.concatenate([small[8:, :TILE], jnp.zeros((TILE - 8, TILE), F32)], 0).T
    table_out[...] = table[: table_out.shape[0], : table_out.shape[1]]
    for copy in copies:
        copy.wait()


def land_kernel(has_small, then, *refs):
    kind, after = then
    keep, got = refs[:2]
    refs = refs[2:]
    rows = keep.shape[0]
    if has_small:
        small, refs = refs[0], refs[1:]
    send = refs[0]
    if kind == "gather":
        send[:rows, :] = keep[...]
        send[rows : 2 * rows, :] = got[...]
        if has_small:
            send[2 * rows :, :] = small[...]
        return
    total = (keep[...].astype(F32) + got[:rows, :].astype(F32)).astype(BF)
    if after == "halve":
        refs[1][...] = total[: rows // 2]
        total = total[rows // 2 :]
    send[: total.shape[0], :] = total
    if has_small:
        half = SMALL // 2
        grown = (small[:half, :].astype(F32) + got[rows : rows + half, :].astype(F32)) + (
            small[half:, :].astype(F32) + got[rows + half :, :].astype(F32)
        )
        rough = grown.astype(BF)
        grown = jnp.concatenate([rough, (grown - rough.astype(F32)).astype(BF)], 0)
        refs[-1][...] = grown
        if after != "gather":
            send[total.shape[0] :, :] = grown
            if after != "halve":
                refs[1][...] = total


def swap_pairs(dp, bits):
    if bits is None:
        return [(i, i ^ 1) for i in range(2 * dp)]
    return [(i, i ^ (2 << bits[i % 2])) for i in range(2 * dp)]


class Piece:
    def __init__(self, calls, keep, send, small, order, rest, dp):
        self.calls, self.keep, self.send, self.small, self.dp = calls, keep, send, small, dp
        steps = [("halve", None)] + [("halve", bits) for bits in order]
        steps += [("exchange", (bit, bit)) for bit in rest]
        self.steps = steps + [("gather", bits) for bits in order[::-1]] + [("finish", None)]
        self.got = None
        self.fly()

    def fly(self):
        self.got = lax.ppermute(self.send, ("dp", "seq"), swap_pairs(self.dp, self.steps[0][1]))

    def land(self):
        kind, _ = self.steps.pop(0)
        after = self.steps[0][0]
        rows, width = self.keep.shape
        small = self.small is not None and (kind != "gather" or after == "finish")
        more = SMALL if small and after != "gather" else 0
        sds = lambda count: jax.ShapeDtypeStruct((count, width), BF)
        if kind == "gather":
            outs = [sds(2 * rows + more)]
        elif after == "halve":
            outs = [sds(rows // 2 + more), sds(rows // 2)]
        else:
            outs = [sds(rows + more)] + [sds(rows)] * (more > 0)
        if small and kind != "gather":
            outs.append(sds(SMALL))
        inputs = [self.keep, self.got] + [self.small] * small
        outs = self.calls.call(
            functools.partial(land_kernel, small, (kind, after)), "land", 0.5, inputs, [whole()] * len(inputs), outs
        )
        self.send = outs[0]
        if small and kind != "gather":
            self.small = outs[-1]
        split = kind != "gather" and (after == "halve" or more > 0)
        self.keep = outs[1] if split else outs[0]
        self.fly()
        return self

    def done(self):
        while len(self.steps) > 1:
            self.land()
        return self.send, self.got


def on_device(
    tokens, cotangent, segments, pad_mask, row_counts, attend_gain, w_query, w_key, w_value, w_out,
    forward_gain, w_in, w_down, position_bias_table,
):
    rows, slots, half, width = tokens.shape
    dp, seq = lax.axis_size("dp"), lax.axis_size("seq")
    bits = dp.bit_length() - 1
    assert seq == 2 and slots == 2 and dp == 1 << bits and bits >= 3
    length = seq * half
    inner = w_query.shape[1]
    ff = w_in.shape[1]
    bucket_count, heads = position_bias_table.shape
    pairs = inner // TILE
    assert heads == 2 * pairs == 8 and inner == width
    blocks = ff // width
    assert blocks == SPLIT + 2
    splits = (SPLIT, 2)
    orders = ORDERS
    rests = [[bit for bit in range(bits) if all(bit not in pair for pair in order)] for order in orders]

    def where_am_i(order):
        def who():
            here = lax.axis_index("dp")
            masks = []
            for core in range(2):
                mask = jnp.int32(0)
                for pair in order:
                    mask = 2 * mask + ((here >> pair[core]) & 1)
                masks.append(mask)
            return [lax.axis_index("seq"), *masks]

        return who

    who = [where_am_i(order) for order in orders]
    swap = lambda a: lax.ppermute(a, ("dp", "seq"), swap_pairs(dp, None))
    tokens, cotangent, w_query, w_key, w_value, w_out, w_in, w_down = (
        pltpu.with_memory_space_constraint(array, pltpu.HBM)
        for array in (tokens, cotangent, w_query, w_key, w_value, w_out, w_in, w_down)
    )
    table = jnp.broadcast_to(position_bias_table[:, :, None], (bucket_count, heads, 1))
    gain, fgain = attend_gain.reshape(1, width), forward_gain.reshape(1, width)
    sds = jax.ShapeDtypeStruct
    vm = pltpu.VMEM
    dma = pltpu.SemaphoreType.DMA
    paired = sds((rows, pairs, length, TILE), BF)
    wide_bf, wide_f32 = sds((rows, length, width), BF), sds((rows, length, width), F32)
    narrow, items = sds((rows, length, TILE), F32), sds((rows, length, TILE), BF)
    square, square_bf = sds((inner, width), F32), sds((inner, width), BF)
    row_half, marked = sds((rows, half, width), BF), sds((2, rows, half), jnp.int32)
    calls = Order()
    call = calls.call

    tok_send, marks_own, marks_send = call(
        pick_kernel, "pick", 1, (tokens, segments, pad_mask), [far(), whole(), whole()],
        (row_half, marked, marked), scratch=[dma((rows,))], who=who[0],
    )
    tok_got, marks_got = swap(tok_send), swap(marks_send)
    tok_own, cot_own, cot_send = call(
        pick_rest_kernel, "pick_rest", 1, (tokens, cotangent), [far(), far()],
        (row_half, row_half, row_half), scratch=[dma((3 * rows,))], who=who[0],
    )
    cot_got = swap(cot_send)
    e_shape = (rows, pairs, 2, length, length)
    x, normed, q, k, v, e, inv, att, kept, middle, second = call(
        forward_kernel, "attend_forward", 14,
        (
            row_counts.reshape(rows), tok_own, tok_got, marks_own, marks_got, table, gain, fgain,
            w_query, w_key, w_value, w_out,
        ),
        [smem()] + [whole()] * 7 + [far()] * 4,
        (
            wide_bf, wide_bf, paired, paired, paired, sds(e_shape, BF),
            sds((rows, pairs, length, TILE), F32), paired, narrow, wide_f32, wide_bf,
        ),
        grid=pairs,
        out_specs=[whole()] * 5 + [pl.BlockSpec((rows, 1, 2, length, length), lambda p: (0, p, 0, 0, 0))] + [whole()] * 5,
        scratch=[vm((rows, length, TILE), BF)] * 2 + [vm((heads, 1, 2 * length), F32)] + [vm((width, inner), BF)] * 4 + [dma((4,))],
        vmem=VMEM[0],
        who=who[0],
    )

    block = vm((width, width), BF)
    piece_halves = lambda count, more=0: (sds((count * width // 2, width), BF), sds((count * width // 2 + more, width), BF))
    first = blocks - 1
    g, fg, acc, sg, keep, send = call(
        functools.partial(feed_first_kernel, steps=first), "feed_first", 5 * first,
        (cot_own, cot_got, kept, second, w_in, w_down),
        [whole()] * 4 + [far()] * 2,
        (wide_bf, wide_bf, wide_f32, wide_f32, *piece_halves(2 * first)),
        grid=first,
        scratch=[vm((first, width, width), BF)] * 2 + [dma((first, 2))],
        vmem=VMEM[1],
        who=who[0],
    )
    a = Piece(calls, keep, send, None, orders[0], rests[0], dp)
    _, _, out_own, out_send, mg, grad_att, gf, *ready = call(
        functools.partial(feed_third_kernel, first), "feed_third", 8,
        (g, fg, acc, sg, kept, middle, second, att, fgain, w_out, w_in, w_down),
        [whole()] * 9 + [far()] * 3,
        (
            wide_f32, wide_f32, row_half, row_half, wide_f32, paired, sds((1, width), F32),
            square_bf, square_bf, square_bf,
        ),
        scratch=[vm((length, width), F32), block, block, block, dma((3,))],
        vmem=VMEM[3],
        aliases={2: 0, 3: 1},
        who=who[0],
    )

    some = sds((rows, pairs // PARTS, length, TILE), BF)
    dq, dk, dv, diag = [], [], [], []
    a.land()
    for part in range(PARTS):
        base = part * (pairs // PARTS)
        outs = call(
            functools.partial(backward_kernel, base=base), "attend_backward", 12 / PARTS,
            (e, q, k, v, inv, att, grad_att),
            [pl.BlockSpec((rows, 1, 2, length, length), lambda p, base=base: (0, p + base, 0, 0, 0))] + [whole()] * 6,
            (some, some, some, sds((heads // PARTS, 1, 2 * length), F32)),
            grid=pairs // PARTS,
            scratch=[vm((2, TILE, 2 * length), F32)],
            vmem=VMEM[4],
        )
        for kept_list, out in zip((dq, dk, dv, diag), outs):
            kept_list.append(out)
        if part == 1:
            a.land()
    keep, send, small = call(
        functools.partial(weight_kernel, PARTS, bucket_count), "weight_grads", 3,
        (normed, *dq, *dk, *dv, *diag, gf, *ready, w_query, w_key, w_value, gain),
        [whole()] * (5 + 4 * PARTS) + [far()] * 3 + [whole()],
        (*piece_halves(6, SMALL), sds((SMALL, width), BF)),
        scratch=[block, block, block, dma((3,))],
        vmem=VMEM[5],
        who=who[1],
    )
    c_piece = Piece(calls, keep, send, small, orders[1], rests[1], dp)
    a.land()
    in_own, in_send = call(
        functools.partial(input_kernel, PARTS), "input_grad", 4,
        (x, mg, *dq, *dk, *dv, w_query, w_key, w_value, gain),
        [whole()] * (2 + 3 * PARTS) + [far()] * 3 + [whole()],
        (row_half, row_half),
        scratch=[vm((length, width), F32), block, block, block, dma((3,))],
        vmem=VMEM[6],
        who=who[0],
    )
    out_got = swap(out_send)
    in_got = swap(in_send)
    grad_down = None
    all_rows = sds((rows, slots, half, width), BF)
    while len(c_piece.steps) > 1:
        c_piece.land()
        if len(a.steps) > 1:
            a.land()
        elif grad_down is None:
            grad_down, grad_in = call(
                feed_result_kernel, "feed_result", 4, a.done(), [whole()] * 2,
                (sds((ff, width), F32), sds((width, ff), F32)),
                out_specs=[far(), far()],
                scratch=[vm((2 * first, width, width), F32), dma((2 * first,))],
                vmem=VMEM[7],
                who=who[0],
            )
            output, grad_input = call(
                place_kernel, "place", 1, (out_own, out_got, in_own, in_got), [whole()] * 4,
                (all_rows, all_rows), out_specs=[far(), far()], scratch=[dma((4 * rows,))], who=who[0],
            )
    grad_down, grad_in, grad_out, grad_query, grad_key, grad_value, ga, gf, grad_table = call(
        rest_result_kernel, "rest_result", 3,
        (*c_piece.done(), grad_down, grad_in), [whole()] * 2 + [far()] * 2,
        (
            sds((ff, width), F32), sds((width, ff), F32), square, square, square, square,
            sds((1, width), F32), sds((1, width), F32), sds((bucket_count, heads), F32),
        ),
        out_specs=[far()] * 6 + [whole()] * 3,
        scratch=[vm((6, width, width), F32), dma((6,))],
        vmem=VMEM[7],
        aliases={2: 0, 3: 1},
        who=who[1],
    )

    return (
        output,
        grad_input,
        ga.reshape(width),
        grad_query,
        grad_key,
        grad_value,
        grad_out,
        gf.reshape(width),
        grad_in,
        grad_down,
        grad_table,
    )


def solution(mesh):
    placed = (P(None, "dp", "seq", None),) * 2 + (P(None, "dp", "seq"),) * 2 + (P(None, "dp"),) + (P(),) * 9
    return jax.shard_map(
        on_device,
        mesh=mesh,
        in_specs=placed,
        out_specs=(P(None, "dp", "seq", None),) * 2 + (P(),) * 9,
        check_vma=False,
    )
```

```python
import functools
import math

import jax
import jax.numpy as jnp
from jax import lax
from jax.experimental import pallas as pl
from jax.experimental.pallas import tpu as pltpu
from jax.sharding import PartitionSpec as P

EPSILON = 1e-06
MASKED = -1000000000.0
LIMITS = (12, 16, 23, 32, 46, 64, 91)
BF = jnp.bfloat16
F32 = jnp.float32
TILE = 128
LEVELS = 4
SPLIT = 2
SMALL = 32
COST = 3e9
PARTS = 2
FREE = ("pick_rest", "attend_forward", "feed_first", "feed_third")
ORDERS = ([(0, 1), (1, 0), (2, 2)], [(1, 0), (0, 1), (2, 2)])
VMEM = (16, 15, 12, 14, 12, 10, 10, 14)


def whole():
    return pl.BlockSpec(memory_space=pltpu.VMEM)


def hbm():
    return pl.BlockSpec(memory_space=pl.ANY)


def far():
    return pl.BlockSpec(memory_space=pltpu.HBM)


def smem():
    return pl.BlockSpec(memory_space=pltpu.SMEM)


class Order:
    def __init__(self):
        self.token = None

    def call(self, kernel, name, micros, inputs, in_specs, out_shape, grid=1, out_specs=None, scratch=(), vmem=8, aliases=None, who=None):
        count, results = len(inputs), len(out_shape)
        extra = () if self.token is None or name in FREE else (self.token,)

        skip = count + len(extra)

        def body(*refs):
            token = refs[skip + results]
            token[...] = jnp.zeros_like(token)
            first = () if who is None else (who(),)
            kernel(*first, *refs[:count], *refs[skip : skip + results], *refs[skip + results + 1 :])

        *outs, self.token = pl.pallas_call(
            body,
            grid=(grid,),
            in_specs=list(in_specs) + [whole()] * len(extra),
            out_specs=list(out_specs or [whole() for _ in out_shape]) + [whole()],
            out_shape=(*out_shape, jax.ShapeDtypeStruct((8, TILE), F32)),
            scratch_shapes=list(scratch),
            input_output_aliases=aliases or {},
            compiler_params=pltpu.CompilerParams(vmem_limit_bytes=vmem * 1024 * 1024),
            cost_estimate=pl.CostEstimate(
                flops=int(micros * COST), bytes_accessed=1 << 20, transcendentals=0
            ),
            name=name,
        )(*inputs, *extra)
        return outs


def dot(a, b, contract=((1,), (0,))):
    return lax.dot_general(a, b, (contract, ((), ())), preferred_element_type=F32)


def dot_nt(a, b):
    return dot(a, b, ((1,), (1,)))


def dot_tn(a, b):
    return dot(a, b, ((0,), (0,)))


def bucket_of(relative, half_count):
    distance = jnp.abs(relative)
    far = jnp.full(relative.shape, 8, jnp.int32)
    for bound in LIMITS:
        far = far + (distance >= bound).astype(jnp.int32)
    near_or_far = jnp.where(distance < 8, distance, far)
    return near_or_far + jnp.where(relative > 0, half_count, 0)


def diagonal_buckets(length, half_count):
    lane = lax.broadcasted_iota(jnp.int32, (8, 2 * length), 1)
    relative = lane - (length - TILE)
    relative = jnp.where(lane < 2 * length - TILE, relative, relative - 2 * length)
    return bucket_of(relative, half_count)


def wide(column, width):
    return jnp.concatenate([column] * (width // TILE), axis=1)


def put_block(keep, send, who, block, blocks, value):
    count = value.shape[0] >> LEVELS
    places = 1 << LEVELS
    for core in range(2):

        @pl.when(who[0] == core)
        def _():
            for k in range(places):
                place = jnp.bitwise_xor(k % (places // 2), who[1 + 2 * k // places])
                start = pl.multiple_of((place * blocks + block) * count, count)
                ref = keep if 2 * k // places == core else send
                ref[pl.ds(start, count), :] = value[k * count : (k + 1) * count].astype(ref.dtype)


def half_of(ref, i, half):
    return ref[pl.ds(pl.multiple_of(i * half, half), half), :]


def fill_row(row_ref, own_ref, got_ref, m, c, half):
    row_ref[m, pl.ds(pl.multiple_of(c * half, half), half), :] = own_ref[m]
    row_ref[m, pl.ds(pl.multiple_of((1 - c) * half, half), half), :] = got_ref[m]
    return row_ref[m]


def join(own, got, c):
    return jnp.where(c == 0, jnp.concatenate([own, got], 1), jnp.concatenate([got, own], 1))


def fetches(sources, targets, sems):
    return [pltpu.make_async_copy(a, b, sems.at[i]) for i, (a, b) in enumerate(zip(sources, targets))]


def feed_weights(w_in, w_down, chunk, width):
    start = pl.multiple_of(chunk * width, width)
    return w_in.at[:, pl.ds(start, width)], w_down.at[pl.ds(start, width), :]


def pick_kernel(who, tok, seg, pad, tok_send, marks_own, marks_send, sems):
    c = who[0]
    rows = tok.shape[0]
    copies = [pltpu.make_async_copy(tok.at[m, 1 - c], tok_send.at[m], sems.at[m]) for m in range(rows)]
    for copy in copies:
        copy.start()
    for kind, marks in enumerate((seg, pad)):
        for m in range(rows):
            first, second = marks[m, pl.ds(0, 1)], marks[m, pl.ds(1, 1)]
            marks_own[kind, pl.ds(m, 1)] = jnp.where(c == 0, first, second)
            marks_send[kind, pl.ds(m, 1)] = jnp.where(c == 0, second, first)
    for copy in copies:
        copy.wait()


def pick_rest_kernel(who, tok, cot, tok_own, cot_own, cot_send, sems):
    c = who[0]
    copies = []
    for m in range(tok.shape[0]):
        for source, slot, target in ((tok, c, tok_own), (cot, 1 - c, cot_send), (cot, c, cot_own)):
            copies.append(pltpu.make_async_copy(source.at[m, slot], target.at[m], sems.at[len(copies)]))
    for copy in copies:
        copy.start()
    for copy in copies:
        copy.wait()


def place_kernel(who, *refs):
    c = who[0]
    count = (len(refs) - 1) // 3
    sems = refs[-1]
    copies = []
    for i in range(count):
        own, got, out = refs[2 * i], refs[2 * i + 1], refs[2 * count + i]
        for m in range(own.shape[0]):
            for source, slot in ((own, c), (got, 1 - c)):
                copies.append(pltpu.make_async_copy(source.at[m], out.at[m, slot], sems.at[len(copies)]))
    for copy in copies:
        copy.start()
    for copy in copies:
        copy.wait()


def forward_kernel(
    who, counts, own, got, marks, marks_got, table, gain, fgain, wq_far, wk_far, wv_far, wo_far,
    x_out, normed_out, q_out, k_out, v_out, e_out, inv_out, att_out, kept_out, middle_out, second_out,
    segq, segk, diag, wq, wk, wv, wo, sems,
):
    c = who[0]
    pair = pl.program_id(0)
    rows, half = own.shape[0], own.shape[1]
    length = 2 * half
    pairs = wq.shape[1] // TILE
    bucket_count = table.shape[0]
    copies = fetches((wq_far, wk_far, wv_far, wo_far), (wq, wk, wv, wo), sems)

    @pl.when(pair == 0)
    def _():
        for copy in copies:
            copy.start()
        buckets = diagonal_buckets(length, bucket_count // 2)
        strip = jnp.zeros(buckets.shape, F32)
        for b in range(bucket_count):
            strip = jnp.where(buckets == b, table[b], strip)
        for h in range(strip.shape[0]):
            diag[h] = strip[h : h + 1]
        for m in range(rows):
            x = fill_row(x_out, own, got, m, c, half).astype(F32)
            r = lax.rsqrt(jnp.mean(x * x, -1, keepdims=True) + EPSILON)
            normed = (x * r * gain[...]).astype(BF)
            normed_out[m] = normed
            if m == 0:
                for copy in copies:
                    copy.wait()
            for w, out in ((wq, q_out), (wk, k_out), (wv, v_out)):
                projected = dot(normed, w[...]).astype(BF)
                for p in range(pairs):
                    out[m, p] = projected[:, p * TILE : (p + 1) * TILE]
            seg = join(marks[0, pl.ds(m, 1)], marks_got[0, pl.ds(m, 1)], c)
            pad = join(marks[1, pl.ds(m, 1)], marks_got[1, pl.ds(m, 1)], c)
            kept = (pad > 0) & (counts[m] > c)
            item = lax.broadcasted_iota(jnp.int32, (TILE, length), 0)
            same = item == seg
            segq[m] = jnp.where(same, 1.0, 0.0).T.astype(BF)
            segk[m] = jnp.where(same & kept, 0.0, MASKED).T.astype(BF)
            kept_out[m] = jnp.broadcast_to(jnp.where(kept, 1.0, 0.0), (TILE, length)).T

    lane = lax.broadcasted_iota(jnp.int32, (length, TILE), 1)
    for head in range(2):
        mine = (lane < TILE // 2) if head == 0 else (lane >= TILE // 2)
        line = jnp.broadcast_to(diag[2 * pair + head], (TILE, 2 * length))
        strip = pltpu.roll(line, 0, 1, stride=1, stride_axis=0)
        bias = jnp.concatenate(
            [strip[:, length - (i + 1) * TILE : 2 * length - (i + 1) * TILE] for i in range(length // TILE)], 0
        )
        for m in range(rows):
            query = jnp.concatenate([q_out[m, pair], segq[m]], 1)
            key = jnp.concatenate([jnp.where(mine, k_out[m, pair], 0), segk[m]], 1)
            value = jnp.concatenate([jnp.where(mine, v_out[m, pair], 0), jnp.where(mine, 1.0, 0.0).astype(BF)], 1)
            scores = dot_nt(query, key) + bias
            e = jnp.exp(scores - jnp.max(scores, -1, keepdims=True)).astype(BF)
            e_out[m, 0, head] = e
            weighed = dot(e, value)
            if head == 0:
                att_acc = weighed
                inv_out[m, pair] = att_acc[:, TILE:]
                half_att = att_acc[:, :TILE]
                middle_out[m, :, :TILE] = half_att
            else:
                inv = 1.0 / (inv_out[m, pair] + weighed[:, TILE:])
                inv_out[m, pair] = inv
                att_out[m, pair] = ((middle_out[m, :, :TILE] + weighed[:, :TILE]) * inv).astype(BF)

    @pl.when(pair == pairs - 1)
    def _():
        for m in range(rows):
            attended = jnp.concatenate([att_out[m, p] for p in range(pairs)], 1)
            branch = dot(attended, wo[...])
            middle = x_out[m].astype(F32) + wide(kept_out[m], branch.shape[1]) * branch
            middle_out[m] = middle
            r = lax.rsqrt(jnp.mean(middle * middle, -1, keepdims=True) + EPSILON)
            second_out[m] = (middle * r * fgain[...]).astype(BF)


def gelu_parts(u):
    z = jnp.abs(u) * (0.5**0.5)
    t = 1.0 / (1.0 + 0.3275911 * z)
    bell = jnp.exp(u * u * -0.5)
    poly = ((((1.061405429 * t - 1.453152027) * t + 1.421413741) * t - 0.284496736) * t + 0.254829592) * t
    tail = 0.5 * poly * bell
    upper = jnp.where(u >= 0, 1.0 - tail, tail)
    return upper, u * bell * ((2.0 * math.pi) ** -0.5)


def feed_chunk(second, fg, w_in, w_down, acc, sg):
    down = into = None
    for m in range(second.shape[0]):
        u = dot(second[m], w_in[...])
        upper, slope = gelu_parts(u)
        active = (u * upper).astype(BF)
        acc[m] += dot(active, w_down[...])
        up = (dot_nt(fg[m], w_down[...]) * (upper + slope)).astype(BF)
        sg[m] += dot_nt(up, w_in[...])
        down_now, into_now = dot_tn(active, fg[m]), dot_tn(second[m], up)
        down = down_now if m == 0 else down + down_now
        into = into_now if m == 0 else into + into_now
    return down, into


def tall(ref):
    return jnp.concatenate([ref[m] for m in range(ref.shape[0])], 0)


def feed_first_kernel(
    who, own, got, kept, second, w_in_far, w_down_far,
    g_out, fg_out, acc_out, sg_out, keep, send,
    w_ins, w_downs, sems,
    *, steps,
):
    step = pl.program_id(0)
    rows, half, width = own.shape
    copies = [
        fetches(feed_weights(w_in_far, w_down_far, i, width), (w_ins.at[i], w_downs.at[i]), sems.at[i])
        for i in range(steps)
    ]

    @pl.when(step == 0)
    def _():
        for copy in sum(copies, []):
            copy.start()
        for m in range(rows):
            g = fill_row(g_out, own, got, m, who[0], half)
            fg_out[m] = (g.astype(F32) * wide(kept[m], g.shape[1])).astype(BF)
        acc_out[...] = jnp.zeros_like(acc_out)
        sg_out[...] = jnp.zeros_like(sg_out)

    for i in range(steps):

        @pl.when(step == i)
        def _():
            for copy in copies[i]:
                copy.wait()

    down, into = feed_chunk(second, fg_out, w_ins.at[step], w_downs.at[step], acc_out, sg_out)
    put_block(keep, send, who, step, 2 * steps, down)
    put_block(keep, send, who, steps + step, 2 * steps, into)


def feed_third_kernel(
    chunk, who, g, fg, acc_in, sg_in, kept, middle, second, att, fgain, wo_far, w_in_far, w_down_far,
    acc, sg, keep_out, send_out, mg_out, back_out, gf_out, down_out, in_out, o_out,
    half_rows, w_in, w_down, wo, sems,
):
    c = who[0]
    rows, length, width = g.shape
    half = length // 2
    pairs = width // TILE
    copies = fetches((*feed_weights(w_in_far, w_down_far, chunk, width), wo_far), (w_in, w_down, wo), sems)
    for copy in copies:
        copy.start()
    for copy in copies:
        copy.wait()
    down, into = feed_chunk(second, fg, w_in, w_down, acc, sg)
    down_out[...] = down.astype(BF)
    in_out[...] = into.astype(BF)
    gf = jnp.zeros(gf_out.shape, F32)
    for m in range(rows):
        mid = middle[m]
        held = wide(kept[m], width)
        half_rows[...] = mid + held * acc[m]
        keep_out[m] = half_of(half_rows, c, half).astype(BF)
        send_out[m] = half_of(half_rows, 1 - c, half).astype(BF)
        r = lax.rsqrt(jnp.mean(mid * mid, -1, keepdims=True) + EPSILON)
        later = sg[m]
        across = later * mid
        gf = gf + jnp.sum(across * r, 0, keepdims=True)
        inner = jnp.mean(across * fgain[...], -1, keepdims=True)
        mg = g[m].astype(F32) + r * (later * fgain[...]) - mid * (r * r * r * inner)
        mg_out[m] = mg
        branch = (held * mg).astype(BF)
        back = dot_nt(branch, wo[...]).astype(BF)
        attended = jnp.concatenate([att[m, p] for p in range(pairs)], 1)
        for p in range(pairs):
            back_out[m, p] = back[:, p * TILE : (p + 1) * TILE]
        out_now = dot_tn(attended, branch)
        go = out_now if m == 0 else go + out_now
    gf_out[...] = gf
    o_out[...] = go.astype(BF)


def backward_kernel(
    e_in, q, k, v, inv, att, grad_att,
    dq_out, dk_out, dv_out, diag_out,
    strip,
    *, base,
):
    step = pl.program_id(0)
    pair = step + base
    rows, length = q.shape[0], q.shape[2]
    lane = lax.broadcasted_iota(jnp.int32, (length, TILE), 1)
    low = lane < TILE // 2
    strip[...] = jnp.zeros_like(strip)
    for m in range(rows):
        got = grad_att[m, pair].astype(F32)
        inverse = inv[m, pair]
        scaled = (got * inverse).astype(BF)
        weighed = got * inverse * att[m, pair].astype(F32)
        extra = jnp.zeros((length, TILE), F32)
        for head in range(2):
            mine = low if head == 0 else jnp.logical_not(low)
            centre = -jnp.sum(jnp.where(mine, weighed, 0.0), -1, keepdims=True)
            rough = centre.astype(BF).astype(F32)
            extra = jnp.where(lane == 2 * head, rough, extra)
            extra = jnp.where(lane == 2 * head + 1, centre - rough, extra)
        left = jnp.concatenate([scaled, extra.astype(BF)], 1)
        dq = dk = dv = None
        for head in range(2):
            mine = low if head == 0 else jnp.logical_not(low)
            ones = jnp.where((lane == 2 * head) | (lane == 2 * head + 1), 1.0, 0.0).astype(BF)
            right = jnp.concatenate([jnp.where(mine, v[m, pair], 0), ones], 1)
            e = e_in[m, 0, head]
            ds = e.astype(F32) * dot_nt(left, right)
            for i in range(length // TILE):
                start = length - (i + 1) * TILE
                strip[head, :, start : start + length] += ds[i * TILE : (i + 1) * TILE]
            ds = ds.astype(BF)
            dq_now = dot(ds, jnp.where(mine, k[m, pair], 0))
            dk_now = dot_tn(ds, jnp.where(mine, q[m, pair], 0))
            dv_now = dot_tn(e, jnp.where(mine, scaled, 0))
            dq = dq_now if dq is None else dq + dq_now
            dk = dk_now if dk is None else dk + dk_now
            dv = dv_now if dv is None else dv + dv_now
        dq_out[m, step] = dq.astype(BF)
        dk_out[m, step] = dk.astype(BF)
        dv_out[m, step] = dv.astype(BF)
    lanes = strip.shape[2]
    for head in range(2):
        total = strip[head]
        count = TILE
        while count > 1:
            count //= 2
            total = total[:count] + pltpu.roll(total[count:], lanes - count, 1)
        diag_out[2 * step + head] = total


def joined(grads, m):
    return jnp.concatenate([grad[m, p] for grad in grads for p in range(grad.shape[1])], 1)


def weight_kernel(parts, bucket_count, *refs):
    who, normed = refs[:2]
    dq, dk, dv, diags = (refs[2 + i * parts : 2 + (i + 1) * parts] for i in range(4))
    gf, *blocks = refs[2 + 4 * parts : 6 + 4 * parts]
    wq_far, wk_far, wv_far, gain, keep, send, small_out, wq, wk, wv, sems = refs[6 + 4 * parts :]
    rows, length, width = normed.shape
    copies = fetches((wq_far, wk_far, wv_far), (wq, wk, wv), sems)
    for copy in copies:
        copy.start()
    n = tall(normed)
    summed = jnp.zeros((width, 1), F32)
    for place, (grads, weight) in enumerate(((dq, wq), (dk, wk), (dv, wv))):
        value = dot_tn(n, jnp.concatenate([joined(grads, m) for m in range(rows)], 0))
        copies[place].wait()
        summed = summed + jnp.sum(value * weight[...].astype(F32), -1, keepdims=True)
        put_block(keep, send, who, 3 + place, 6, value)
    for place, ready in enumerate(blocks):
        put_block(keep, send, who, place, 6, ready[...])
    ga = jnp.broadcast_to(summed, (width, TILE)).T[:1] / gain[...]
    lines = jnp.concatenate([diag[h] for diag in diags for h in range(diag.shape[0])], 0)
    buckets = diagonal_buckets(length, bucket_count // 2)
    lane = lax.broadcasted_iota(jnp.int32, (8, width), 1)
    table = jnp.zeros((8, width), F32)
    for b in range(bucket_count):
        total = jnp.sum(jnp.where(buckets == b, lines, 0.0), -1, keepdims=True)
        table = jnp.where(lane == b, total, table)
    small = jnp.concatenate([ga, gf[...], jnp.zeros((6, width), F32), table], 0)
    rough = small.astype(BF)
    small = jnp.concatenate([rough, (small - rough.astype(F32)).astype(BF)], 0)
    small_out[...] = small
    send[send.shape[0] - small.shape[0] :, :] = small


def input_kernel(parts, *refs):
    who, x, mg = refs[:3]
    dq, dk, dv = (refs[3 + i * parts : 3 + (i + 1) * parts] for i in range(3))
    wq_far, wk_far, wv_far, gain, keep_out, send_out, half_rows, wq, wk, wv, sems = refs[3 + 3 * parts :]
    copies = fetches((wq_far, wk_far, wv_far), (wq, wk, wv), sems)
    for copy in copies:
        copy.start()
    c = who[0]
    rows, length, width = x.shape
    half = length // 2
    for m in range(rows):
        back = None
        for i, (grads, weight) in enumerate(((dq, wq), (dk, wk), (dv, wv))):
            if m == 0:
                copies[i].wait()
            now = dot_nt(joined(grads, m), weight[...])
            back = now if back is None else back + now
        xm = x[m].astype(F32)
        r = lax.rsqrt(jnp.mean(xm * xm, -1, keepdims=True) + EPSILON)
        grown = back * gain[...]
        inner = jnp.mean(grown * xm, -1, keepdims=True)
        half_rows[...] = mg[m] + r * grown - xm * (r * r * r * inner)
        keep_out[m] = half_of(half_rows, c, half).astype(BF)
        send_out[m] = half_of(half_rows, 1 - c, half).astype(BF)


def fill_block(target, i, blocks, who, own, got):
    places = 1 << LEVELS
    count = target.shape[0] >> LEVELS
    for k in range(places):
        core = 2 * k // places
        place = jnp.bitwise_xor(k % (places // 2), who[1 + core])
        start = pl.multiple_of((place * blocks + i) * count, count)
        mine = who[0] == core
        value = jnp.where(mine, own[pl.ds(start, count), :], got[pl.ds(start, count), :])
        target[k * count : (k + 1) * count, :] = value.astype(F32)


def feed_result_kernel(who, own, got, down_out, in_out, made, sems):
    width = own.shape[1]
    steps = made.shape[0] // 2
    copies = []
    for i in range(2 * steps):
        fill_block(made.at[i], i, 2 * steps, who, own, got)
        part = slice((i % steps) * width, (i % steps + 1) * width)
        target = down_out.at[part, :] if i < steps else in_out.at[:, part]
        copies.append(pltpu.make_async_copy(made.at[i], target, sems.at[i]))
        copies[-1].start()
    for copy in copies:
        copy.wait()


def rest_result_kernel(
    who, own, got, down_in, in_in, down_out, in_out, o_out, q_out, k_out, v_out, ga_out, gf_out, table_out, made, sems
):
    width = own.shape[1]
    last = slice(down_out.shape[0] - width, down_out.shape[0])
    targets = (down_out.at[last, :], in_out.at[:, last], o_out, q_out, k_out, v_out)
    copies = []
    for i, target in enumerate(targets):
        fill_block(made.at[i], i, 6, who, own, got)
        copies.append(pltpu.make_async_copy(made.at[i], target, sems.at[i]))
        copies[-1].start()
    tail = own.shape[0] - SMALL
    small = jnp.where(who[0] == 0, own[tail:, :].astype(F32), got[tail:, :].astype(F32))
    small = small[: SMALL // 2] + small[SMALL // 2 :]
    ga_out[...] = small[:1]
    gf_out[...] = small[1:2]
    table = jnp.concatenate([small[8:, :TILE], jnp.zeros((TILE - 8, TILE), F32)], 0).T
    table_out[...] = table[: table_out.shape[0], : table_out.shape[1]]
    for copy in copies:
        copy.wait()


def land_kernel(has_small, then, *refs):
    kind, after = then
    keep, got = refs[:2]
    refs = refs[2:]
    rows = keep.shape[0]
    if has_small:
        small, refs = refs[0], refs[1:]
    send = refs[0]
    if kind == "gather":
        send[:rows, :] = keep[...]
        send[rows : 2 * rows, :] = got[...]
        if has_small:
            send[2 * rows :, :] = small[...]
        return
    total = (keep[...].astype(F32) + got[:rows, :].astype(F32)).astype(BF)
    if after == "halve":
        refs[1][...] = total[: rows // 2]
        total = total[rows // 2 :]
    send[: total.shape[0], :] = total
    if has_small:
        half = SMALL // 2
        grown = (small[:half, :].astype(F32) + got[rows : rows + half, :].astype(F32)) + (
            small[half:, :].astype(F32) + got[rows + half :, :].astype(F32)
        )
        rough = grown.astype(BF)
        grown = jnp.concatenate([rough, (grown - rough.astype(F32)).astype(BF)], 0)
        refs[-1][...] = grown
        if after != "gather":
            send[total.shape[0] :, :] = grown
            if after != "halve":
                refs[1][...] = total


def swap_pairs(dp, bits):
    if bits is None:
        return [(i, i ^ 1) for i in range(2 * dp)]
    return [(i, i ^ (2 << bits[i % 2])) for i in range(2 * dp)]


class Piece:
    def __init__(self, calls, keep, send, small, order, rest, dp):
        self.calls, self.keep, self.send, self.small, self.dp = calls, keep, send, small, dp
        steps = [("halve", None)] + [("halve", bits) for bits in order]
        steps += [("exchange", (bit, bit)) for bit in rest]
        self.steps = steps + [("gather", bits) for bits in order[::-1]] + [("finish", None)]
        self.got = None
        self.fly()

    def fly(self):
        self.got = lax.ppermute(self.send, ("dp", "seq"), swap_pairs(self.dp, self.steps[0][1]))

    def land(self):
        kind, _ = self.steps.pop(0)
        after = self.steps[0][0]
        rows, width = self.keep.shape
        small = self.small is not None and (kind != "gather" or after == "finish")
        more = SMALL if small and after != "gather" else 0
        sds = lambda count: jax.ShapeDtypeStruct((count, width), BF)
        if kind == "gather":
            outs = [sds(2 * rows + more)]
        elif after == "halve":
            outs = [sds(rows // 2 + more), sds(rows // 2)]
        else:
            outs = [sds(rows + more)] + [sds(rows)] * (more > 0)
        if small and kind != "gather":
            outs.append(sds(SMALL))
        inputs = [self.keep, self.got] + [self.small] * small
        outs = self.calls.call(
            functools.partial(land_kernel, small, (kind, after)), "land", 0.5, inputs, [whole()] * len(inputs), outs
        )
        self.send = outs[0]
        if small and kind != "gather":
            self.small = outs[-1]
        split = kind != "gather" and (after == "halve" or more > 0)
        self.keep = outs[1] if split else outs[0]
        self.fly()
        return self

    def done(self):
        while len(self.steps) > 1:
            self.land()
        return self.send, self.got


def on_device(
    tokens, cotangent, segments, pad_mask, row_counts, attend_gain, w_query, w_key, w_value, w_out,
    forward_gain, w_in, w_down, position_bias_table,
):
    rows, slots, half, width = tokens.shape
    dp, seq = lax.axis_size("dp"), lax.axis_size("seq")
    bits = dp.bit_length() - 1
    assert seq == 2 and slots == 2 and dp == 1 << bits and bits >= 3
    length = seq * half
    inner = w_query.shape[1]
    ff = w_in.shape[1]
    bucket_count, heads = position_bias_table.shape
    pairs = inner // TILE
    assert heads == 2 * pairs == 8 and inner == width
    blocks = ff // width
    assert blocks == SPLIT + 2
    splits = (SPLIT, 2)
    orders = ORDERS
    rests = [[bit for bit in range(bits) if all(bit not in pair for pair in order)] for order in orders]

    def where_am_i(order):
        def who():
            here = lax.axis_index("dp")
            masks = []
            for core in range(2):
                mask = jnp.int32(0)
                for pair in order:
                    mask = 2 * mask + ((here >> pair[core]) & 1)
                masks.append(mask)
            return [lax.axis_index("seq"), *masks]

        return who

    who = [where_am_i(order) for order in orders]
    swap = lambda a: lax.ppermute(a, ("dp", "seq"), swap_pairs(dp, None))
    tokens, cotangent, w_query, w_key, w_value, w_out, w_in, w_down = (
        pltpu.with_memory_space_constraint(array, pltpu.HBM)
        for array in (tokens, cotangent, w_query, w_key, w_value, w_out, w_in, w_down)
    )
    table = jnp.broadcast_to(position_bias_table[:, :, None], (bucket_count, heads, 1))
    gain, fgain = attend_gain.reshape(1, width), forward_gain.reshape(1, width)
    sds = jax.ShapeDtypeStruct
    vm = pltpu.VMEM
    dma = pltpu.SemaphoreType.DMA
    paired = sds((rows, pairs, length, TILE), BF)
    wide_bf, wide_f32 = sds((rows, length, width), BF), sds((rows, length, width), F32)
    narrow, items = sds((rows, length, TILE), F32), sds((rows, length, TILE), BF)
    square, square_bf = sds((inner, width), F32), sds((inner, width), BF)
    row_half, marked = sds((rows, half, width), BF), sds((2, rows, half), jnp.int32)
    calls = Order()
    call = calls.call

    tok_send, marks_own, marks_send = call(
        pick_kernel, "pick", 1, (tokens, segments, pad_mask), [far(), whole(), whole()],
        (row_half, marked, marked), scratch=[dma((rows,))], who=who[0],
    )
    tok_got, marks_got = swap(tok_send), swap(marks_send)
    tok_own, cot_own, cot_send = call(
        pick_rest_kernel, "pick_rest", 1, (tokens, cotangent), [far(), far()],
        (row_half, row_half, row_half), scratch=[dma((3 * rows,))], who=who[0],
    )
    cot_got = swap(cot_send)
    e_shape = (rows, pairs, 2, length, length)
    x, normed, q, k, v, e, inv, att, kept, middle, second = call(
        forward_kernel, "attend_forward", 14,
        (
            row_counts.reshape(rows), tok_own, tok_got, marks_own, marks_got, table, gain, fgain,
            w_query, w_key, w_value, w_out,
        ),
        [smem()] + [whole()] * 7 + [far()] * 4,
        (
            wide_bf, wide_bf, paired, paired, paired, sds(e_shape, BF),
            sds((rows, pairs, length, TILE), F32), paired, narrow, wide_f32, wide_bf,
        ),
        grid=pairs,
        out_specs=[whole()] * 5 + [pl.BlockSpec((rows, 1, 2, length, length), lambda p: (0, p, 0, 0, 0))] + [whole()] * 5,
        scratch=[vm((rows, length, TILE), BF)] * 2 + [vm((heads, 1, 2 * length), F32)] + [vm((width, inner), BF)] * 4 + [dma((4,))],
        vmem=VMEM[0],
        who=who[0],
    )

    block = vm((width, width), BF)
    piece_halves = lambda count, more=0: (sds((count * width // 2, width), BF), sds((count * width // 2 + more, width), BF))
    first = blocks - 1
    g, fg, acc, sg, keep, send = call(
        functools.partial(feed_first_kernel, steps=first), "feed_first", 5 * first,
        (cot_own, cot_got, kept, second, w_in, w_down),
        [whole()] * 4 + [far()] * 2,
        (wide_bf, wide_bf, wide_f32, wide_f32, *piece_halves(2 * first)),
        grid=first,
        scratch=[vm((first, width, width), BF)] * 2 + [dma((first, 2))],
        vmem=VMEM[1],
        who=who[0],
    )
    a = Piece(calls, keep, send, None, orders[0], rests[0], dp)
    _, _, out_own, out_send, mg, grad_att, gf, *ready = call(
        functools.partial(feed_third_kernel, first), "feed_third", 8,
        (g, fg, acc, sg, kept, middle, second, att, fgain, w_out, w_in, w_down),
        [whole()] * 9 + [far()] * 3,
        (
            wide_f32, wide_f32, row_half, row_half, wide_f32, paired, sds((1, width), F32),
            square_bf, square_bf, square_bf,
        ),
        scratch=[vm((length, width), F32), block, block, block, dma((3,))],
        vmem=VMEM[3],
        aliases={2: 0, 3: 1},
        who=who[0],
    )

    some = sds((rows, pairs // PARTS, length, TILE), BF)
    dq, dk, dv, diag = [], [], [], []
    a.land()
    for part in range(PARTS):
        base = part * (pairs // PARTS)
        outs = call(
            functools.partial(backward_kernel, base=base), "attend_backward", 12 / PARTS,
            (e, q, k, v, inv, att, grad_att),
            [pl.BlockSpec((rows, 1, 2, length, length), lambda p, base=base: (0, p + base, 0, 0, 0))] + [whole()] * 6,
            (some, some, some, sds((heads // PARTS, 1, 2 * length), F32)),
            grid=pairs // PARTS,
            scratch=[vm((2, TILE, 2 * length), F32)],
            vmem=VMEM[4],
        )
        for kept_list, out in zip((dq, dk, dv, diag), outs):
            kept_list.append(out)
        a.land()
    keep, send, small = call(
        functools.partial(weight_kernel, PARTS, bucket_count), "weight_grads", 3,
        (normed, *dq, *dk, *dv, *diag, gf, *ready, w_query, w_key, w_value, gain),
        [whole()] * (5 + 4 * PARTS) + [far()] * 3 + [whole()],
        (*piece_halves(6, SMALL), sds((SMALL, width), BF)),
        scratch=[block, block, block, dma((3,))],
        vmem=VMEM[5],
        who=who[1],
    )
    c_piece = Piece(calls, keep, send, small, orders[1], rests[1], dp)
    in_own, in_send = call(
        functools.partial(input_kernel, PARTS), "input_grad", 4,
        (x, mg, *dq, *dk, *dv, w_query, w_key, w_value, gain),
        [whole()] * (2 + 3 * PARTS) + [far()] * 3 + [whole()],
        (row_half, row_half),
        scratch=[vm((length, width), F32), block, block, block, dma((3,))],
        vmem=VMEM[6],
        who=who[0],
    )
    a.land()
    out_got = swap(out_send)
    in_got = swap(in_send)
    grad_down = None
    all_rows = sds((rows, slots, half, width), BF)
    c_piece.land()
    a.land()
    c_piece.land()
    a.land()
    c_piece.land()
    while len(a.steps) > 1 or grad_down is None:
        if len(a.steps) > 1 or len(c_piece.steps) > 1:
            c_piece.land()
        if len(a.steps) > 1:
            a.land()
        else:
            grad_down, grad_in = call(
                feed_result_kernel, "feed_result", 4, a.done(), [whole()] * 2,
                (sds((ff, width), F32), sds((width, ff), F32)),
                out_specs=[far(), far()],
                scratch=[vm((2 * first, width, width), F32), dma((2 * first,))],
                vmem=VMEM[7],
                who=who[0],
            )
            output, grad_input = call(
                place_kernel, "place", 1, (out_own, out_got, in_own, in_got), [whole()] * 4,
                (all_rows, all_rows), out_specs=[far(), far()], scratch=[dma((4 * rows,))], who=who[0],
            )
    grad_down, grad_in, grad_out, grad_query, grad_key, grad_value, ga, gf, grad_table = call(
        rest_result_kernel, "rest_result", 3,
        (*c_piece.done(), grad_down, grad_in), [whole()] * 2 + [far()] * 2,
        (
            sds((ff, width), F32), sds((width, ff), F32), square, square, square, square,
            sds((1, width), F32), sds((1, width), F32), sds((bucket_count, heads), F32),
        ),
        out_specs=[far()] * 6 + [whole()] * 3,
        scratch=[vm((6, width, width), F32), dma((6,))],
        vmem=VMEM[7],
        aliases={2: 0, 3: 1},
        who=who[1],
    )

    return (
        output,
        grad_input,
        ga.reshape(width),
        grad_query,
        grad_key,
        grad_value,
        grad_out,
        gf.reshape(width),
        grad_in,
        grad_down,
        grad_table,
    )


def solution(mesh):
    placed = (P(None, "dp", "seq", None),) * 2 + (P(None, "dp", "seq"),) * 2 + (P(None, "dp"),) + (P(),) * 9
    return jax.shard_map(
        on_device,
        mesh=mesh,
        in_specs=placed,
        out_specs=(P(None, "dp", "seq", None),) * 2 + (P(),) * 9,
        check_vma=False,
    )
```

```python
import functools
import math

import jax
import jax.numpy as jnp
from jax import lax
from jax.experimental import pallas as pl
from jax.experimental.pallas import tpu as pltpu
from jax.sharding import PartitionSpec as P

EPSILON = 1e-06
MASKED = -1000000000.0
LIMITS = (12, 16, 23, 32, 46, 64, 91)
BF = jnp.bfloat16
F32 = jnp.float32
TILE = 128
LEVELS = 4
SPLIT = 2
SMALL = 32
COST = 3e9
PARTS = 2
FREE = ("pick_rest", "attend_forward", "feed_first", "feed_third")
ORDERS = ([(0, 1), (1, 0), (2, 2)], [(1, 0), (0, 1), (2, 2)])
VMEM = (16, 15, 12, 14, 12, 10, 10, 14)


def whole():
    return pl.BlockSpec(memory_space=pltpu.VMEM)


def hbm():
    return pl.BlockSpec(memory_space=pl.ANY)


def far():
    return pl.BlockSpec(memory_space=pltpu.HBM)


def smem():
    return pl.BlockSpec(memory_space=pltpu.SMEM)


class Order:
    def __init__(self):
        self.token = None

    def call(self, kernel, name, micros, inputs, in_specs, out_shape, grid=1, out_specs=None, scratch=(), vmem=8, aliases=None, who=None):
        count, results = len(inputs), len(out_shape)
        extra = () if self.token is None or name in FREE else (self.token,)

        skip = count + len(extra)

        def body(*refs):
            token = refs[skip + results]
            token[...] = jnp.zeros_like(token)
            first = () if who is None else (who(),)
            kernel(*first, *refs[:count], *refs[skip : skip + results], *refs[skip + results + 1 :])

        *outs, self.token = pl.pallas_call(
            body,
            grid=(grid,),
            in_specs=list(in_specs) + [whole()] * len(extra),
            out_specs=list(out_specs or [whole() for _ in out_shape]) + [whole()],
            out_shape=(*out_shape, jax.ShapeDtypeStruct((8, TILE), F32)),
            scratch_shapes=list(scratch),
            input_output_aliases=aliases or {},
            compiler_params=pltpu.CompilerParams(vmem_limit_bytes=vmem * 1024 * 1024),
            cost_estimate=pl.CostEstimate(
                flops=int(micros * COST), bytes_accessed=1 << 20, transcendentals=0
            ),
            name=name,
        )(*inputs, *extra)
        return outs


def dot(a, b, contract=((1,), (0,))):
    return lax.dot_general(a, b, (contract, ((), ())), preferred_element_type=F32)


def dot_nt(a, b):
    return dot(a, b, ((1,), (1,)))


def dot_tn(a, b):
    return dot(a, b, ((0,), (0,)))


def bucket_of(relative, half_count):
    distance = jnp.abs(relative)
    far = jnp.full(relative.shape, 8, jnp.int32)
    for bound in LIMITS:
        far = far + (distance >= bound).astype(jnp.int32)
    near_or_far = jnp.where(distance < 8, distance, far)
    return near_or_far + jnp.where(relative > 0, half_count, 0)


def diagonal_buckets(length, half_count):
    lane = lax.broadcasted_iota(jnp.int32, (8, 2 * length), 1)
    relative = lane - (length - TILE)
    relative = jnp.where(lane < 2 * length - TILE, relative, relative - 2 * length)
    return bucket_of(relative, half_count)


def wide(column, width):
    return jnp.concatenate([column] * (width // TILE), axis=1)


def put_block(keep, send, who, block, blocks, value):
    count = value.shape[0] >> LEVELS
    places = 1 << LEVELS
    for core in range(2):

        @pl.when(who[0] == core)
        def _():
            for k in range(places):
                place = jnp.bitwise_xor(k % (places // 2), who[1 + 2 * k // places])
                start = pl.multiple_of((place * blocks + block) * count, count)
                ref = keep if 2 * k // places == core else send
                ref[pl.ds(start, count), :] = value[k * count : (k + 1) * count].astype(ref.dtype)


def half_of(ref, i, half):
    return ref[pl.ds(pl.multiple_of(i * half, half), half), :]


def fill_row(row_ref, own_ref, got_ref, m, c, half):
    row_ref[m, pl.ds(pl.multiple_of(c * half, half), half), :] = own_ref[m]
    row_ref[m, pl.ds(pl.multiple_of((1 - c) * half, half), half), :] = got_ref[m]
    return row_ref[m]


def join(own, got, c):
    return jnp.where(c == 0, jnp.concatenate([own, got], 1), jnp.concatenate([got, own], 1))


def fetches(sources, targets, sems):
    return [pltpu.make_async_copy(a, b, sems.at[i]) for i, (a, b) in enumerate(zip(sources, targets))]


def feed_weights(w_in, w_down, chunk, width):
    start = pl.multiple_of(chunk * width, width)
    return w_in.at[:, pl.ds(start, width)], w_down.at[pl.ds(start, width), :]


def pick_kernel(who, tok, seg, pad, tok_send, marks_own, marks_send, near, sems):
    c = who[0]
    rows = tok.shape[0]
    copies = [pltpu.make_async_copy(tok.at[m, 1 - c], tok_send.at[m], sems.at[m]) for m in range(rows)]
    marked = [pltpu.make_async_copy(marks, near.at[i], sems.at[rows + i]) for i, marks in enumerate((seg, pad))]
    for copy in copies + marked:
        copy.start()
    for copy in marked:
        copy.wait()
    for kind in range(2):
        for m in range(rows):
            first, second = near[kind, m, pl.ds(0, 1)], near[kind, m, pl.ds(1, 1)]
            marks_own[kind, pl.ds(m, 1)] = jnp.where(c == 0, first, second)
            marks_send[kind, pl.ds(m, 1)] = jnp.where(c == 0, second, first)
    for copy in copies:
        copy.wait()


def pick_rest_kernel(who, tok, cot, tok_own, cot_own, cot_send, sems):
    c = who[0]
    copies = []
    for m in range(tok.shape[0]):
        for source, slot, target in ((tok, c, tok_own), (cot, 1 - c, cot_send), (cot, c, cot_own)):
            copies.append(pltpu.make_async_copy(source.at[m, slot], target.at[m], sems.at[len(copies)]))
    for copy in copies:
        copy.start()
    for copy in copies:
        copy.wait()


def place_kernel(who, *refs):
    c = who[0]
    count = (len(refs) - 1) // 3
    sems = refs[-1]
    copies = []
    for i in range(count):
        own, got, out = refs[2 * i], refs[2 * i + 1], refs[2 * count + i]
        for m in range(own.shape[0]):
            for source, slot in ((own, c), (got, 1 - c)):
                copies.append(pltpu.make_async_copy(source.at[m], out.at[m, slot], sems.at[len(copies)]))
    for copy in copies:
        copy.start()
    for copy in copies:
        copy.wait()


def forward_kernel(
    who, counts, own, got, marks, marks_got, table, gain, fgain, wq_far, wk_far, wv_far, wo_far,
    x_out, normed_out, q_out, k_out, v_out, e_out, inv_out, att_out, kept_out, middle_out, second_out,
    segq, segk, diag, wq, wk, wv, wo, sems,
):
    c = who[0]
    pair = pl.program_id(0)
    rows, half = own.shape[0], own.shape[1]
    length = 2 * half
    pairs = wq.shape[1] // TILE
    bucket_count = table.shape[0]
    copies = fetches((wq_far, wk_far, wv_far, wo_far), (wq, wk, wv, wo), sems)

    @pl.when(pair == 0)
    def _():
        for copy in copies:
            copy.start()
        buckets = diagonal_buckets(length, bucket_count // 2)
        strip = jnp.zeros(buckets.shape, F32)
        for b in range(bucket_count):
            strip = jnp.where(buckets == b, table[b], strip)
        for h in range(strip.shape[0]):
            diag[h] = strip[h : h + 1]
        for m in range(rows):
            x = fill_row(x_out, own, got, m, c, half).astype(F32)
            r = lax.rsqrt(jnp.mean(x * x, -1, keepdims=True) + EPSILON)
            normed = (x * r * gain[...]).astype(BF)
            normed_out[m] = normed
            if m == 0:
                for copy in copies:
                    copy.wait()
            for w, out in ((wq, q_out), (wk, k_out), (wv, v_out)):
                projected = dot(normed, w[...]).astype(BF)
                for p in range(pairs):
                    out[m, p] = projected[:, p * TILE : (p + 1) * TILE]
            seg = join(marks[0, pl.ds(m, 1)], marks_got[0, pl.ds(m, 1)], c)
            pad = join(marks[1, pl.ds(m, 1)], marks_got[1, pl.ds(m, 1)], c)
            kept = (pad > 0) & (counts[m] > c)
            item = lax.broadcasted_iota(jnp.int32, (TILE, length), 0)
            same = item == seg
            segq[m] = jnp.where(same, 1.0, 0.0).T.astype(BF)
            segk[m] = jnp.where(same & kept, 0.0, MASKED).T.astype(BF)
            kept_out[m] = jnp.broadcast_to(jnp.where(kept, 1.0, 0.0), (TILE, length)).T

    lane = lax.broadcasted_iota(jnp.int32, (length, TILE), 1)
    for head in range(2):
        mine = (lane < TILE // 2) if head == 0 else (lane >= TILE // 2)
        line = jnp.broadcast_to(diag[2 * pair + head], (TILE, 2 * length))
        strip = pltpu.roll(line, 0, 1, stride=1, stride_axis=0)
        bias = jnp.concatenate(
            [strip[:, length - (i + 1) * TILE : 2 * length - (i + 1) * TILE] for i in range(length // TILE)], 0
        )
        for m in range(rows):
            query = jnp.concatenate([q_out[m, pair], segq[m]], 1)
            key = jnp.concatenate([jnp.where(mine, k_out[m, pair], 0), segk[m]], 1)
            value = jnp.concatenate([jnp.where(mine, v_out[m, pair], 0), jnp.where(mine, 1.0, 0.0).astype(BF)], 1)
            scores = dot_nt(query, key) + bias
            e = jnp.exp(scores - jnp.max(scores, -1, keepdims=True)).astype(BF)
            e_out[m, 0, head] = e
            weighed = dot(e, value)
            if head == 0:
                att_acc = weighed
                inv_out[m, pair] = att_acc[:, TILE:]
                half_att = att_acc[:, :TILE]
                middle_out[m, :, :TILE] = half_att
            else:
                inv = 1.0 / (inv_out[m, pair] + weighed[:, TILE:])
                inv_out[m, pair] = inv
                att_out[m, pair] = ((middle_out[m, :, :TILE] + weighed[:, :TILE]) * inv).astype(BF)

    @pl.when(pair == pairs - 1)
    def _():
        for m in range(rows):
            attended = jnp.concatenate([att_out[m, p] for p in range(pairs)], 1)
            branch = dot(attended, wo[...])
            middle = x_out[m].astype(F32) + wide(kept_out[m], branch.shape[1]) * branch
            middle_out[m] = middle
            r = lax.rsqrt(jnp.mean(middle * middle, -1, keepdims=True) + EPSILON)
            second_out[m] = (middle * r * fgain[...]).astype(BF)


def gelu_parts(u):
    z = jnp.abs(u) * (0.5**0.5)
    t = 1.0 / (1.0 + 0.3275911 * z)
    bell = jnp.exp(u * u * -0.5)
    poly = ((((1.061405429 * t - 1.453152027) * t + 1.421413741) * t - 0.284496736) * t + 0.254829592) * t
    tail = 0.5 * poly * bell
    upper = jnp.where(u >= 0, 1.0 - tail, tail)
    return upper, u * bell * ((2.0 * math.pi) ** -0.5)


def feed_chunk(second, fg, w_in, w_down, acc, sg):
    down = into = None
    for m in range(second.shape[0]):
        u = dot(second[m], w_in[...])
        upper, slope = gelu_parts(u)
        active = (u * upper).astype(BF)
        acc[m] += dot(active, w_down[...])
        up = (dot_nt(fg[m], w_down[...]) * (upper + slope)).astype(BF)
        sg[m] += dot_nt(up, w_in[...])
        down_now, into_now = dot_tn(active, fg[m]), dot_tn(second[m], up)
        down = down_now if m == 0 else down + down_now
        into = into_now if m == 0 else into + into_now
    return down, into


def tall(ref):
    return jnp.concatenate([ref[m] for m in range(ref.shape[0])], 0)


def feed_first_kernel(
    who, own, got, kept, second, w_in_far, w_down_far,
    g_out, fg_out, acc_out, sg_out, keep, send,
    w_ins, w_downs, sems,
    *, steps,
):
    step = pl.program_id(0)
    rows, half, width = own.shape
    copies = [
        fetches(feed_weights(w_in_far, w_down_far, i, width), (w_ins.at[i], w_downs.at[i]), sems.at[i])
        for i in range(steps)
    ]

    @pl.when(step == 0)
    def _():
        for copy in sum(copies, []):
            copy.start()
        for m in range(rows):
            g = fill_row(g_out, own, got, m, who[0], half)
            fg_out[m] = (g.astype(F32) * wide(kept[m], g.shape[1])).astype(BF)
        acc_out[...] = jnp.zeros_like(acc_out)
        sg_out[...] = jnp.zeros_like(sg_out)

    for i in range(steps):

        @pl.when(step == i)
        def _():
            for copy in copies[i]:
                copy.wait()

    down, into = feed_chunk(second, fg_out, w_ins.at[step], w_downs.at[step], acc_out, sg_out)
    put_block(keep, send, who, step, 2 * steps, down)
    put_block(keep, send, who, steps + step, 2 * steps, into)


def feed_third_kernel(
    chunk, who, g, fg, acc_in, sg_in, kept, middle, second, att, fgain, wo_far, w_in_far, w_down_far,
    acc, sg, keep_out, send_out, mg_out, back_out, gf_out, down_out, in_out, o_out,
    half_rows, w_in, w_down, wo, sems,
):
    c = who[0]
    rows, length, width = g.shape
    half = length // 2
    pairs = width // TILE
    copies = fetches((*feed_weights(w_in_far, w_down_far, chunk, width), wo_far), (w_in, w_down, wo), sems)
    for copy in copies:
        copy.start()
    for copy in copies:
        copy.wait()
    down, into = feed_chunk(second, fg, w_in, w_down, acc, sg)
    down_out[...] = down.astype(BF)
    in_out[...] = into.astype(BF)
    gf = jnp.zeros(gf_out.shape, F32)
    for m in range(rows):
        mid = middle[m]
        held = wide(kept[m], width)
        half_rows[...] = mid + held * acc[m]
        keep_out[m] = half_of(half_rows, c, half).astype(BF)
        send_out[m] = half_of(half_rows, 1 - c, half).astype(BF)
        r = lax.rsqrt(jnp.mean(mid * mid, -1, keepdims=True) + EPSILON)
        later = sg[m]
        across = later * mid
        gf = gf + jnp.sum(across * r, 0, keepdims=True)
        inner = jnp.mean(across * fgain[...], -1, keepdims=True)
        mg = g[m].astype(F32) + r * (later * fgain[...]) - mid * (r * r * r * inner)
        mg_out[m] = mg
        branch = (held * mg).astype(BF)
        back = dot_nt(branch, wo[...]).astype(BF)
        attended = jnp.concatenate([att[m, p] for p in range(pairs)], 1)
        for p in range(pairs):
            back_out[m, p] = back[:, p * TILE : (p + 1) * TILE]
        out_now = dot_tn(attended, branch)
        go = out_now if m == 0 else go + out_now
    gf_out[...] = gf
    o_out[...] = go.astype(BF)


def backward_kernel(
    e_in, q, k, v, inv, att, grad_att,
    dq_out, dk_out, dv_out, diag_out,
    strip,
    *, base,
):
    step = pl.program_id(0)
    pair = step + base
    rows, length = q.shape[0], q.shape[2]
    lane = lax.broadcasted_iota(jnp.int32, (length, TILE), 1)
    low = lane < TILE // 2
    strip[...] = jnp.zeros_like(strip)
    for m in range(rows):
        got = grad_att[m, pair].astype(F32)
        inverse = inv[m, pair]
        scaled = (got * inverse).astype(BF)
        weighed = got * inverse * att[m, pair].astype(F32)
        extra = jnp.zeros((length, TILE), F32)
        for head in range(2):
            mine = low if head == 0 else jnp.logical_not(low)
            centre = -jnp.sum(jnp.where(mine, weighed, 0.0), -1, keepdims=True)
            rough = centre.astype(BF).astype(F32)
            extra = jnp.where(lane == 2 * head, rough, extra)
            extra = jnp.where(lane == 2 * head + 1, centre - rough, extra)
        left = jnp.concatenate([scaled, extra.astype(BF)], 1)
        dq = dk = dv = None
        for head in range(2):
            mine = low if head == 0 else jnp.logical_not(low)
            ones = jnp.where((lane == 2 * head) | (lane == 2 * head + 1), 1.0, 0.0).astype(BF)
            right = jnp.concatenate([jnp.where(mine, v[m, pair], 0), ones], 1)
            e = e_in[m, 0, head]
            ds = e.astype(F32) * dot_nt(left, right)
            for i in range(length // TILE):
                start = length - (i + 1) * TILE
                strip[head, :, start : start + length] += ds[i * TILE : (i + 1) * TILE]
            ds = ds.astype(BF)
            dq_now = dot(ds, jnp.where(mine, k[m, pair], 0))
            dk_now = dot_tn(ds, jnp.where(mine, q[m, pair], 0))
            dv_now = dot_tn(e, jnp.where(mine, scaled, 0))
            dq = dq_now if dq is None else dq + dq_now
            dk = dk_now if dk is None else dk + dk_now
            dv = dv_now if dv is None else dv + dv_now
        dq_out[m, step] = dq.astype(BF)
        dk_out[m, step] = dk.astype(BF)
        dv_out[m, step] = dv.astype(BF)
    lanes = strip.shape[2]
    for head in range(2):
        total = strip[head]
        count = TILE
        while count > 1:
            count //= 2
            total = total[:count] + pltpu.roll(total[count:], lanes - count, 1)
        diag_out[2 * step + head] = total


def joined(grads, m):
    return jnp.concatenate([grad[m, p] for grad in grads for p in range(grad.shape[1])], 1)


def weight_kernel(parts, bucket_count, *refs):
    who, normed = refs[:2]
    dq, dk, dv, diags = (refs[2 + i * parts : 2 + (i + 1) * parts] for i in range(4))
    gf, *blocks = refs[2 + 4 * parts : 6 + 4 * parts]
    wq_far, wk_far, wv_far, gain, keep, send, small_out, wq, wk, wv, sems = refs[6 + 4 * parts :]
    rows, length, width = normed.shape
    copies = fetches((wq_far, wk_far, wv_far), (wq, wk, wv), sems)
    for copy in copies:
        copy.start()
    n = tall(normed)
    summed = jnp.zeros((width, 1), F32)
    for place, (grads, weight) in enumerate(((dq, wq), (dk, wk), (dv, wv))):
        value = dot_tn(n, jnp.concatenate([joined(grads, m) for m in range(rows)], 0))
        copies[place].wait()
        summed = summed + jnp.sum(value * weight[...].astype(F32), -1, keepdims=True)
        put_block(keep, send, who, 3 + place, 6, value)
    for place, ready in enumerate(blocks):
        put_block(keep, send, who, place, 6, ready[...])
    ga = jnp.broadcast_to(summed, (width, TILE)).T[:1] / gain[...]
    lines = jnp.concatenate([diag[h] for diag in diags for h in range(diag.shape[0])], 0)
    buckets = diagonal_buckets(length, bucket_count // 2)
    lane = lax.broadcasted_iota(jnp.int32, (8, width), 1)
    table = jnp.zeros((8, width), F32)
    for b in range(bucket_count):
        total = jnp.sum(jnp.where(buckets == b, lines, 0.0), -1, keepdims=True)
        table = jnp.where(lane == b, total, table)
    small = jnp.concatenate([ga, gf[...], jnp.zeros((6, width), F32), table], 0)
    rough = small.astype(BF)
    small = jnp.concatenate([rough, (small - rough.astype(F32)).astype(BF)], 0)
    small_out[...] = small
    send[send.shape[0] - small.shape[0] :, :] = small


def input_kernel(parts, *refs):
    who, x, mg = refs[:3]
    dq, dk, dv = (refs[3 + i * parts : 3 + (i + 1) * parts] for i in range(3))
    wq_far, wk_far, wv_far, gain, keep_out, send_out, half_rows, wq, wk, wv, sems = refs[3 + 3 * parts :]
    copies = fetches((wq_far, wk_far, wv_far), (wq, wk, wv), sems)
    for copy in copies:
        copy.start()
    c = who[0]
    rows, length, width = x.shape
    half = length // 2
    for m in range(rows):
        back = None
        for i, (grads, weight) in enumerate(((dq, wq), (dk, wk), (dv, wv))):
            if m == 0:
                copies[i].wait()
            now = dot_nt(joined(grads, m), weight[...])
            back = now if back is None else back + now
        xm = x[m].astype(F32)
        r = lax.rsqrt(jnp.mean(xm * xm, -1, keepdims=True) + EPSILON)
        grown = back * gain[...]
        inner = jnp.mean(grown * xm, -1, keepdims=True)
        half_rows[...] = mg[m] + r * grown - xm * (r * r * r * inner)
        keep_out[m] = half_of(half_rows, c, half).astype(BF)
        send_out[m] = half_of(half_rows, 1 - c, half).astype(BF)


def fill_block(target, i, blocks, who, own, got):
    places = 1 << LEVELS
    count = target.shape[0] >> LEVELS
    for k in range(places):
        core = 2 * k // places
        place = jnp.bitwise_xor(k % (places // 2), who[1 + core])
        start = pl.multiple_of((place * blocks + i) * count, count)
        mine = who[0] == core
        value = jnp.where(mine, own[pl.ds(start, count), :], got[pl.ds(start, count), :])
        target[k * count : (k + 1) * count, :] = value.astype(F32)


def feed_result_kernel(who, own, got, down_out, in_out, made, sems):
    width = own.shape[1]
    steps = made.shape[0] // 2
    copies = []
    for i in range(2 * steps):
        fill_block(made.at[i], i, 2 * steps, who, own, got)
        part = slice((i % steps) * width, (i % steps + 1) * width)
        target = down_out.at[part, :] if i < steps else in_out.at[:, part]
        copies.append(pltpu.make_async_copy(made.at[i], target, sems.at[i]))
        copies[-1].start()
    for copy in copies:
        copy.wait()


def rest_half_kernel(theirs, who, part, *refs):
    core = 1 - who[0] if theirs else who[0]
    refs = refs[7:] if theirs else refs[2:]
    down_out, in_out, o_out, q_out, k_out, v_out = refs[:6]
    made, sems = refs[-2:]
    width = part.shape[1]
    half = width // 2
    start = lambda base: pl.ds(pl.multiple_of(base + core * half, half), half)
    last = down_out.shape[0] - width
    targets = [down_out.at[start(last), :], in_out.at[start(0), last : last + width]]
    targets += [out.at[start(0), :] for out in (o_out, q_out, k_out, v_out)]
    places = 1 << (LEVELS - 1)
    count = half // places
    mask = jnp.where(core == 0, who[1], who[2])
    copies = []
    for i, target in enumerate(targets):
        for k in range(places):
            first = pl.multiple_of((jnp.bitwise_xor(k, mask) * 6 + i) * count, count)
            made[i, k * count : (k + 1) * count, :] = part[pl.ds(first, count), :].astype(F32)
        copies.append(pltpu.make_async_copy(made.at[i], target, sems.at[i]))
        copies[-1].start()
    for copy in copies:
        copy.wait()


def other_result_kernel(who, part, *refs):
    own, outs = refs[6], refs[7:13]
    ga_out, gf_out, table_out, made, sems = refs[13:]
    rest_half_kernel(True, who, part, *refs[:7], *outs, made, sems)
    tail = own.shape[0] - SMALL
    small = jnp.where(who[0] == 0, own[tail:, :].astype(F32), part[tail:, :].astype(F32))
    small = small[: SMALL // 2] + small[SMALL // 2 :]
    ga_out[...] = small[:1]
    gf_out[...] = small[1:2]
    table_out[...] = small[8:, : table_out.shape[1]]


def land_kernel(has_small, then, *refs):
    kind, after = then
    keep, got = refs[:2]
    refs = refs[2:]
    rows = keep.shape[0]
    if has_small:
        small, refs = refs[0], refs[1:]
    send = refs[0]
    if kind == "gather":
        send[:rows, :] = keep[...]
        send[rows : 2 * rows, :] = got[...]
        if has_small:
            send[2 * rows :, :] = small[...]
        return
    total = (keep[...].astype(F32) + got[:rows, :].astype(F32)).astype(BF)
    if after == "halve":
        refs[1][...] = total[: rows // 2]
        total = total[rows // 2 :]
    send[: total.shape[0], :] = total
    if has_small:
        half = SMALL // 2
        grown = (small[:half, :].astype(F32) + got[rows : rows + half, :].astype(F32)) + (
            small[half:, :].astype(F32) + got[rows + half :, :].astype(F32)
        )
        rough = grown.astype(BF)
        grown = jnp.concatenate([rough, (grown - rough.astype(F32)).astype(BF)], 0)
        refs[-1][...] = grown
        if after != "gather":
            send[total.shape[0] :, :] = grown
            if after != "halve":
                refs[1][...] = total


def swap_pairs(dp, bits):
    if bits is None:
        return [(i, i ^ 1) for i in range(2 * dp)]
    return [(i, i ^ (2 << bits[i % 2])) for i in range(2 * dp)]


class Piece:
    def __init__(self, calls, keep, send, small, order, rest, dp):
        self.calls, self.keep, self.send, self.small, self.dp = calls, keep, send, small, dp
        steps = [("halve", None)] + [("halve", bits) for bits in order]
        steps += [("exchange", (bit, bit)) for bit in rest]
        self.steps = steps + [("gather", bits) for bits in order[::-1]] + [("finish", None)]
        self.got = None
        self.fly()

    def fly(self):
        self.got = lax.ppermute(self.send, ("dp", "seq"), swap_pairs(self.dp, self.steps[0][1]))

    def land(self):
        kind, _ = self.steps.pop(0)
        after = self.steps[0][0]
        rows, width = self.keep.shape
        small = self.small is not None and (kind != "gather" or after == "finish")
        more = SMALL if small and after != "gather" else 0
        sds = lambda count: jax.ShapeDtypeStruct((count, width), BF)
        if kind == "gather":
            outs = [sds(2 * rows + more)]
        elif after == "halve":
            outs = [sds(rows // 2 + more), sds(rows // 2)]
        else:
            outs = [sds(rows + more)] + [sds(rows)] * (more > 0)
        if small and kind != "gather":
            outs.append(sds(SMALL))
        inputs = [self.keep, self.got] + [self.small] * small
        outs = self.calls.call(
            functools.partial(land_kernel, small, (kind, after)), "land", 0.5, inputs, [whole()] * len(inputs), outs
        )
        self.send = outs[0]
        if small and kind != "gather":
            self.small = outs[-1]
        split = kind != "gather" and (after == "halve" or more > 0)
        self.keep = outs[1] if split else outs[0]
        self.fly()
        return self

    def done(self):
        while len(self.steps) > 1:
            self.land()
        return self.send, self.got


def on_device(
    tokens, cotangent, segments, pad_mask, row_counts, attend_gain, w_query, w_key, w_value, w_out,
    forward_gain, w_in, w_down, position_bias_table,
):
    rows, slots, half, width = tokens.shape
    dp, seq = lax.axis_size("dp"), lax.axis_size("seq")
    bits = dp.bit_length() - 1
    assert seq == 2 and slots == 2 and dp == 1 << bits and bits >= 3
    length = seq * half
    inner = w_query.shape[1]
    ff = w_in.shape[1]
    bucket_count, heads = position_bias_table.shape
    pairs = inner // TILE
    assert heads == 2 * pairs == 8 and inner == width
    blocks = ff // width
    assert blocks == SPLIT + 2
    splits = (SPLIT, 2)
    orders = ORDERS
    rests = [[bit for bit in range(bits) if all(bit not in pair for pair in order)] for order in orders]

    def where_am_i(order):
        def who():
            here = lax.axis_index("dp")
            masks = []
            for core in range(2):
                mask = jnp.int32(0)
                for pair in order:
                    mask = 2 * mask + ((here >> pair[core]) & 1)
                masks.append(mask)
            return [lax.axis_index("seq"), *masks]

        return who

    who = [where_am_i(order) for order in orders]
    swap = lambda a: lax.ppermute(a, ("dp", "seq"), swap_pairs(dp, None))
    tokens, cotangent, segments, pad_mask, w_query, w_key, w_value, w_out, w_in, w_down = (
        pltpu.with_memory_space_constraint(array, pltpu.HBM)
        for array in (tokens, cotangent, segments, pad_mask, w_query, w_key, w_value, w_out, w_in, w_down)
    )
    table = jnp.broadcast_to(position_bias_table[:, :, None], (bucket_count, heads, 1))
    gain, fgain = attend_gain.reshape(1, width), forward_gain.reshape(1, width)
    sds = jax.ShapeDtypeStruct
    vm = pltpu.VMEM
    dma = pltpu.SemaphoreType.DMA
    paired = sds((rows, pairs, length, TILE), BF)
    wide_bf, wide_f32 = sds((rows, length, width), BF), sds((rows, length, width), F32)
    narrow, items = sds((rows, length, TILE), F32), sds((rows, length, TILE), BF)
    square, square_bf = sds((inner, width), F32), sds((inner, width), BF)
    row_half, marked = sds((rows, half, width), BF), sds((2, rows, half), jnp.int32)
    calls = Order()
    call = calls.call

    tok_send, marks_own, marks_send = call(
        pick_kernel, "pick", 1, (tokens, segments, pad_mask), [far()] * 3,
        (row_half, marked, marked), scratch=[vm((2, rows, slots, half), jnp.int32), dma((rows + 2,))], who=who[0],
    )
    tok_got, marks_got = swap(tok_send), swap(marks_send)
    tok_own, cot_own, cot_send = call(
        pick_rest_kernel, "pick_rest", 1, (tokens, cotangent), [far(), far()],
        (row_half, row_half, row_half), scratch=[dma((3 * rows,))], who=who[0],
    )
    cot_got = swap(cot_send)
    e_shape = (rows, pairs, 2, length, length)
    x, normed, q, k, v, e, inv, att, kept, middle, second = call(
        forward_kernel, "attend_forward", 14,
        (
            row_counts.reshape(rows), tok_own, tok_got, marks_own, marks_got, table, gain, fgain,
            w_query, w_key, w_value, w_out,
        ),
        [smem()] + [whole()] * 7 + [far()] * 4,
        (
            wide_bf, wide_bf, paired, paired, paired, sds(e_shape, BF),
            sds((rows, pairs, length, TILE), F32), paired, narrow, wide_f32, wide_bf,
        ),
        grid=pairs,
        out_specs=[whole()] * 5 + [pl.BlockSpec((rows, 1, 2, length, length), lambda p: (0, p, 0, 0, 0))] + [whole()] * 5,
        scratch=[vm((rows, length, TILE), BF)] * 2 + [vm((heads, 1, 2 * length), F32)] + [vm((width, inner), BF)] * 4 + [dma((4,))],
        vmem=VMEM[0],
        who=who[0],
    )

    block = vm((width, width), BF)
    piece_halves = lambda count, more=0: (sds((count * width // 2, width), BF), sds((count * width // 2 + more, width), BF))
    first = blocks - 1
    g, fg, acc, sg, keep, send = call(
        functools.partial(feed_first_kernel, steps=first), "feed_first", 5 * first,
        (cot_own, cot_got, kept, second, w_in, w_down),
        [whole()] * 4 + [far()] * 2,
        (wide_bf, wide_bf, wide_f32, wide_f32, *piece_halves(2 * first)),
        grid=first,
        scratch=[vm((first, width, width), BF)] * 2 + [dma((first, 2))],
        vmem=VMEM[1],
        who=who[0],
    )
    a = Piece(calls, keep, send, None, orders[0], rests[0], dp)
    _, _, out_own, out_send, mg, grad_att, gf, *ready = call(
        functools.partial(feed_third_kernel, first), "feed_third", 8,
        (g, fg, acc, sg, kept, middle, second, att, fgain, w_out, w_in, w_down),
        [whole()] * 9 + [far()] * 3,
        (
            wide_f32, wide_f32, row_half, row_half, wide_f32, paired, sds((1, width), F32),
            square_bf, square_bf, square_bf,
        ),
        scratch=[vm((length, width), F32), block, block, block, dma((3,))],
        vmem=VMEM[3],
        aliases={2: 0, 3: 1},
        who=who[0],
    )

    some = sds((rows, pairs // PARTS, length, TILE), BF)
    dq, dk, dv, diag = [], [], [], []
    a.land()
    for part in range(PARTS):
        base = part * (pairs // PARTS)
        outs = call(
            functools.partial(backward_kernel, base=base), "attend_backward", 12 / PARTS,
            (e, q, k, v, inv, att, grad_att),
            [pl.BlockSpec((rows, 1, 2, length, length), lambda p, base=base: (0, p + base, 0, 0, 0))] + [whole()] * 6,
            (some, some, some, sds((heads // PARTS, 1, 2 * length), F32)),
            grid=pairs // PARTS,
            scratch=[vm((2, TILE, 2 * length), F32)],
            vmem=VMEM[4],
        )
        for kept_list, out in zip((dq, dk, dv, diag), outs):
            kept_list.append(out)
        a.land()
    keep, send, small = call(
        functools.partial(weight_kernel, PARTS, bucket_count), "weight_grads", 3,
        (normed, *dq, *dk, *dv, *diag, gf, *ready, w_query, w_key, w_value, gain),
        [whole()] * (5 + 4 * PARTS) + [far()] * 3 + [whole()],
        (*piece_halves(6, SMALL), sds((SMALL, width), BF)),
        scratch=[block, block, block, dma((3,))],
        vmem=VMEM[5],
        who=who[1],
    )
    c_piece = Piece(calls, keep, send, small, orders[1], rests[1], dp)
    in_own, in_send = call(
        functools.partial(input_kernel, PARTS), "input_grad", 4,
        (x, mg, *dq, *dk, *dv, w_query, w_key, w_value, gain),
        [whole()] * (2 + 3 * PARTS) + [far()] * 3 + [whole()],
        (row_half, row_half),
        scratch=[vm((length, width), F32), block, block, block, dma((3,))],
        vmem=VMEM[6],
        who=who[0],
    )
    a.land()
    out_got = swap(out_send)
    in_got = swap(in_send)
    grad_down = None
    all_rows = sds((rows, slots, half, width), BF)
    c_piece.land()
    a.land()
    c_piece.land()
    a.land()
    c_piece.land()
    while len(a.steps) > 1 or grad_down is None:
        if len(a.steps) > 1 or len(c_piece.steps) > 1:
            c_piece.land()
        if len(a.steps) > 1:
            a.land()
        else:
            grad_down, grad_in = call(
                feed_result_kernel, "feed_result", 4, a.done(), [whole()] * 2,
                (sds((ff, width), F32), sds((width, ff), F32)),
                out_specs=[far(), far()],
                scratch=[vm((2 * first, width, width), F32), dma((2 * first,))],
                vmem=VMEM[7],
                who=who[0],
            )
            output, grad_input = call(
                place_kernel, "place", 1, (out_own, out_got, in_own, in_got), [whole()] * 4,
                (all_rows, all_rows), out_specs=[far(), far()], scratch=[dma((4 * rows,))], who=who[0],
            )
    own, got = c_piece.done()
    shapes = (sds((ff, width), F32), sds((width, ff), F32), square, square, square, square)
    result_scratch = [vm((6, width // 2, width), F32), dma((6,))]
    results = call(
        functools.partial(rest_half_kernel, False), "own_result", 2, (own, grad_down, grad_in), [whole()] + [far()] * 2,
        shapes, out_specs=[far()] * 6, scratch=result_scratch, vmem=VMEM[7], aliases={1: 0, 2: 1}, who=who[1],
    )
    *results, ga, gf, grad_table = call(
        functools.partial(other_result_kernel), "other_result", 2, (got, *results, own), [whole()] + [far()] * 6 + [whole()],
        (*shapes, sds((1, width), F32), sds((1, width), F32), sds((heads, bucket_count), F32)),
        out_specs=[far()] * 6 + [whole()] * 3,
        scratch=result_scratch, vmem=VMEM[7], aliases={1 + n: n for n in range(6)}, who=who[1],
    )
    grad_down, grad_in, grad_out, grad_query, grad_key, grad_value = results

    return (
        output,
        grad_input,
        ga.reshape(width),
        grad_query,
        grad_key,
        grad_value,
        grad_out,
        gf.reshape(width),
        grad_in,
        grad_down,
        grad_table.T,
    )


def solution(mesh):
    placed = (P(None, "dp", "seq", None),) * 2 + (P(None, "dp", "seq"),) * 2 + (P(None, "dp"),) + (P(),) * 9
    return jax.shard_map(
        on_device,
        mesh=mesh,
        in_specs=placed,
        out_specs=(P(None, "dp", "seq", None),) * 2 + (P(),) * 9,
        check_vma=False,
    )
```

```python
import functools
import math

import jax
import jax.numpy as jnp
from jax import lax
from jax.experimental import pallas as pl
from jax.experimental.pallas import tpu as pltpu
from jax.sharding import PartitionSpec as P

EPSILON = 1e-06
MASKED = -1000000000.0
LIMITS = (12, 16, 23, 32, 46, 64, 91)
BF = jnp.bfloat16
F32 = jnp.float32
TILE = 128
LEVELS = 4
SPLIT = 2
SMALL = 32
COST = 3e9
PARTS = 2
FREE = ("pick_rest", "attend_forward", "feed_first", "feed_third")
ORDERS = ([(0, 1), (1, 0), (2, 2)], [(1, 0), (0, 1), (2, 2)])
VMEM = (16, 15, 12, 14, 12, 10, 10, 14)


def whole():
    return pl.BlockSpec(memory_space=pltpu.VMEM)


def hbm():
    return pl.BlockSpec(memory_space=pl.ANY)


def far():
    return pl.BlockSpec(memory_space=pltpu.HBM)


def smem():
    return pl.BlockSpec(memory_space=pltpu.SMEM)


class Order:
    def __init__(self):
        self.token = None

    def call(self, kernel, name, micros, inputs, in_specs, out_shape, grid=1, out_specs=None, scratch=(), vmem=8, aliases=None, who=None):
        count, results = len(inputs), len(out_shape)
        extra = () if self.token is None or name in FREE else (self.token,)

        skip = count + len(extra)

        def body(*refs):
            token = refs[skip + results]
            token[...] = jnp.zeros_like(token)
            first = () if who is None else (who(),)
            kernel(*first, *refs[:count], *refs[skip : skip + results], *refs[skip + results + 1 :])

        *outs, self.token = pl.pallas_call(
            body,
            grid=(grid,),
            in_specs=list(in_specs) + [whole()] * len(extra),
            out_specs=list(out_specs or [whole() for _ in out_shape]) + [whole()],
            out_shape=(*out_shape, jax.ShapeDtypeStruct((8, TILE), F32)),
            scratch_shapes=list(scratch),
            input_output_aliases=aliases or {},
            compiler_params=pltpu.CompilerParams(vmem_limit_bytes=vmem * 1024 * 1024),
            cost_estimate=pl.CostEstimate(
                flops=int(micros * COST), bytes_accessed=1 << 20, transcendentals=0
            ),
            name=name,
        )(*inputs, *extra)
        return outs


def dot(a, b, contract=((1,), (0,))):
    return lax.dot_general(a, b, (contract, ((), ())), preferred_element_type=F32)


def dot_nt(a, b):
    return dot(a, b, ((1,), (1,)))


def dot_tn(a, b):
    return dot(a, b, ((0,), (0,)))


def bucket_of(relative, half_count):
    distance = jnp.abs(relative)
    far = jnp.full(relative.shape, 8, jnp.int32)
    for bound in LIMITS:
        far = far + (distance >= bound).astype(jnp.int32)
    near_or_far = jnp.where(distance < 8, distance, far)
    return near_or_far + jnp.where(relative > 0, half_count, 0)


def diagonal_buckets(length, half_count):
    lane = lax.broadcasted_iota(jnp.int32, (8, 2 * length), 1)
    relative = lane - (length - TILE)
    relative = jnp.where(lane < 2 * length - TILE, relative, relative - 2 * length)
    return bucket_of(relative, half_count)


def wide(column, width):
    return jnp.concatenate([column] * (width // TILE), axis=1)


def put_block(keep, send, who, block, blocks, value):
    count = value.shape[0] >> LEVELS
    places = 1 << LEVELS
    for core in range(2):

        @pl.when(who[0] == core)
        def _():
            for k in range(places):
                place = jnp.bitwise_xor(k % (places // 2), who[1 + 2 * k // places])
                start = pl.multiple_of((place * blocks + block) * count, count)
                ref = keep if 2 * k // places == core else send
                ref[pl.ds(start, count), :] = value[k * count : (k + 1) * count].astype(ref.dtype)


def half_of(ref, i, half):
    return ref[pl.ds(pl.multiple_of(i * half, half), half), :]


def fill_row(row_ref, own_ref, got_ref, m, c, half):
    row_ref[m, pl.ds(pl.multiple_of(c * half, half), half), :] = own_ref[m]
    row_ref[m, pl.ds(pl.multiple_of((1 - c) * half, half), half), :] = got_ref[m]
    return row_ref[m]


def join(own, got, c):
    return jnp.where(c == 0, jnp.concatenate([own, got], 1), jnp.concatenate([got, own], 1))


def fetches(sources, targets, sems):
    return [pltpu.make_async_copy(a, b, sems.at[i]) for i, (a, b) in enumerate(zip(sources, targets))]


def feed_weights(w_in, w_down, chunk, width):
    start = pl.multiple_of(chunk * width, width)
    return w_in.at[:, pl.ds(start, width)], w_down.at[pl.ds(start, width), :]


def pick_kernel(who, tok, seg, pad, tok_send, marks_own, marks_send, near, sems):
    c = who[0]
    rows = tok.shape[0]
    copies = [pltpu.make_async_copy(tok.at[m, 1 - c], tok_send.at[m], sems.at[m]) for m in range(rows)]
    marked = [pltpu.make_async_copy(marks, near.at[i], sems.at[rows + i]) for i, marks in enumerate((seg, pad))]
    for copy in copies + marked:
        copy.start()
    for copy in marked:
        copy.wait()
    for kind in range(2):
        for m in range(rows):
            first, second = near[kind, m, pl.ds(0, 1)], near[kind, m, pl.ds(1, 1)]
            marks_own[kind, pl.ds(m, 1)] = jnp.where(c == 0, first, second)
            marks_send[kind, pl.ds(m, 1)] = jnp.where(c == 0, second, first)
    for copy in copies:
        copy.wait()


def pick_rest_kernel(who, tok, cot, tok_own, cot_own, cot_send, sems):
    c = who[0]
    copies = []
    for m in range(tok.shape[0]):
        for source, slot, target in ((tok, c, tok_own), (cot, 1 - c, cot_send), (cot, c, cot_own)):
            copies.append(pltpu.make_async_copy(source.at[m, slot], target.at[m], sems.at[len(copies)]))
    for copy in copies:
        copy.start()
    for copy in copies:
        copy.wait()


def place_kernel(who, *refs):
    c = who[0]
    count = (len(refs) - 1) // 3
    sems = refs[-1]
    copies = []
    for i in range(count):
        own, got, out = refs[2 * i], refs[2 * i + 1], refs[2 * count + i]
        for m in range(own.shape[0]):
            for source, slot in ((own, c), (got, 1 - c)):
                copies.append(pltpu.make_async_copy(source.at[m], out.at[m, slot], sems.at[len(copies)]))
    for copy in copies:
        copy.start()
    for copy in copies:
        copy.wait()


def forward_kernel(
    who, counts, own, got, marks, marks_got, table, gain, fgain, wq_far, wk_far, wv_far, wo_far,
    x_out, normed_out, q_out, k_out, v_out, e_out, inv_out, att_out, kept_out, middle_out, second_out,
    segq, segk, diag, wq, wk, wv, wo, sems,
):
    c = who[0]
    pair = pl.program_id(0)
    rows, half = own.shape[0], own.shape[1]
    length = 2 * half
    pairs = wq.shape[1] // TILE
    bucket_count = table.shape[0]
    copies = fetches((wq_far, wk_far, wv_far, wo_far), (wq, wk, wv, wo), sems)

    @pl.when(pair == 0)
    def _():
        for copy in copies:
            copy.start()
        buckets = diagonal_buckets(length, bucket_count // 2)
        strip = jnp.zeros(buckets.shape, F32)
        for b in range(bucket_count):
            strip = jnp.where(buckets == b, table[b], strip)
        for h in range(strip.shape[0]):
            diag[h] = strip[h : h + 1]
        for m in range(rows):
            x = fill_row(x_out, own, got, m, c, half).astype(F32)
            r = lax.rsqrt(jnp.mean(x * x, -1, keepdims=True) + EPSILON)
            normed = (x * r * gain[...]).astype(BF)
            normed_out[m] = normed
            if m == 0:
                for copy in copies:
                    copy.wait()
            for w, out in ((wq, q_out), (wk, k_out), (wv, v_out)):
                projected = dot(normed, w[...]).astype(BF)
                for p in range(pairs):
                    out[m, p] = projected[:, p * TILE : (p + 1) * TILE]
            seg = join(marks[0, pl.ds(m, 1)], marks_got[0, pl.ds(m, 1)], c)
            pad = join(marks[1, pl.ds(m, 1)], marks_got[1, pl.ds(m, 1)], c)
            kept = (pad > 0) & (counts[m] > c)
            item = lax.broadcasted_iota(jnp.int32, (TILE, length), 0)
            same = item == seg
            segq[m] = jnp.where(same, 1.0, 0.0).T.astype(BF)
            segk[m] = jnp.where(same & kept, 0.0, MASKED).T.astype(BF)
            kept_out[m] = jnp.broadcast_to(jnp.where(kept, 1.0, 0.0), (TILE, length)).T

    lane = lax.broadcasted_iota(jnp.int32, (length, TILE), 1)
    for head in range(2):
        mine = (lane < TILE // 2) if head == 0 else (lane >= TILE // 2)
        line = jnp.broadcast_to(diag[2 * pair + head], (TILE, 2 * length))
        strip = pltpu.roll(line, 0, 1, stride=1, stride_axis=0)
        bias = jnp.concatenate(
            [strip[:, length - (i + 1) * TILE : 2 * length - (i + 1) * TILE] for i in range(length // TILE)], 0
        )
        for m in range(rows):
            query = jnp.concatenate([q_out[m, pair], segq[m]], 1)
            key = jnp.concatenate([jnp.where(mine, k_out[m, pair], 0), segk[m]], 1)
            value = jnp.concatenate([jnp.where(mine, v_out[m, pair], 0), jnp.where(mine, 1.0, 0.0).astype(BF)], 1)
            scores = dot_nt(query, key) + bias
            e = jnp.exp(scores - jnp.max(scores, -1, keepdims=True)).astype(BF)
            e_out[m, 0, head] = e
            weighed = dot(e, value)
            if head == 0:
                att_acc = weighed
                inv_out[m, pair] = att_acc[:, TILE:]
                half_att = att_acc[:, :TILE]
                middle_out[m, :, :TILE] = half_att
            else:
                inv = 1.0 / (inv_out[m, pair] + weighed[:, TILE:])
                inv_out[m, pair] = inv
                att_out[m, pair] = ((middle_out[m, :, :TILE] + weighed[:, :TILE]) * inv).astype(BF)

    @pl.when(pair == pairs - 1)
    def _():
        for m in range(rows):
            attended = jnp.concatenate([att_out[m, p] for p in range(pairs)], 1)
            branch = dot(attended, wo[...])
            middle = x_out[m].astype(F32) + wide(kept_out[m], branch.shape[1]) * branch
            middle_out[m] = middle
            r = lax.rsqrt(jnp.mean(middle * middle, -1, keepdims=True) + EPSILON)
            second_out[m] = (middle * r * fgain[...]).astype(BF)


def gelu_parts(u):
    z = jnp.abs(u) * (0.5**0.5)
    t = 1.0 / (1.0 + 0.3275911 * z)
    bell = jnp.exp(u * u * -0.5)
    poly = ((((1.061405429 * t - 1.453152027) * t + 1.421413741) * t - 0.284496736) * t + 0.254829592) * t
    tail = 0.5 * poly * bell
    upper = jnp.where(u >= 0, 1.0 - tail, tail)
    return upper, u * bell * ((2.0 * math.pi) ** -0.5)


def feed_chunk(second, fg, w_in, w_down, acc, sg):
    down = into = None
    for m in range(second.shape[0]):
        u = dot(second[m], w_in[...])
        upper, slope = gelu_parts(u)
        active = (u * upper).astype(BF)
        acc[m] += dot(active, w_down[...])
        up = (dot_nt(fg[m], w_down[...]) * (upper + slope)).astype(BF)
        sg[m] += dot_nt(up, w_in[...])
        down_now, into_now = dot_tn(active, fg[m]), dot_tn(second[m], up)
        down = down_now if m == 0 else down + down_now
        into = into_now if m == 0 else into + into_now
    return down, into


def tall(ref):
    return jnp.concatenate([ref[m] for m in range(ref.shape[0])], 0)


def feed_first_kernel(
    who, own, got, kept, second, w_in_far, w_down_far,
    g_out, fg_out, acc_out, sg_out, keep, send,
    w_ins, w_downs, sems,
    *, steps,
):
    step = pl.program_id(0)
    rows, half, width = own.shape
    copies = [
        fetches(feed_weights(w_in_far, w_down_far, i, width), (w_ins.at[i], w_downs.at[i]), sems.at[i])
        for i in range(steps)
    ]

    @pl.when(step == 0)
    def _():
        for copy in sum(copies, []):
            copy.start()
        for m in range(rows):
            g = fill_row(g_out, own, got, m, who[0], half)
            fg_out[m] = (g.astype(F32) * wide(kept[m], g.shape[1])).astype(BF)
        acc_out[...] = jnp.zeros_like(acc_out)
        sg_out[...] = jnp.zeros_like(sg_out)

    for i in range(steps):

        @pl.when(step == i)
        def _():
            for copy in copies[i]:
                copy.wait()

    down, into = feed_chunk(second, fg_out, w_ins.at[step], w_downs.at[step], acc_out, sg_out)
    put_block(keep, send, who, step, 2 * steps, down)
    put_block(keep, send, who, steps + step, 2 * steps, into)


def feed_third_kernel(
    chunk, who, g, fg, acc_in, sg_in, kept, middle, second, att, fgain, wo_far, w_in_far, w_down_far,
    acc, sg, keep_out, send_out, mg_out, back_out, gf_out, down_out, in_out, o_out,
    half_rows, w_in, w_down, wo, sems,
):
    c = who[0]
    rows, length, width = g.shape
    half = length // 2
    pairs = width // TILE
    copies = fetches((*feed_weights(w_in_far, w_down_far, chunk, width), wo_far), (w_in, w_down, wo), sems)
    for copy in copies:
        copy.start()
    for copy in copies:
        copy.wait()
    down, into = feed_chunk(second, fg, w_in, w_down, acc, sg)
    down_out[...] = down.astype(BF)
    in_out[...] = into.astype(BF)
    gf = jnp.zeros(gf_out.shape, F32)
    for m in range(rows):
        mid = middle[m]
        held = wide(kept[m], width)
        half_rows[...] = mid + held * acc[m]
        keep_out[m] = half_of(half_rows, c, half).astype(BF)
        send_out[m] = half_of(half_rows, 1 - c, half).astype(BF)
        r = lax.rsqrt(jnp.mean(mid * mid, -1, keepdims=True) + EPSILON)
        later = sg[m]
        across = later * mid
        gf = gf + jnp.sum(across * r, 0, keepdims=True)
        inner = jnp.mean(across * fgain[...], -1, keepdims=True)
        mg = g[m].astype(F32) + r * (later * fgain[...]) - mid * (r * r * r * inner)
        mg_out[m] = mg
        branch = (held * mg).astype(BF)
        back = dot_nt(branch, wo[...]).astype(BF)
        attended = jnp.concatenate([att[m, p] for p in range(pairs)], 1)
        for p in range(pairs):
            back_out[m, p] = back[:, p * TILE : (p + 1) * TILE]
        out_now = dot_tn(attended, branch)
        go = out_now if m == 0 else go + out_now
    gf_out[...] = gf
    o_out[...] = go.astype(BF)


def backward_kernel(
    e_in, q, k, v, inv, att, grad_att,
    dq_out, dk_out, dv_out, diag_out,
    strip,
    *, base,
):
    step = pl.program_id(0)
    pair = step + base
    rows, length = q.shape[0], q.shape[2]
    lane = lax.broadcasted_iota(jnp.int32, (length, TILE), 1)
    low = lane < TILE // 2
    strip[...] = jnp.zeros_like(strip)
    for m in range(rows):
        got = grad_att[m, pair].astype(F32)
        inverse = inv[m, pair]
        scaled = (got * inverse).astype(BF)
        weighed = got * inverse * att[m, pair].astype(F32)
        extra = jnp.zeros((length, TILE), F32)
        for head in range(2):
            mine = low if head == 0 else jnp.logical_not(low)
            centre = -jnp.sum(jnp.where(mine, weighed, 0.0), -1, keepdims=True)
            rough = centre.astype(BF).astype(F32)
            extra = jnp.where(lane == 2 * head, rough, extra)
            extra = jnp.where(lane == 2 * head + 1, centre - rough, extra)
        left = jnp.concatenate([scaled, extra.astype(BF)], 1)
        dq = dk = dv = None
        for head in range(2):
            mine = low if head == 0 else jnp.logical_not(low)
            ones = jnp.where((lane == 2 * head) | (lane == 2 * head + 1), 1.0, 0.0).astype(BF)
            right = jnp.concatenate([jnp.where(mine, v[m, pair], 0), ones], 1)
            e = e_in[m, 0, head]
            ds = e.astype(F32) * dot_nt(left, right)
            for i in range(length // TILE):
                start = length - (i + 1) * TILE
                strip[head, :, start : start + length] += ds[i * TILE : (i + 1) * TILE]
            ds = ds.astype(BF)
            dq_now = dot(ds, jnp.where(mine, k[m, pair], 0))
            dk_now = dot_tn(ds, jnp.where(mine, q[m, pair], 0))
            dv_now = dot_tn(e, jnp.where(mine, scaled, 0))
            dq = dq_now if dq is None else dq + dq_now
            dk = dk_now if dk is None else dk + dk_now
            dv = dv_now if dv is None else dv + dv_now
        dq_out[m, step] = dq.astype(BF)
        dk_out[m, step] = dk.astype(BF)
        dv_out[m, step] = dv.astype(BF)
    lanes = strip.shape[2]
    for head in range(2):
        total = strip[head]
        count = TILE
        while count > 1:
            count //= 2
            total = total[:count] + pltpu.roll(total[count:], lanes - count, 1)
        diag_out[2 * step + head] = total


def joined(grads, m):
    return jnp.concatenate([grad[m, p] for grad in grads for p in range(grad.shape[1])], 1)


def weight_kernel(parts, bucket_count, *refs):
    who, normed = refs[:2]
    dq, dk, dv, diags = (refs[2 + i * parts : 2 + (i + 1) * parts] for i in range(4))
    gf, *blocks = refs[2 + 4 * parts : 6 + 4 * parts]
    wq_far, wk_far, wv_far, gain, keep, send, small_out, wq, wk, wv, sems = refs[6 + 4 * parts :]
    rows, length, width = normed.shape
    copies = fetches((wq_far, wk_far, wv_far), (wq, wk, wv), sems)
    for copy in copies:
        copy.start()
    n = tall(normed)
    summed = jnp.zeros((width, 1), F32)
    for place, (grads, weight) in enumerate(((dq, wq), (dk, wk), (dv, wv))):
        value = dot_tn(n, jnp.concatenate([joined(grads, m) for m in range(rows)], 0))
        copies[place].wait()
        summed = summed + jnp.sum(value * weight[...].astype(F32), -1, keepdims=True)
        put_block(keep, send, who, 3 + place, 6, value)
    for place, ready in enumerate(blocks):
        put_block(keep, send, who, place, 6, ready[...])
    ga = jnp.broadcast_to(summed, (width, TILE)).T[:1] / gain[...]
    lines = jnp.concatenate([diag[h] for diag in diags for h in range(diag.shape[0])], 0)
    buckets = diagonal_buckets(length, bucket_count // 2)
    lane = lax.broadcasted_iota(jnp.int32, (8, width), 1)
    table = jnp.zeros((8, width), F32)
    for b in range(bucket_count):
        total = jnp.sum(jnp.where(buckets == b, lines, 0.0), -1, keepdims=True)
        table = jnp.where(lane == b, total, table)
    small = jnp.concatenate([ga, gf[...], jnp.zeros((6, width), F32), table], 0)
    rough = small.astype(BF)
    small = jnp.concatenate([rough, (small - rough.astype(F32)).astype(BF)], 0)
    small_out[...] = small
    send[send.shape[0] - small.shape[0] :, :] = small


def input_kernel(parts, *refs):
    who, x, mg = refs[:3]
    dq, dk, dv = (refs[3 + i * parts : 3 + (i + 1) * parts] for i in range(3))
    wq_far, wk_far, wv_far, gain, keep_out, send_out, half_rows, wq, wk, wv, sems = refs[3 + 3 * parts :]
    copies = fetches((wq_far, wk_far, wv_far), (wq, wk, wv), sems)
    for copy in copies:
        copy.start()
    c = who[0]
    rows, length, width = x.shape
    half = length // 2
    for m in range(rows):
        back = None
        for i, (grads, weight) in enumerate(((dq, wq), (dk, wk), (dv, wv))):
            if m == 0:
                copies[i].wait()
            now = dot_nt(joined(grads, m), weight[...])
            back = now if back is None else back + now
        xm = x[m].astype(F32)
        r = lax.rsqrt(jnp.mean(xm * xm, -1, keepdims=True) + EPSILON)
        grown = back * gain[...]
        inner = jnp.mean(grown * xm, -1, keepdims=True)
        half_rows[...] = mg[m] + r * grown - xm * (r * r * r * inner)
        keep_out[m] = half_of(half_rows, c, half).astype(BF)
        send_out[m] = half_of(half_rows, 1 - c, half).astype(BF)


def fill_block(target, i, blocks, who, own, got):
    places = 1 << LEVELS
    count = target.shape[0] >> LEVELS
    for k in range(places):
        core = 2 * k // places
        place = jnp.bitwise_xor(k % (places // 2), who[1 + core])
        start = pl.multiple_of((place * blocks + i) * count, count)
        mine = who[0] == core
        value = jnp.where(mine, own[pl.ds(start, count), :], got[pl.ds(start, count), :])
        target[k * count : (k + 1) * count, :] = value.astype(F32)


def feed_result_kernel(who, own, got, down_out, in_out, made, sems):
    width = own.shape[1]
    steps = made.shape[0] // 2
    copies = []
    for i in range(2 * steps):
        fill_block(made.at[i], i, 2 * steps, who, own, got)
        part = slice((i % steps) * width, (i % steps + 1) * width)
        target = down_out.at[part, :] if i < steps else in_out.at[:, part]
        copies.append(pltpu.make_async_copy(made.at[i], target, sems.at[i]))
        copies[-1].start()
    for copy in copies:
        copy.wait()


def rest_half_kernel(theirs, who, part, *refs):
    core = 1 - who[0] if theirs else who[0]
    refs = refs[7:] if theirs else refs[2:]
    down_out, in_out, o_out, q_out, k_out, v_out = refs[:6]
    made, sems = refs[-2:]
    width = part.shape[1]
    half = width // 2
    start = lambda base: pl.ds(pl.multiple_of(base + core * half, half), half)
    last = down_out.shape[0] - width
    targets = [down_out.at[start(last), :], in_out.at[start(0), last : last + width]]
    targets += [out.at[start(0), :] for out in (o_out, q_out, k_out, v_out)]
    places = 1 << (LEVELS - 1)
    count = half // places
    mask = jnp.where(core == 0, who[1], who[2])
    copies = []
    for i, target in enumerate(targets):
        for k in range(places):
            first = pl.multiple_of((jnp.bitwise_xor(k, mask) * 6 + i) * count, count)
            made[i, k * count : (k + 1) * count, :] = part[pl.ds(first, count), :].astype(F32)
        copies.append(pltpu.make_async_copy(made.at[i], target, sems.at[i]))
        copies[-1].start()
    for copy in copies:
        copy.wait()


def other_result_kernel(who, part, *refs):
    own, outs = refs[6], refs[7:13]
    ga_out, gf_out, table_out, made, sems = refs[13:]
    rest_half_kernel(True, who, part, *refs[:7], *outs, made, sems)
    tail = own.shape[0] - SMALL
    small = jnp.where(who[0] == 0, own[tail:, :].astype(F32), part[tail:, :].astype(F32))
    small = small[: SMALL // 2] + small[SMALL // 2 :]
    ga_out[...] = small[:1]
    gf_out[...] = small[1:2]
    table_out[...] = small[8:, : table_out.shape[1]]


def land_kernel(has_small, then, *refs):
    kind, after = then
    keep, got = refs[:2]
    refs = refs[2:]
    rows = keep.shape[0]
    if has_small:
        small, refs = refs[0], refs[1:]
    send = refs[0]
    if kind == "gather":
        send[:rows, :] = keep[...]
        send[rows : 2 * rows, :] = got[...]
        if has_small:
            send[2 * rows :, :] = small[...]
        return
    total = (keep[...].astype(F32) + got[:rows, :].astype(F32)).astype(BF)
    if after == "halve":
        refs[1][...] = total[: rows // 2]
        total = total[rows // 2 :]
    send[: total.shape[0], :] = total
    if has_small:
        half = SMALL // 2
        grown = (small[:half, :].astype(F32) + got[rows : rows + half, :].astype(F32)) + (
            small[half:, :].astype(F32) + got[rows + half :, :].astype(F32)
        )
        rough = grown.astype(BF)
        grown = jnp.concatenate([rough, (grown - rough.astype(F32)).astype(BF)], 0)
        refs[-1][...] = grown
        if after != "gather":
            send[total.shape[0] :, :] = grown
            if after != "halve":
                refs[1][...] = total


def swap_pairs(dp, bits):
    if bits is None:
        return [(i, i ^ 1) for i in range(2 * dp)]
    return [(i, i ^ (2 << bits[i % 2])) for i in range(2 * dp)]


class Piece:
    def __init__(self, calls, keep, send, small, order, rest, dp):
        self.calls, self.keep, self.send, self.small, self.dp = calls, keep, send, small, dp
        steps = [("halve", None)] + [("halve", bits) for bits in order]
        steps += [("exchange", (bit, bit)) for bit in rest]
        self.steps = steps + [("gather", bits) for bits in order[::-1]] + [("finish", None)]
        self.got = None
        self.fly()

    def fly(self):
        self.got = lax.ppermute(self.send, ("dp", "seq"), swap_pairs(self.dp, self.steps[0][1]))

    def land(self):
        kind, _ = self.steps.pop(0)
        after = self.steps[0][0]
        rows, width = self.keep.shape
        small = self.small is not None and (kind != "gather" or after == "finish")
        more = SMALL if small and after != "gather" else 0
        sds = lambda count: jax.ShapeDtypeStruct((count, width), BF)
        if kind == "gather":
            outs = [sds(2 * rows + more)]
        elif after == "halve":
            outs = [sds(rows // 2 + more), sds(rows // 2)]
        else:
            outs = [sds(rows + more)] + [sds(rows)] * (more > 0)
        if small and kind != "gather":
            outs.append(sds(SMALL))
        inputs = [self.keep, self.got] + [self.small] * small
        outs = self.calls.call(
            functools.partial(land_kernel, small, (kind, after)), "land", 0.5, inputs, [whole()] * len(inputs), outs
        )
        self.send = outs[0]
        if small and kind != "gather":
            self.small = outs[-1]
        split = kind != "gather" and (after == "halve" or more > 0)
        self.keep = outs[1] if split else outs[0]
        self.fly()
        return self

    def done(self):
        while len(self.steps) > 1:
            self.land()
        return self.send, self.got


def on_device(
    tokens, cotangent, segments, pad_mask, row_counts, attend_gain, w_query, w_key, w_value, w_out,
    forward_gain, w_in, w_down, position_bias_table,
):
    rows, slots, half, width = tokens.shape
    dp, seq = lax.axis_size("dp"), lax.axis_size("seq")
    bits = dp.bit_length() - 1
    assert seq == 2 and slots == 2 and dp == 1 << bits and bits >= 3
    length = seq * half
    inner = w_query.shape[1]
    ff = w_in.shape[1]
    bucket_count, heads = position_bias_table.shape
    pairs = inner // TILE
    assert heads == 2 * pairs == 8 and inner == width
    blocks = ff // width
    assert blocks == SPLIT + 2
    splits = (SPLIT, 2)
    orders = ORDERS
    rests = [[bit for bit in range(bits) if all(bit not in pair for pair in order)] for order in orders]

    def where_am_i(order):
        def who():
            here = lax.axis_index("dp")
            masks = []
            for core in range(2):
                mask = jnp.int32(0)
                for pair in order:
                    mask = 2 * mask + ((here >> pair[core]) & 1)
                masks.append(mask)
            return [lax.axis_index("seq"), *masks]

        return who

    who = [where_am_i(order) for order in orders]
    swap = lambda a: lax.ppermute(a, ("dp", "seq"), swap_pairs(dp, None))
    tokens, cotangent, segments, pad_mask, w_query, w_key, w_value, w_out, w_in, w_down = (
        pltpu.with_memory_space_constraint(array, pltpu.HBM)
        for array in (tokens, cotangent, segments, pad_mask, w_query, w_key, w_value, w_out, w_in, w_down)
    )
    table = jnp.broadcast_to(position_bias_table[:, :, None], (bucket_count, heads, 1))
    gain, fgain = attend_gain.reshape(1, width), forward_gain.reshape(1, width)
    sds = jax.ShapeDtypeStruct
    vm = pltpu.VMEM
    dma = pltpu.SemaphoreType.DMA
    paired = sds((rows, pairs, length, TILE), BF)
    wide_bf, wide_f32 = sds((rows, length, width), BF), sds((rows, length, width), F32)
    narrow, items = sds((rows, length, TILE), F32), sds((rows, length, TILE), BF)
    square, square_bf = sds((inner, width), F32), sds((inner, width), BF)
    row_half, marked = sds((rows, half, width), BF), sds((2, rows, half), jnp.int32)
    calls = Order()
    call = calls.call

    tok_send, marks_own, marks_send = call(
        pick_kernel, "pick", 1, (tokens, segments, pad_mask), [far()] * 3,
        (row_half, marked, marked), scratch=[vm((2, rows, slots, half), jnp.int32), dma((rows + 2,))], who=who[0],
    )
    tok_got, marks_got = swap(tok_send), swap(marks_send)
    tok_own, cot_own, cot_send = call(
        pick_rest_kernel, "pick_rest", 1, (tokens, cotangent), [far(), far()],
        (row_half, row_half, row_half), scratch=[dma((3 * rows,))], who=who[0],
    )
    cot_got = swap(cot_send)
    e_shape = (rows, pairs, 2, length, length)
    x, normed, q, k, v, e, inv, att, kept, middle, second = call(
        forward_kernel, "attend_forward", 14,
        (
            row_counts.reshape(rows), tok_own, tok_got, marks_own, marks_got, table, gain, fgain,
            w_query, w_key, w_value, w_out,
        ),
        [smem()] + [whole()] * 7 + [far()] * 4,
        (
            wide_bf, wide_bf, paired, paired, paired, sds(e_shape, BF),
            sds((rows, pairs, length, TILE), F32), paired, narrow, wide_f32, wide_bf,
        ),
        grid=pairs,
        out_specs=[whole()] * 5 + [pl.BlockSpec((rows, 1, 2, length, length), lambda p: (0, p, 0, 0, 0))] + [whole()] * 5,
        scratch=[vm((rows, length, TILE), BF)] * 2 + [vm((heads, 1, 2 * length), F32)] + [vm((width, inner), BF)] * 4 + [dma((4,))],
        vmem=VMEM[0],
        who=who[0],
    )

    block = vm((width, width), BF)
    piece_halves = lambda count, more=0: (sds((count * width // 2, width), BF), sds((count * width // 2 + more, width), BF))
    first = blocks - 1
    g, fg, acc, sg, keep, send = call(
        functools.partial(feed_first_kernel, steps=first), "feed_first", 5 * first,
        (cot_own, cot_got, kept, second, w_in, w_down),
        [whole()] * 4 + [far()] * 2,
        (wide_bf, wide_bf, wide_f32, wide_f32, *piece_halves(2 * first)),
        grid=first,
        scratch=[vm((first, width, width), BF)] * 2 + [dma((first, 2))],
        vmem=VMEM[1],
        who=who[0],
    )
    a = Piece(calls, keep, send, None, orders[0], rests[0], dp)
    _, _, out_own, out_send, mg, grad_att, gf, *ready = call(
        functools.partial(feed_third_kernel, first), "feed_third", 8,
        (g, fg, acc, sg, kept, middle, second, att, fgain, w_out, w_in, w_down),
        [whole()] * 9 + [far()] * 3,
        (
            wide_f32, wide_f32, row_half, row_half, wide_f32, paired, sds((1, width), F32),
            square_bf, square_bf, square_bf,
        ),
        scratch=[vm((length, width), F32), block, block, block, dma((3,))],
        vmem=VMEM[3],
        aliases={2: 0, 3: 1},
        who=who[0],
    )

    some = sds((rows, pairs // PARTS, length, TILE), BF)
    dq, dk, dv, diag = [], [], [], []
    a.land()
    for part in range(PARTS):
        base = part * (pairs // PARTS)
        outs = call(
            functools.partial(backward_kernel, base=base), "attend_backward", 12 / PARTS,
            (e, q, k, v, inv, att, grad_att),
            [pl.BlockSpec((rows, 1, 2, length, length), lambda p, base=base: (0, p + base, 0, 0, 0))] + [whole()] * 6,
            (some, some, some, sds((heads // PARTS, 1, 2 * length), F32)),
            grid=pairs // PARTS,
            scratch=[vm((2, TILE, 2 * length), F32)],
            vmem=VMEM[4],
        )
        for kept_list, out in zip((dq, dk, dv, diag), outs):
            kept_list.append(out)
        a.land()
    keep, send, small = call(
        functools.partial(weight_kernel, PARTS, bucket_count), "weight_grads", 3,
        (normed, *dq, *dk, *dv, *diag, gf, *ready, w_query, w_key, w_value, gain),
        [whole()] * (5 + 4 * PARTS) + [far()] * 3 + [whole()],
        (*piece_halves(6, SMALL), sds((SMALL, width), BF)),
        scratch=[block, block, block, dma((3,))],
        vmem=VMEM[5],
        who=who[1],
    )
    c_piece = Piece(calls, keep, send, small, orders[1], rests[1], dp)
    in_own, in_send = call(
        functools.partial(input_kernel, PARTS), "input_grad", 4,
        (x, mg, *dq, *dk, *dv, w_query, w_key, w_value, gain),
        [whole()] * (2 + 3 * PARTS) + [far()] * 3 + [whole()],
        (row_half, row_half),
        scratch=[vm((length, width), F32), block, block, block, dma((3,))],
        vmem=VMEM[6],
        who=who[0],
    )
    a.land()
    out_got = swap(out_send)
    in_got = swap(in_send)
    grad_down = None
    all_rows = sds((rows, slots, half, width), BF)
    c_piece.land()
    output, grad_input = call(
        place_kernel, "place", 1, (out_own, out_got, in_own, in_got), [whole()] * 4,
        (all_rows, all_rows), out_specs=[far(), far()], scratch=[dma((4 * rows,))], who=who[0],
    )
    a.land()
    c_piece.land()
    a.land()
    c_piece.land()
    while len(a.steps) > 1 or grad_down is None:
        if len(a.steps) > 1 or len(c_piece.steps) > 1:
            c_piece.land()
        if len(a.steps) > 1:
            a.land()
        else:
            grad_down, grad_in = call(
                feed_result_kernel, "feed_result", 4, a.done(), [whole()] * 2,
                (sds((ff, width), F32), sds((width, ff), F32)),
                out_specs=[far(), far()],
                scratch=[vm((2 * first, width, width), F32), dma((2 * first,))],
                vmem=VMEM[7],
                who=who[0],
            )
    own, got = c_piece.done()
    shapes = (sds((ff, width), F32), sds((width, ff), F32), square, square, square, square)
    result_scratch = [vm((6, width // 2, width), F32), dma((6,))]
    results = call(
        functools.partial(rest_half_kernel, False), "own_result", 2, (own, grad_down, grad_in), [whole()] + [far()] * 2,
        shapes, out_specs=[far()] * 6, scratch=result_scratch, vmem=VMEM[7], aliases={1: 0, 2: 1}, who=who[1],
    )
    *results, ga, gf, grad_table = call(
        functools.partial(other_result_kernel), "other_result", 2, (got, *results, own), [whole()] + [far()] * 6 + [whole()],
        (*shapes, sds((1, width), F32), sds((1, width), F32), sds((heads, bucket_count), F32)),
        out_specs=[far()] * 6 + [whole()] * 3,
        scratch=result_scratch, vmem=VMEM[7], aliases={1 + n: n for n in range(6)}, who=who[1],
    )
    grad_down, grad_in, grad_out, grad_query, grad_key, grad_value = results

    return (
        output,
        grad_input,
        ga.reshape(width),
        grad_query,
        grad_key,
        grad_value,
        grad_out,
        gf.reshape(width),
        grad_in,
        grad_down,
        grad_table.T,
    )


def solution(mesh):
    placed = (P(None, "dp", "seq", None),) * 2 + (P(None, "dp", "seq"),) * 2 + (P(None, "dp"),) + (P(),) * 9
    return jax.shard_map(
        on_device,
        mesh=mesh,
        in_specs=placed,
        out_specs=(P(None, "dp", "seq", None),) * 2 + (P(),) * 9,
        check_vma=False,
    )
```
